32 devices in a mesh: section: 2 (over y), dp: 8 (over z, x), tensor: 2 (over core).
Axes of the slice: x: 2, y: 2, z: 4, core: 2. Of those that a mesh axis runs over, the one named last changes fastest.
Arguments:
- chain_inputs: bfloat16 [7680, 768], P('dp', 'tensor'), may hold values from -6 to 6
- cotangent: bfloat16 [7680, 768], P('dp', 'tensor'), may hold values from -6 to 6
- chain_tags: int32 [48], P('dp'), may hold values 0 or 1
- pad_mask: int32 [7680], P('dp'), may hold values from 0 to 1, as said below
- predicted: int32 [7680], P('dp'), may hold values from 0 to 23
- target_ids: int32 [7680], P('dp'), may hold values from 0 to 23
- joint_proj: bfloat16 [2, 2, 768, 3, 768], P('section', None, None, None, 'tensor'), may hold values from -0.21875 to 0.21875
- output_proj: bfloat16 [2, 2, 768, 768], P('section', None, 'tensor'), may hold values from -0.875 to 0.875
- up_proj: bfloat16 [2, 2, 768, 3072], P('section', None, None, 'tensor'), may hold values from -0.21875 to 0.21875
- up_bias: bfloat16 [2, 2, 3072], P('section', None, 'tensor'), may hold values from -3 to 3
- down_proj: bfloat16 [2, 2, 3072, 768], P('section', None, 'tensor'), may hold values from -0.109375 to 0.109375
- norm_gain: float32 [2, 2, 768], P('section'), may hold values from 0.25 to 1.75
- norm_shift: float32 [2, 2, 768], P('section'), may hold values from -2 to 2
Outputs:
- layer_outputs: bfloat16 [2, 7680, 768], P('section', 'dp', 'tensor')
- input_grads: float32 [2, 7680, 768], P('section', 'dp', 'tensor')
- joint_grad: float32 [2, 2, 768, 3, 768], P('section', None, None, None, 'tensor')
- output_grad: float32 [2, 2, 768, 768], P('section', None, 'tensor')
- up_grad: float32 [2, 2, 768, 3072], P('section', None, None, 'tensor')
- bias_grad: float32 [2, 2, 3072], P('section', None, 'tensor')
- down_grad: float32 [2, 2, 3072, 768], P('section', None, 'tensor')
- gain_grad: float32 [2, 2, 768], P('section')
- shift_grad: float32 [2, 2, 768], P('section')
- residue_counts: int32 [2, 24], replicated
The draws below stay inside these ranges and needn't reach their ends.
Inputs may be any that keep to these rules, and one draw needn't show every extreme that they name: `pad_mask`: each chain's live positions are its first ones, at least 40 of them; some chains are padded.
All inputs are finite; a program needn't handle non-finite values. No bound on the sum of `chain_tags` on one device may be relied on, other than what follows from the above.
Results may differ from the reference program's by a relative error of at most 0.035.
Values may be sent and summed in bfloat16 or wider, within the bound.
No kernel may reach another device: no remote copies, remote signals or barrier semaphores. Data moves between devices by JAX's collectives and lax.ppermute only.
A program may use at most 256 MiB of HBM per device.

```python
import jax
import jax.numpy as jnp
from jax import lax

D = 768
HEADS = 12
HEAD_DIM = 64
FF = 3072
SYMBOLS = 24
SEQ = 160
SETS = 2
LAYERS = 2
CHAINS = 48
TOKENS = 7680


def draw_pad_mask(key, part):
    key = jax.random.fold_in(key, 11)
    lengths = jax.random.randint(key, (CHAINS,), SEQ // 4, SEQ + 1)
    lengths = lengths.at[0].set(SEQ // 2)
    positions = jnp.arange(SEQ, dtype=jnp.int32)
    return (positions[None, :] < lengths[:, None]).astype(jnp.int32).reshape(CHAINS * SEQ)


def set_ends(array, key, smallest, top_value):
    longest = array.shape.index(max(array.shape))
    spots = []
    for shift in (0, 1):
        where = [jax.random.randint(jax.random.fold_in(key, axis), (), 0, length) for axis, length in enumerate(array.shape)]
        where[longest] = (where[longest] + shift) % array.shape[longest]
        spots.append(tuple(where))
    return array.at[spots[0]].set(smallest).at[spots[1]].set(top_value)


def shard_levels(own_key, shape, shards, smallest, largest):
    loudness = 1.0
    for axis_at, blocks in shards:
        draws = jax.random.uniform(jax.random.fold_in(jax.random.fold_in(own_key, 6), axis_at), (blocks,), jnp.float32, smallest / len(shards), largest / len(shards))
        loudness = loudness * jnp.repeat(jnp.exp(draws), shape[axis_at] // blocks).reshape((-1,) + (1,) * (len(shape) - 1 - axis_at))
    return loudness


def normal_values(key, dims, scale, reach, split=(), held_as=jnp.bfloat16):
    loudness = shard_levels(key, dims, split, -0.22, 0.18) if split else 1.0
    array = jax.random.normal(key, dims, jnp.float32) * scale * loudness
    return jnp.minimum(jnp.maximum(array, -reach), reach).astype(held_as)


def setup_inputs(seed: int = 0) -> dict:
    arg_keys = jax.random.split(jax.random.key(seed), 14)
    return {
        "chain_inputs": normal_values(arg_keys[0], (TOKENS, D), 1.0, 6.0, ((0, 8), (1, 2))),
        "cotangent": normal_values(arg_keys[1], (TOKENS, D), 1.0, 6.0, ((0, 8), (1, 2))),
        "chain_tags": set_ends((jax.random.randint(arg_keys[2], (CHAINS,), 0, 3) < 1).astype(jnp.int32), jax.random.fold_in(arg_keys[2], 1), 0, 1),
        "pad_mask": draw_pad_mask(jax.random.fold_in(arg_keys[13], 71), 0),
        "predicted": set_ends(jax.random.randint(arg_keys[4], (TOKENS,), 0, SYMBOLS), jax.random.fold_in(arg_keys[4], 1), 0, SYMBOLS - 1).astype(jnp.int32),
        "target_ids": set_ends(jax.random.randint(arg_keys[5], (TOKENS,), 0, SYMBOLS), jax.random.fold_in(arg_keys[5], 1), 0, SYMBOLS - 1).astype(jnp.int32),
        "joint_proj": normal_values(arg_keys[6], (LAYERS, SETS, D, 3, D), D ** -0.5, 0.21875, ((0, 2), (4, 2))),
        "output_proj": normal_values(arg_keys[7], (LAYERS, SETS, D, D), (D // 16) ** -0.5, 0.875, ((0, 2), (2, 2))),
        "up_proj": normal_values(arg_keys[8], (LAYERS, SETS, D, FF), D ** -0.5, 0.21875, ((0, 2), (3, 2))),
        "up_bias": normal_values(arg_keys[9], (LAYERS, SETS, FF), 0.5, 3.0, ((0, 2), (2, 2))),
        "down_proj": normal_values(arg_keys[10], (LAYERS, SETS, FF, D), FF ** -0.5, 0.109375, ((0, 2), (2, 2))),
        "norm_gain": jnp.clip(1.0 + 0.15 * jax.random.normal(arg_keys[11], (LAYERS, 2, D), jnp.float32), 0.25, 1.75),
        "norm_shift": normal_values(arg_keys[12], (LAYERS, 2, D), 0.3, 2.0, ((0, 2),), jnp.float32),
    }


@jax.custom_vjp
def low(v):
    return lax.optimization_barrier(v.astype(jnp.bfloat16)).astype(jnp.float32)

@jax.custom_vjp
def low_back(v):
    return v

def low_keep(v):
    return (low(v), None)

def low_pass(kept, grad):
    return (grad,)

def back_keep(v):
    return (v, None)

def back_low(kept, grad):
    return (low(grad),)
low.defvjp(low_keep, low_pass)
low_back.defvjp(back_keep, back_low)
highest = lax.Precision.HIGHEST

def both_round(values):
    return low(low_back(values))

def pick_product(rows, weights, is_light):
    first_set = jnp.dot(rows, weights[0], precision=highest)
    second_set = jnp.dot(rows, weights[1], precision=highest)
    return jnp.where(is_light, second_set, first_set)

def layer_norm(rows, gain, shift):
    centred = rows - lax.optimization_barrier(jnp.mean(rows, axis=-1, keepdims=True))
    inv_root = lax.rsqrt(lax.optimization_barrier(jnp.mean(centred * centred, axis=-1, keepdims=True)) + 1e-05)
    return centred * inv_root * gain + shift

def attend(block):
    queries, key_rows, values, key_live = block
    raw_scores = jnp.einsum('cqhd,ckhd->chqk', queries, key_rows, precision=highest)
    scores = low_back(raw_scores) * HEAD_DIM ** (-0.5)
    scores = jnp.where(key_live[:, None, None, :] > 0, scores, -1000000000.0)
    shifted = jnp.exp(scores - lax.optimization_barrier(jnp.max(scores, axis=-1, keepdims=True)))
    attn_probs = shifted / lax.optimization_barrier(jnp.sum(shifted, axis=-1, keepdims=True))
    return jnp.einsum('chqk,ckhd->cqhd', low(attn_probs), values, precision=highest)

def encoder_layer(rows, is_light, key_live, layer_params, blocks, group):
    joint, output, up_w, up_b, down_w, gains, shifts = layer_params
    joined = both_round(pick_product(rows, joint.reshape(2, D, 3 * D), is_light))
    pieces = joined.reshape(blocks, group, SEQ, 3, HEADS, HEAD_DIM)
    mixed_heads = lax.map(jax.checkpoint(attend), (pieces[:, :, :, 0], pieces[:, :, :, 1], pieces[:, :, :, 2], key_live))
    mixed_heads = both_round(mixed_heads.reshape(TOKENS, D))
    attn_total = low_back(pick_product(mixed_heads, output, is_light))
    normed_one = layer_norm(rows + attn_total, gains[0], shifts[0])
    pre_act = low_back(pick_product(low(normed_one), up_w, is_light) + jnp.where(is_light, up_b[1], up_b[0]))
    hidden = low(jax.nn.gelu(pre_act, approximate=False))
    down_total = low_back(pick_product(hidden, down_w, is_light))
    return layer_norm(normed_one + down_total, gains[1], shifts[1])

def reference(chain_inputs, cotangent, chain_tags, pad_mask, predicted, target_ids, joint_proj, output_proj, up_proj, up_bias, down_proj, norm_gain, norm_shift):
    group = max((divisor for divisor in range(1, CHAINS + 1) if CHAINS % divisor == 0 and divisor * SEQ <= 4096))
    blocks = CHAINS // group
    is_light = (jnp.repeat(chain_tags, SEQ) > 0)[:, None]
    key_live = pad_mask.reshape(blocks, group, SEQ)

    def forward(rows, extra, joint, output, up_w, up_b, down_w, gains, shifts):

        def layer(layer_rows, level):
            layer_params = (joint[level], output[level], up_w[level], up_b[level], down_w[level], gains[level], shifts[level])
            return encoder_layer(layer_rows, is_light, key_live, layer_params, blocks, group)
        first_out = layer(rows, 0)
        passed = low_back(low(first_out)) + extra
        second_out = layer(passed, 1)
        return (first_out, second_out)
    results, pullback = jax.vjp(forward, chain_inputs.astype(jnp.float32), jnp.zeros((TOKENS, D), jnp.float32), joint_proj.astype(jnp.float32), output_proj.astype(jnp.float32), up_proj.astype(jnp.float32), up_bias.astype(jnp.float32), down_proj.astype(jnp.float32), norm_gain.astype(jnp.float32), norm_shift.astype(jnp.float32))
    grads = pullback((jnp.zeros_like(results[0]), cotangent.astype(jnp.float32)))
    layer_outputs = jnp.stack([results[0], results[1]]).astype(jnp.bfloat16)
    input_grads = jnp.stack([grads[0], grads[1]])
    symbols = jnp.arange(SYMBOLS, dtype=jnp.int32)
    target_hits = (target_ids[:, None] == symbols[None, :]) & (pad_mask[:, None] > 0)
    correct_hits = target_hits & (predicted == target_ids)[:, None]
    residue_counts = jnp.stack([lax.optimization_barrier(jnp.sum(target_hits, 0)), lax.optimization_barrier(jnp.sum(correct_hits, 0))]).astype(jnp.int32)
    return (layer_outputs, input_grads, grads[2], grads[3], grads[4], grads[5], grads[6], grads[7], grads[8], residue_counts)
```

```python
import jax
import jax.numpy as jnp
from jax import lax
from jax.sharding import PartitionSpec as P

HEAD_DIM = 64
SYMBOLS = 24
SEQ = 160
PARTS = 2

root_half = 0.7071067811865476
root_two_pi = 0.3989422804014327
BF = jnp.bfloat16
F32 = jnp.float32


def swap(value):
    return lax.ppermute(value, "tensor", [(0, 1), (1, 0)])


def pick_product(rows, weights, is_light):
    first_set = jnp.dot(rows, weights[0], preferred_element_type=F32)
    second_set = jnp.dot(rows, weights[1], preferred_element_type=F32)
    return jnp.where(is_light, second_set, first_set)


def back_product(grads, weights, is_light):
    contract_cols = (((1,), (1,)), ((), ()))
    first_set = lax.dot_general(grads, weights[0], contract_cols, preferred_element_type=F32)
    second_set = lax.dot_general(grads, weights[1], contract_cols, preferred_element_type=F32)
    return jnp.where(is_light, second_set, first_set)


def weight_pair(rows, grads, is_light):
    contract_rows = (((0,), (0,)), ((), ()))
    zero_rows = jnp.zeros_like(rows)
    heavy_rows = jnp.where(is_light, zero_rows, rows)
    light_rows = jnp.where(is_light, rows, zero_rows)
    first_set = lax.dot_general(heavy_rows, grads, contract_rows, preferred_element_type=F32)
    second_set = lax.dot_general(light_rows, grads, contract_rows, preferred_element_type=F32)
    return [first_set.astype(BF), second_set.astype(BF)]


def layer_norm(rows, gain, shift):
    centred = rows - jnp.mean(rows, axis=-1, keepdims=True)
    inv_root = lax.rsqrt(jnp.mean(centred * centred, axis=-1, keepdims=True) + 1e-05)
    normal = centred * inv_root
    return (normal * gain + shift, normal, inv_root)


def norm_back(grads, normal, inv_root, gain):
    scaled = grads * gain
    inner = (
        scaled
        - jnp.mean(scaled, axis=-1, keepdims=True)
        - normal * jnp.mean(scaled * normal, axis=-1, keepdims=True)
    )
    return inner * inv_root


def attn_forward(rows_in, is_light, key_live, params):
    joint, output = params[:2]
    chains = key_live.shape[0]
    local_heads = output.shape[1] // HEAD_DIM
    joined = pick_product(rows_in, joint, is_light).astype(BF)
    pieces = joined.reshape(chains, SEQ, 3, local_heads, HEAD_DIM)
    q, k, v = pieces[:, :, 0], pieces[:, :, 1], pieces[:, :, 2]
    raw_scores = jnp.einsum("cqhd,ckhd->chqk", q, k, preferred_element_type=F32)
    scores = jnp.where(key_live[:, None, None, :], raw_scores * HEAD_DIM ** (-0.5), -1000000000.0)
    shifted = jnp.exp(scores - jnp.max(scores, axis=-1, keepdims=True))
    probs = shifted / jnp.sum(shifted, axis=-1, keepdims=True)
    mixed = jnp.einsum("chqk,ckhd->cqhd", probs.astype(BF), v, preferred_element_type=F32)
    mixed = mixed.astype(BF).reshape(rows_in.shape[0], -1)
    part = pick_product(mixed, output, is_light).astype(BF)
    return part, (q, k, v, probs, mixed)


def feed_forward(rows_in, part, other, is_light, params):
    joint, output, up_w, up_b, down_w, gains, shifts = params
    attn = part.astype(F32) + other.astype(F32)
    first, normal_one, root_one = layer_norm(rows_in.astype(F32) + attn, gains[0], shifts[0])
    first_low = first.astype(BF)
    pre = pick_product(first_low, up_w, is_light) + jnp.where(is_light, up_b[1], up_b[0]).astype(F32)
    hidden = jax.nn.gelu(pre, approximate=False).astype(BF)
    down = pick_product(hidden, down_w, is_light).astype(BF)
    return down, (first, normal_one, root_one, first_low, pre, hidden)


def last_norm(first, down, other, params):
    gains, shifts = params[5:]
    return layer_norm(first + (down.astype(F32) + other.astype(F32)), gains[1], shifts[1])


def feed_back(grad, normal_two, root_two, kept, is_light, params):
    joint, output, up_w, up_b, down_w, gains, shifts = params
    first, normal_one, root_one, first_low, pre, hidden = kept
    dr2 = norm_back(grad, normal_two, root_two, gains[1])
    d_down = dr2.astype(BF)
    d_hidden = back_product(d_down, down_w, is_light)
    slope = 0.5 * (1.0 + lax.erf(pre * root_half)) + pre * jnp.exp(-0.5 * pre * pre) * root_two_pi
    d_pre = (d_hidden * slope).astype(BF)
    part = back_product(d_pre, up_w, is_light).astype(BF)
    return dr2, d_down, d_pre, part


def attn_back(dr2, part, other, feed_kept, attn_kept, is_light, params):
    joint, output, up_w, up_b, down_w, gains, shifts = params
    first, normal_one, root_one, first_low, pre, hidden = feed_kept
    q, k, v, probs, mixed = attn_kept
    d_first = dr2 + (part.astype(F32) + other.astype(F32))
    dr1 = norm_back(d_first, normal_one, root_one, gains[0])
    d_attn = dr1.astype(BF)
    d_mixed = back_product(d_attn, output, is_light).astype(BF).reshape(q.shape)
    d_probs = jnp.einsum("cqhd,ckhd->chqk", d_mixed, v, preferred_element_type=F32)
    d_scores = (
        probs * (d_probs - jnp.sum(probs * d_probs, axis=-1, keepdims=True))
    ).astype(BF)
    scale = HEAD_DIM ** (-0.5)
    dq = jnp.einsum("chqk,ckhd->cqhd", d_scores, k, preferred_element_type=F32) * scale
    dk = jnp.einsum("chqk,cqhd->ckhd", d_scores, q, preferred_element_type=F32) * scale
    dv = jnp.einsum("chqk,cqhd->ckhd", probs.astype(BF), d_mixed, preferred_element_type=F32)
    d_joined = jnp.stack([dq, dk, dv], axis=2).astype(BF).reshape(dr1.shape[0], -1)
    d_rows = back_product(d_joined, joint, is_light).astype(BF)
    return d_first, dr1, d_attn, d_joined, d_rows


def ring_order(count):
    return list(range(0, count, 2)) + list(range(1, count, 2))[::-1]


def ring_sum(heavy, light):
    count = lax.axis_size("dp")
    order = ring_order(count)
    rank = lax.axis_index("dp")
    place = jnp.zeros((), jnp.int32)
    for at, member in enumerate(order):
        place = jnp.where(rank == member, at, place)
    ahead = [(order[i], order[(i + 1) % count]) for i in range(count)]
    behind = [(b, a) for a, b in ahead]
    shape = heavy.shape
    rows = shape[0] // count

    def shard(whole, index):
        return lax.dynamic_slice_in_dim(whole, lax.rem(index, count) * rows, rows, 0)

    results = []
    for whole, pairs, sign in ((heavy, ahead, -1), (light, behind, 1)):
        moving = shard(whole, place + sign + count)
        for step in range(count - 1):
            moving = lax.ppermute(moving, "dp", pairs)
            index = place + sign * (step + 2) + 2 * count
            moving = (moving.astype(F32) + shard(whole, index).astype(F32)).astype(BF)
        out = jnp.zeros(shape, F32)
        index = place
        for step in range(count):
            out = lax.dynamic_update_slice_in_dim(
                out, moving.astype(F32), lax.rem(index, count) * rows, 0
            )
            if step < count - 1:
                moving = lax.ppermute(moving, "dp", pairs)
                index = place + sign * (step + 1) + count
        results.append(out)
    return jnp.stack(results)


def shards(
    chain_inputs,
    cotangent,
    chain_tags,
    pad_mask,
    predicted,
    target_ids,
    joint_proj,
    output_proj,
    up_proj,
    up_bias,
    down_proj,
    norm_gain,
    norm_shift,
):
    section = lax.axis_index("section")
    core = lax.axis_index("tensor")
    tokens, half = chain_inputs.shape
    width = 2 * half

    def side_by_side(own, other):
        return jnp.where(
            core == 0,
            jnp.concatenate([own, other], axis=1),
            jnp.concatenate([other, own], axis=1),
        )

    def own_half(value):
        return lax.dynamic_slice_in_dim(value, core * half, half, 1)

    rows_all = side_by_side(chain_inputs, swap(chain_inputs))
    cot_all = side_by_side(cotangent, swap(cotangent))
    size = tokens // PARTS
    joint = joint_proj[0].reshape(2, width, -1)
    params = (
        joint,
        output_proj[0],
        up_proj[0],
        up_bias[0],
        down_proj[0],
        norm_gain[0],
        norm_shift[0],
    )
    light_all = (jnp.repeat(chain_tags, SEQ) > 0)[:, None]
    live_all = (pad_mask > 0).reshape(-1, SEQ)
    spans = [slice(p * size, (p + 1) * size) for p in range(PARTS)]
    lights = [light_all[s] for s in spans]
    lives = [live_all[s.start // SEQ : s.stop // SEQ] for s in spans]
    own_rows = [rows_all[s] for s in spans]
    own_cot = [cot_all[s] for s in spans]

    def forward(rows, p):
        part, attn_kept = attn_forward(rows, lights[p], lives[p], params)
        down, feed_kept = feed_forward(rows, part, swap(part), lights[p], params)
        result, normal, root = last_norm(feed_kept[0], down, swap(down), params)
        return result.astype(BF), attn_kept, feed_kept, normal, root

    def backward(grad, kept, p):
        low, attn_kept, feed_kept, normal, root = kept
        dr2, d_down, d_pre, part = feed_back(grad, normal, root, feed_kept, lights[p], params)
        d_first, dr1, d_attn, d_joined, d_rows = attn_back(
            dr2, part, swap(part), feed_kept, attn_kept, lights[p], params
        )
        return d_down, d_pre, d_first, dr1, d_attn, d_joined, d_rows

    def to_section(value, pairs):
        moved = lax.ppermute(own_half(value), "section", pairs)
        return side_by_side(moved, swap(moved))

    arrived = []
    for p in range(PARTS):
        low = forward(own_rows[p], p)[0]
        arrived.append(to_section(low, [(0, 1)]))
    rows_in = [jnp.where(section == 0, own_rows[p], arrived[p]) for p in range(PARTS)]
    kept = [forward(rows_in[p], p) for p in range(PARTS)]
    grads_in = []
    for p in range(PARTS):
        d_down, d_pre, d_first, dr1, d_attn, d_joined, d_rows = backward(
            own_cot[p].astype(F32), kept[p], p
        )
        own = own_half(d_rows)
        total = own_half(dr1) + (own.astype(F32) + swap_other(d_rows, core, half).astype(F32))
        moved = lax.ppermute(total.astype(BF), "section", [(1, 0)])
        back = side_by_side(moved, swap(moved))
        grads_in.append(jnp.where(section == 1, own_cot[p], back).astype(F32))
    outs = [backward(grads_in[p], kept[p], p) for p in range(PARTS)]

    def whole(pieces):
        return jnp.concatenate(pieces, axis=0)

    d_down = whole([o[0] for o in outs])
    d_pre = whole([o[1] for o in outs])
    d_first = whole([o[2] for o in outs])
    d_attn = whole([o[4] for o in outs])
    d_joined = whole([o[5] for o in outs])
    hidden = whole([k[2][5] for k in kept])
    first_low = whole([k[2][3] for k in kept])
    mixed = whole([k[1][4] for k in kept])
    rows_whole = whole(rows_in)
    normal_one = whole([k[2][1] for k in kept])
    normal_two = whole([k[3] for k in kept])
    grad_whole = whole(grads_in)

    down_sum = ring_sum(*weight_pair(hidden, d_down, light_all))
    up_sum = ring_sum(*weight_pair(first_low, d_pre, light_all))
    output_sum = ring_sum(*weight_pair(mixed, d_attn, light_all))
    pair = weight_pair(rows_whole, d_joined, light_all)
    pair = [g.reshape(width, 3, half).transpose(1, 0, 2).reshape(3 * width, half) for g in pair]
    joint_sum = ring_sum(*pair).reshape(2, 3, width, half).transpose(0, 2, 1, 3)

    input_pieces = []
    for p in range(PARTS):
        d_rows, dr1 = outs[p][6], outs[p][3]
        input_pieces.append(
            own_half(dr1)
            + (own_half(d_rows).astype(F32) + swap_other(d_rows, core, half).astype(F32))
        )
    input_grads = whole(input_pieces)[None]
    layer_outputs = own_half(whole([k[0] for k in kept]))[None]

    pre_wide = d_pre.astype(F32)
    zero = jnp.zeros_like(pre_wide)
    bias = jnp.stack(
        [
            jnp.sum(jnp.where(light_all, zero, pre_wide), 0),
            jnp.sum(jnp.where(light_all, pre_wide, zero), 0),
        ]
    )
    gain = jnp.stack([jnp.sum(d_first * normal_one, 0), jnp.sum(grad_whole * normal_two, 0)])
    shift = jnp.stack([jnp.sum(d_first, 0), jnp.sum(grad_whole, 0)])
    symbols = jnp.arange(SYMBOLS, dtype=jnp.int32)
    target_hits = (target_ids[:, None] == symbols[None, :]) & (pad_mask[:, None] > 0)
    correct_hits = target_hits & (predicted == target_ids)[:, None]
    counts = jnp.stack([jnp.sum(target_hits, 0), jnp.sum(correct_hits, 0)]).astype(F32)
    small = [bias, gain, shift, counts]
    packed = jnp.concatenate([s.reshape(-1) for s in small])
    packed = lax.psum(packed, "dp")
    results = []
    start = 0
    for s in small:
        results.append(packed[start : start + s.size].reshape(s.shape))
        start += s.size
    bias, gain, shift, counts = results
    return (
        layer_outputs,
        input_grads,
        joint_sum[None],
        output_sum[None],
        up_sum[None],
        bias[None],
        down_sum[None],
        gain[None],
        shift[None],
        counts.astype(jnp.int32),
    )


def swap_other(value, core, half):
    theirs = lax.dynamic_slice_in_dim(value, (1 - core) * half, half, 1)
    return swap(theirs)


def solution(mesh):
    return jax.shard_map(
        shards,
        mesh=mesh,
        in_specs=(
            P("dp", "tensor"),
            P("dp", "tensor"),
            P("dp"),
            P("dp"),
            P("dp"),
            P("dp"),
            P("section", None, None, None, "tensor"),
            P("section", None, "tensor", None),
            P("section", None, None, "tensor"),
            P("section", None, "tensor"),
            P("section", None, "tensor", None),
            P("section", None, None),
            P("section", None, None),
        ),
        out_specs=(
            P("section", "dp", "tensor"),
            P("section", "dp", "tensor"),
            P("section", None, None, None, "tensor"),
            P("section", None, "tensor", None),
            P("section", None, None, "tensor"),
            P("section", None, "tensor"),
            P("section", None, "tensor", None),
            P("section", None, None),
            P("section", None, None),
            P(),
        ),
        check_vma=False,
    )
```

```python
import functools

import jax
import jax.numpy as jnp
from jax import lax
from jax.experimental import pallas as pl
from jax.experimental.pallas import tpu as pltpu
from jax.sharding import PartitionSpec as P

HEAD_DIM = 64
SYMBOLS = 24
SEQ = 160
PARTS = 2
EPS = 1e-05
SCALE = HEAD_DIM**-0.5
VMEM_LIMIT = 40 * 1024 * 1024

root_half = 0.7071067811865476
root_two_pi = 0.3989422804014327
BF = jnp.bfloat16
F32 = jnp.float32


def swap(value):
    return lax.ppermute(value, "tensor", [(0, 1), (1, 0)])


def dot(a, b):
    return jnp.dot(a, b, preferred_element_type=F32)


def dot_rows(a, b):
    return lax.dot_general(a, b, (((1,), (1,)), ((), ())), preferred_element_type=F32)


def dot_cols(a, b):
    return lax.dot_general(a, b, (((0,), (0,)), ((), ())), preferred_element_type=F32)


def in_order(core, own, other):
    first = core == 0
    return jnp.concatenate(
        [jnp.where(first, own, other), jnp.where(first, other, own)], axis=1
    )


def own_part(core, value):
    half = value.shape[1] // 2
    return jnp.where(core == 0, value[:, :half], value[:, half:])


def normalise(rows):
    centred = rows - jnp.mean(rows, axis=-1, keepdims=True)
    inv_root = lax.rsqrt(jnp.mean(centred * centred, axis=-1, keepdims=True) + EPS)
    return centred * inv_root, inv_root


def norm_back(grads, normal, inv_root, gain):
    scaled = grads * gain
    inner = (
        scaled
        - jnp.mean(scaled, axis=-1, keepdims=True)
        - normal * jnp.mean(scaled * normal, axis=-1, keepdims=True)
    )
    return inner * inv_root


def pair_masks(dtype):
    lane = lax.broadcasted_iota(jnp.int32, (1, 2 * HEAD_DIM), 1)
    return (lane < HEAD_DIM).astype(dtype), (lane >= HEAD_DIM).astype(dtype)


def attn_forward_kernel(choose, keep, start, marks, *refs):
    refs = list(refs)
    own, other = refs.pop(0), refs.pop(0)
    if choose:
        own_late, other_late = refs.pop(0), refs.pop(0)
    live, joint, output = refs.pop(0), refs.pop(0), refs.pop(0)
    chain = pl.program_id(0)
    tag = marks[2 + start + chain]
    core = marks[1]
    a, b = own[...], other[...]
    if choose:
        early = marks[0] == 0
        a = jnp.where(early, a, own_late[...])
        b = jnp.where(early, b, other_late[...])
    rows = in_order(core, a, b)
    q, k, v = [dot(rows, joint[tag, j]).astype(BF) for j in range(3)]
    key_live = live[0] > 0
    masks = pair_masks(BF)
    left = pair_masks(F32)[0] > 0
    pieces = []
    kept = []
    for at in range(0, q.shape[1], 2 * HEAD_DIM):
        span = slice(at, at + 2 * HEAD_DIM)
        q2, k2, v2 = q[:, span] * jnp.asarray(SCALE, BF), k[:, span], v[:, span]
        mixed = []
        for mask in masks:
            scores = jnp.where(key_live, dot_rows(q2 * mask, k2), -1000000000.0)
            shifted = jnp.exp(scores - jnp.max(scores, axis=-1, keepdims=True))
            probs = (shifted * (1.0 / jnp.sum(shifted, axis=-1, keepdims=True))).astype(BF)
            kept.append(probs)
            mixed.append(dot(probs, v2))
        pieces.append(jnp.where(left, mixed[0], mixed[1]).astype(BF))
    mixed = jnp.concatenate(pieces, axis=1)
    refs[0][...] = rows
    refs[1][...] = dot(mixed, output[tag]).astype(BF)
    if keep:
        refs[2][...] = jnp.concatenate([q, k, v], axis=1)
        for at, probs in enumerate(kept):
            refs[3][0, at] = probs
        refs[4][...] = mixed


def feed_forward_kernel(keep, start, marks, rows, part, other, gains, shifts, up, bias, down, *outs):
    tag = marks[2 + start + pl.program_id(0)]
    total = rows[...].astype(F32) + (part[...].astype(F32) + other[...].astype(F32))
    normal, inv_root = normalise(total)
    low = (normal * gains[0:1] + shifts[0:1]).astype(BF)
    pre = dot(low, up[tag]) + jnp.where(tag == 0, bias[0:1], bias[1:2]).astype(F32)
    cdf = 0.5 * (1.0 + lax.erf(pre * root_half))
    hidden = (pre * cdf).astype(BF)
    outs[0][...] = dot(hidden, down[tag]).astype(BF)
    outs[1][...] = normal
    if keep:
        outs[2][...] = inv_root
        outs[3][...] = low
        outs[4][...] = hidden
        outs[5][...] = (cdf + pre * jnp.exp(-0.5 * pre * pre) * root_two_pi).astype(BF)


def second_norm(normal, part, other, gains, shifts):
    first = normal[...] * gains[0:1] + shifts[0:1]
    return normalise(first + (part[...].astype(F32) + other[...].astype(F32)))


def last_norm_kernel(marks, normal, part, other, gains, shifts, out):
    second, _ = second_norm(normal, part, other, gains, shifts)
    out[...] = own_part(marks[1], (second * gains[1:2] + shifts[1:2]).astype(BF))


def add_sums(grads, normal, sums):
    @pl.when(pl.program_id(0) == 0)
    def _():
        sums[...] = jnp.zeros_like(sums)

    sums[0:1] += jnp.sum(grads * normal, axis=0, keepdims=True)
    sums[1:2] += jnp.sum(grads, axis=0, keepdims=True)


def feed_back_kernel(last, start, marks, *refs):
    refs = list(refs)
    normal, part, other, gains, shifts, own_cot, other_cot = refs[:7]
    refs = refs[7:]
    tag = marks[2 + start + pl.program_id(0)]
    core = marks[1]
    a, b = own_cot[...], other_cot[...]
    if last:
        late = marks[0] == 1
        a = jnp.where(late, a, refs.pop(0)[...])
        b = jnp.where(late, b, refs.pop(0)[...])
    slope, up, down = refs[:3]
    outs = refs[3:]
    grads = in_order(core, a, b).astype(F32)
    second, inv_root = second_norm(normal, part, other, gains, shifts)
    back = norm_back(grads, second, inv_root, gains[1:2])
    low = back.astype(BF)
    d_pre = (dot_rows(low, down[tag]) * slope[...].astype(F32)).astype(BF)
    outs[0][...] = back
    outs[1][...] = dot_rows(d_pre, up[tag]).astype(BF)
    if last:
        outs[2][...] = low
        outs[3][...] = d_pre
        outs[4][...] = own_part(core, (second * gains[1:2] + shifts[1:2]).astype(BF))
        add_sums(grads, second, outs[5])


def attn_back_kernel(
    last, start, marks, back, part, other, normal, inv_root, gains, joined, probs, joint, output, *outs
):
    tag = marks[2 + start + pl.program_id(0)]
    core = marks[1]
    grads = back[...] + (part[...].astype(F32) + other[...].astype(F32))
    back_one = norm_back(grads, normal[...], inv_root[...], gains[0:1])
    low = back_one.astype(BF)
    d_mixed = dot_rows(low, output[tag]).astype(BF)
    masks = pair_masks(BF)
    left = pair_masks(F32)[0] > 0
    width = d_mixed.shape[1]
    q, k, v = [joined[:, j * width : (j + 1) * width] for j in range(3)]
    pieces = [[], [], []]
    head = 0
    for at in range(0, width, 2 * HEAD_DIM):
        span = slice(at, at + 2 * HEAD_DIM)
        q2, k2, v2, m2 = q[:, span], k[:, span], v[:, span], d_mixed[:, span]
        found = []
        for mask in masks:
            held = probs[0, head]
            wide = held.astype(F32)
            head += 1
            d_probs = dot_rows(m2 * mask, v2)
            inner = jnp.sum(wide * d_probs, axis=-1, keepdims=True)
            d_scores = (wide * (d_probs - inner)).astype(BF)
            found.append(
                (dot(d_scores, k2) * SCALE, dot_cols(d_scores, q2) * SCALE, dot_cols(held, m2))
            )
        for j in range(3):
            pieces[j].append(jnp.where(left, found[0][j], found[1][j]).astype(BF))
    blocks = [jnp.concatenate(p, axis=1) for p in pieces]
    d_rows = sum(dot_rows(blocks[j], joint[tag, j]) for j in range(3)).astype(BF)
    outs[0][...] = own_part(core, back_one) + own_part(core, d_rows).astype(F32)
    outs[1][...] = own_part(1 - core, d_rows)
    if last:
        outs[2][...] = low
        outs[3][...] = jnp.concatenate(blocks, axis=1)
        add_sums(grads, normal[...], outs[4])


def run_chains(kernel, name, marks, chains, ins, outs, flops):
    specs = []
    for array, kind, first in ins:
        if kind == "rows":
            specs.append(
                pl.BlockSpec((SEQ, array.shape[1]), lambda i, *_, first=first: (first + i, 0))
            )
        elif kind == "chain":
            rest = array.shape[1:]
            specs.append(
                pl.BlockSpec(
                    (1,) + rest, lambda i, *_, first=first, n=len(rest): (first + i,) + (0,) * n
                )
            )
        else:
            specs.append(pl.BlockSpec(memory_space=pltpu.VMEM))
    shapes, out_specs = [], []
    for trailing, dtype, kind in outs:
        if kind == "rows":
            shapes.append(jax.ShapeDtypeStruct((chains * SEQ,) + trailing, dtype))
            out_specs.append(pl.BlockSpec((SEQ,) + trailing, lambda i, *_: (i, 0)))
        elif kind == "chain":
            shapes.append(jax.ShapeDtypeStruct((chains,) + trailing, dtype))
            out_specs.append(
                pl.BlockSpec((1,) + trailing, lambda i, *_, n=len(trailing): (i,) + (0,) * n)
            )
        else:
            shapes.append(jax.ShapeDtypeStruct(trailing, dtype))
            out_specs.append(pl.BlockSpec(trailing, lambda i, *_, n=len(trailing): (0,) * n))
    moved = sum(a.size * a.dtype.itemsize for a, _, _ in ins)
    moved += sum(s.size * s.dtype.itemsize for s in shapes)
    return pl.pallas_call(
        kernel,
        grid_spec=pltpu.PrefetchScalarGridSpec(
            num_scalar_prefetch=1, grid=(chains,), in_specs=specs, out_specs=out_specs
        ),
        out_shape=shapes,
        compiler_params=pltpu.CompilerParams(vmem_limit_bytes=VMEM_LIMIT),
        cost_estimate=pl.CostEstimate(
            flops=flops, bytes_accessed=moved, transcendentals=0
        ),
        name=name,
    )(marks, *[a for a, _, _ in ins])


def weight_pair(rows, grads, is_light):
    zero_rows = jnp.zeros_like(rows)
    heavy = dot_cols(jnp.where(is_light, zero_rows, rows), grads)
    light = dot_cols(jnp.where(is_light, rows, zero_rows), grads)
    return [heavy.astype(BF), light.astype(BF)]


def ring_order(count):
    return list(range(0, count, 2)) + list(range(1, count, 2))[::-1]


def ring_sum(heavy, light):
    count = lax.axis_size("dp")
    order = ring_order(count)
    rank = lax.axis_index("dp")
    place = jnp.zeros((), jnp.int32)
    for at, member in enumerate(order):
        place = jnp.where(rank == member, at, place)
    ahead = [(order[i], order[(i + 1) % count]) for i in range(count)]
    behind = [(b, a) for a, b in ahead]
    shape = heavy.shape
    rows = shape[0] // count

    def shard(whole, index):
        return lax.dynamic_slice_in_dim(whole, lax.rem(index, count) * rows, rows, 0)

    results = []
    for whole, pairs, sign in ((heavy, ahead, -1), (light, behind, 1)):
        moving = shard(whole, place + sign + count)
        for step in range(count - 1):
            moving = lax.ppermute(moving, "dp", pairs)
            index = place + sign * (step + 2) + 2 * count
            moving = (moving.astype(F32) + shard(whole, index).astype(F32)).astype(BF)
        out = jnp.zeros(shape, F32)
        index = place
        for step in range(count):
            out = lax.dynamic_update_slice_in_dim(
                out, moving.astype(F32), lax.rem(index, count) * rows, 0
            )
            if step < count - 1:
                moving = lax.ppermute(moving, "dp", pairs)
                index = place + sign * (step + 1) + count
        results.append(out)
    return jnp.stack(results)


def small_sum(value):
    count = lax.axis_size("dp")
    if count & (count - 1):
        return lax.psum(value, "dp")
    apart = 1
    while apart < count:
        value = value + lax.ppermute(value, "dp", [(i, i ^ apart) for i in range(count)])
        apart *= 2
    return value


def shards(
    chain_inputs,
    cotangent,
    chain_tags,
    pad_mask,
    predicted,
    target_ids,
    joint_proj,
    output_proj,
    up_proj,
    up_bias,
    down_proj,
    norm_gain,
    norm_shift,
):
    section = lax.axis_index("section")
    core = lax.axis_index("tensor")
    tokens, half = chain_inputs.shape
    width = 2 * half
    all_chains = tokens // SEQ
    chains = all_chains // PARTS
    light_all = (jnp.repeat(chain_tags, SEQ) > 0)[:, None]
    tags = (chain_tags > 0).astype(jnp.int32)
    marks = jnp.concatenate([jnp.stack([section, core]).astype(jnp.int32), tags])
    live = pad_mask.reshape(all_chains, 1, SEQ)
    joint = joint_proj[0].transpose(0, 2, 1, 3)
    output, up, bias, down = output_proj[0], up_proj[0], up_bias[0], down_proj[0]
    gains, shifts = norm_gain[0], norm_shift[0]
    units = up.shape[2]
    local = output.shape[1]
    heads = local // HEAD_DIM
    rows = chains * SEQ
    attn_flops = 2 * rows * (width * 4 * local + 2 * local * SEQ)
    feed_flops = 2 * rows * width * 2 * units

    cot_other = swap(cotangent)
    rows_other = swap(chain_inputs)

    def attn_forward(p, late, keep):
        start = p * chains
        ins = [(chain_inputs, "rows", start), (rows_other, "rows", start)]
        if late is not None:
            ins += [(late[0], "rows", 0), (late[1], "rows", 0)]
        ins += [(live, "chain", start), (joint, "whole", 0), (output, "whole", 0)]
        outs = [((width,), BF, "rows"), ((width,), BF, "rows")]
        if keep:
            outs += [
                ((3 * local,), BF, "rows"),
                ((heads, SEQ, SEQ), BF, "chain"),
                ((local,), BF, "rows"),
            ]
        kernel = functools.partial(attn_forward_kernel, late is not None, keep, start)
        return run_chains(kernel, "attn_forward", marks, chains, ins, outs, attn_flops)

    def feed_forward(p, x, part, keep):
        ins = [(x, "rows", 0), (part, "rows", 0), (swap(part), "rows", 0)]
        ins += [(a, "whole", 0) for a in (gains, shifts, up, bias, down)]
        outs = [((width,), BF, "rows"), ((width,), F32, "rows")]
        if keep:
            outs += [
                ((1,), F32, "rows"),
                ((width,), BF, "rows"),
                ((units,), BF, "rows"),
                ((units,), BF, "rows"),
            ]
        kernel = functools.partial(feed_forward_kernel, keep, p * chains)
        return run_chains(kernel, "feed_forward", marks, chains, ins, outs, feed_flops)

    def last_norm(p, normal, part):
        ins = [(normal, "rows", 0), (part, "rows", 0), (swap(part), "rows", 0)]
        ins += [(gains, "whole", 0), (shifts, "whole", 0)]
        return run_chains(
            last_norm_kernel, "last_norm", marks, chains, ins, [((half,), BF, "rows")], 0
        )[0]

    def feed_back(p, kept, late):
        ins = [(kept[n], "rows", 0) for n in ("normal", "down", "down_other")]
        ins += [(gains, "whole", 0), (shifts, "whole", 0)]
        ins += [(cotangent, "rows", p * chains), (cot_other, "rows", p * chains)]
        if late is not None:
            ins += [(late[0], "rows", 0), (late[1], "rows", 0)]
        ins += [(kept["slope"], "rows", 0), (up, "whole", 0), (down, "whole", 0)]
        outs = [((width,), F32, "rows"), ((width,), BF, "rows")]
        if late is not None:
            outs += [
                ((width,), BF, "rows"),
                ((units,), BF, "rows"),
                ((half,), BF, "rows"),
                ((2, width), F32, "whole"),
            ]
        kernel = functools.partial(feed_back_kernel, late is not None, p * chains)
        return run_chains(kernel, "feed_back", marks, chains, ins, outs, feed_flops)

    def attn_back(p, kept, back, part, last):
        ins = [(back, "rows", 0), (part, "rows", 0), (swap(part), "rows", 0)]
        ins += [(kept["normal"], "rows", 0), (kept["inv_root"], "rows", 0), (gains, "whole", 0)]
        ins += [(kept["joined"], "rows", 0), (kept["probs"], "chain", 0)]
        ins += [(joint, "whole", 0), (output, "whole", 0)]
        outs = [((half,), F32, "rows"), ((half,), BF, "rows")]
        if last:
            outs += [
                ((width,), BF, "rows"),
                ((3 * local,), BF, "rows"),
                ((2, width), F32, "whole"),
            ]
        kernel = functools.partial(attn_back_kernel, last, p * chains)
        return run_chains(kernel, "attn_back", marks, chains, ins, outs, attn_flops)

    parts = range(PARTS)
    attn = [attn_forward(p, None, False) for p in parts]
    feed = [feed_forward(p, attn[p][0], attn[p][1], False) for p in parts]
    late = []
    for p in parts:
        moved = lax.ppermute(last_norm(p, feed[p][1], feed[p][0]), "section", [(0, 1)])
        late.append((moved, swap(moved)))
    attn = [attn_forward(p, late[p], True) for p in parts]
    kept = []
    for p in parts:
        x, part, joined, probs, mixed = attn[p]
        down_part, normal, inv_root, low, hidden, slope = feed_forward(p, x, part, True)
        kept.append(
            dict(
                rows=x,
                joined=joined,
                probs=probs,
                mixed=mixed,
                down=down_part,
                down_other=swap(down_part),
                normal=normal,
                inv_root=inv_root,
                low=low,
                hidden=hidden,
                slope=slope,
            )
        )
    feed = [feed_back(p, kept[p], None) for p in parts]
    late = []
    for p in parts:
        mine, theirs = attn_back(p, kept[p], feed[p][0], feed[p][1], False)
        total = (mine + swap(theirs).astype(F32)).astype(BF)
        moved = lax.ppermute(total, "section", [(1, 0)])
        late.append((moved, swap(moved)))
    feed = [feed_back(p, kept[p], late[p]) for p in parts]
    attn = [attn_back(p, kept[p], feed[p][0], feed[p][1], True) for p in parts]
    input_grads = jnp.concatenate(
        [attn[p][0] + swap(attn[p][1]).astype(F32) for p in parts], axis=0
    )

    def whole(pieces):
        return jnp.concatenate(pieces, axis=0)

    d_pre = whole([f[3] for f in feed])
    down_sum = ring_sum(
        *weight_pair(whole([k["hidden"] for k in kept]), whole([f[2] for f in feed]), light_all)
    )
    up_sum = ring_sum(*weight_pair(whole([k["low"] for k in kept]), d_pre, light_all))
    output_sum = ring_sum(
        *weight_pair(whole([k["mixed"] for k in kept]), whole([a[2] for a in attn]), light_all)
    )
    pair = weight_pair(whole([k["rows"] for k in kept]), whole([a[3] for a in attn]), light_all)
    pair = [g.reshape(width, 3, local).transpose(1, 0, 2).reshape(3 * width, local) for g in pair]
    joint_sum = ring_sum(*pair).reshape(2, 3, width, local).transpose(0, 2, 1, 3)

    pre_wide = d_pre.astype(F32)
    zero = jnp.zeros_like(pre_wide)
    bias_grad = jnp.stack(
        [
            jnp.sum(jnp.where(light_all, zero, pre_wide), 0),
            jnp.sum(jnp.where(light_all, pre_wide, zero), 0),
        ]
    )
    sums_two = sum(f[5] for f in feed)
    sums_one = sum(a[4] for a in attn)
    sums = jnp.stack([sums_one, sums_two], axis=1)
    symbols = jnp.arange(SYMBOLS, dtype=jnp.int32)
    target_hits = (target_ids[:, None] == symbols[None, :]) & (pad_mask[:, None] > 0)
    correct_hits = target_hits & (predicted == target_ids)[:, None]
    counts = jnp.stack([jnp.sum(target_hits, 0), jnp.sum(correct_hits, 0)]).astype(F32)
    small = [bias_grad, sums, counts]
    packed = small_sum(jnp.concatenate([s.reshape(-1) for s in small]))
    results = []
    at = 0
    for s in small:
        results.append(packed[at : at + s.size].reshape(s.shape))
        at += s.size
    bias_grad, sums, counts = results
    return (
        whole([f[4] for f in feed])[None],
        input_grads[None],
        joint_sum[None],
        output_sum[None],
        up_sum[None],
        bias_grad[None],
        down_sum[None],
        sums[0][None],
        sums[1][None],
        counts.astype(jnp.int32),
    )


def solution(mesh):
    return jax.shard_map(
        shards,
        mesh=mesh,
        in_specs=(
            P("dp", "tensor"),
            P("dp", "tensor"),
            P("dp"),
            P("dp"),
            P("dp"),
            P("dp"),
            P("section", None, None, None, "tensor"),
            P("section", None, "tensor", None),
            P("section", None, None, "tensor"),
            P("section", None, "tensor"),
            P("section", None, "tensor", None),
            P("section", None, None),
            P("section", None, None),
        ),
        out_specs=(
            P("section", "dp", "tensor"),
            P("section", "dp", "tensor"),
            P("section", None, None, None, "tensor"),
            P("section", None, "tensor", None),
            P("section", None, None, "tensor"),
            P("section", None, "tensor"),
            P("section", None, "tensor", None),
            P("section", None, None),
            P("section", None, None),
            P(),
        ),
        check_vma=False,
    )
```

```python
import functools

import jax
import jax.numpy as jnp
from jax import lax
from jax.experimental import pallas as pl
from jax.experimental.pallas import tpu as pltpu
from jax.sharding import PartitionSpec as P

HEAD_DIM = 64
SYMBOLS = 24
SEQ = 160
PARTS = 3
RING = 8
BLOCK = 384
TAIL = 16
EPS = 1e-05
SCALE = HEAD_DIM**-0.5
VMEM_LIMIT = 14 * 1024 * 1024

root_half = 0.7071067811865476
root_two_pi = 0.3989422804014327
BF = jnp.bfloat16
F32 = jnp.float32


def swap(value):
    return lax.ppermute(value, "tensor", [(0, 1), (1, 0)])


def dot(a, b):
    return jnp.dot(a, b, preferred_element_type=F32)


def dot_rows(a, b):
    return lax.dot_general(a, b, (((1,), (1,)), ((), ())), preferred_element_type=F32)


def dot_cols(a, b):
    return lax.dot_general(a, b, (((0,), (0,)), ((), ())), preferred_element_type=F32)


def in_order(core, own, other):
    first = core == 0
    return jnp.concatenate(
        [jnp.where(first, own, other), jnp.where(first, other, own)], axis=1
    )


def own_part(core, value):
    half = value.shape[1] // 2
    return jnp.where(core == 0, value[:, :half], value[:, half:])


def normalise(rows):
    centred = rows - jnp.mean(rows, axis=-1, keepdims=True)
    inv_root = lax.rsqrt(jnp.mean(centred * centred, axis=-1, keepdims=True) + EPS)
    return centred * inv_root, inv_root


def norm_back(grads, normal, inv_root, gain):
    scaled = grads * gain
    inner = (
        scaled
        - jnp.mean(scaled, axis=-1, keepdims=True)
        - normal * jnp.mean(scaled * normal, axis=-1, keepdims=True)
    )
    return inner * inv_root


def pair_spans(width):
    return [slice(at, at + 2 * HEAD_DIM) for at in range(0, width, 2 * HEAD_DIM)]


def left_head():
    return lax.broadcasted_iota(jnp.int32, (1, 2 * HEAD_DIM), 1) < HEAD_DIM


def pair_scores(first, second):
    left = left_head().astype(BF)
    both = jnp.concatenate([first * left, first * (1 - left)], axis=0)
    return dot_rows(both, second).reshape(2, SEQ, SEQ)


def pair_product(matrices, block):
    found = dot(matrices.reshape(2 * SEQ, SEQ), block)
    return jnp.where(left_head(), found[:SEQ], found[SEQ:]).astype(BF)


def turned(matrices):
    return jnp.concatenate([matrices[0].T, matrices[1].T], axis=0)


def attn_forward_kernel(choose, keep, start, count, marks, *refs):
    refs = list(refs)
    own, other = refs.pop(0), refs.pop(0)
    if choose:
        own_late, other_late = refs.pop(0), refs.pop(0)
    joint, output = refs.pop(0), refs.pop(0)
    chain = pl.program_id(0)
    tag = marks[3 + start + chain]
    core = marks[1]
    a, b = own[...], other[...]
    if choose:
        early = marks[0] == 0
        a = jnp.where(early, a, own_late[...])
        b = jnp.where(early, b, other_late[...])
    rows = in_order(core, a, b)
    q, k, v = [dot(rows, joint[tag, j]).astype(BF) for j in range(3)]
    key_live = lax.broadcasted_iota(jnp.int32, (1, SEQ, 1), 1) < marks[3 + count + start + chain]
    spans = pair_spans(q.shape[1])
    scores = [pair_scores(k[:, s], q[:, s] * jnp.asarray(SCALE, BF)) for s in spans]
    probs = []
    for found in scores:
        found = jnp.where(key_live, found, -1000000000.0)
        shifted = jnp.exp(found - jnp.max(found, axis=1, keepdims=True))
        probs.append((shifted * (1.0 / jnp.sum(shifted, axis=1, keepdims=True))).astype(BF))
    mixed = jnp.concatenate(
        [pair_product(turned(p), v[:, s]) for p, s in zip(probs, spans)], axis=1
    )
    refs[0][...] = rows
    refs[1][...] = dot(mixed, output[tag]).astype(BF)
    if keep:
        refs[2][...] = jnp.concatenate([q, k, v], axis=1)
        for at, found in enumerate(probs):
            refs[3][0, 2 * at : 2 * at + 2] = found
        refs[4][...] = mixed


def feed_forward_kernel(keep, start, marks, rows, part, other, gains, shifts, up, bias, down, *outs):
    tag = marks[3 + start + pl.program_id(0)]
    total = rows[...].astype(F32) + (part[...].astype(F32) + other[...].astype(F32))
    normal, inv_root = normalise(total)
    low = (normal * gains[0:1] + shifts[0:1]).astype(BF)
    pre = dot(low, up[tag]) + jnp.where(tag == 0, bias[0:1], bias[1:2]).astype(F32)
    cdf = 0.5 * (1.0 + lax.erf(pre * root_half))
    hidden = (pre * cdf).astype(BF)
    outs[0][...] = dot(hidden, down[tag]).astype(BF)
    outs[1][...] = normal
    if keep:
        outs[2][...] = inv_root
        outs[3][...] = low
        outs[4][...] = hidden
        outs[5][...] = (cdf + pre * jnp.exp(-0.5 * pre * pre) * root_two_pi).astype(BF)


def second_norm(normal, part, other, gains, shifts):
    first = normal[...] * gains[0:1] + shifts[0:1]
    return normalise(first + (part[...].astype(F32) + other[...].astype(F32)))


def last_norm_kernel(marks, normal, part, other, gains, shifts, out):
    second, _ = second_norm(normal, part, other, gains, shifts)
    out[...] = own_part(marks[1], (second * gains[1:2] + shifts[1:2]).astype(BF))


def carry_over(carried, sums):
    @pl.when(pl.program_id(0) == 0)
    def _():
        sums[...] = carried[...]


def add_sums(grads, normal, carried, sums):
    carry_over(carried, sums)
    sums[0] += jnp.sum(grads * normal, axis=0, keepdims=True)
    sums[1] += jnp.sum(grads, axis=0, keepdims=True)


def feed_back_kernel(last, start, marks, *refs):
    refs = list(refs)
    normal, part, other, gains, shifts, own_cot, other_cot = refs[:7]
    refs = refs[7:]
    tag = marks[3 + start + pl.program_id(0)]
    core = marks[1]
    a, b = own_cot[...], other_cot[...]
    if last:
        late = marks[0] == 1
        a = jnp.where(late, a, refs.pop(0)[...])
        b = jnp.where(late, b, refs.pop(0)[...])
    slope, up, down = refs[:3]
    refs = refs[3:]
    if last:
        carried_sums, carried_bias = refs.pop(0), refs.pop(0)
    outs = refs
    grads = in_order(core, a, b).astype(F32)
    second, inv_root = second_norm(normal, part, other, gains, shifts)
    back = norm_back(grads, second, inv_root, gains[1:2])
    low = back.astype(BF)
    d_pre = (dot_rows(low, down[tag]) * slope[...].astype(F32)).astype(BF)
    outs[0][...] = back
    outs[1][...] = dot_rows(d_pre, up[tag]).astype(BF)
    if last:
        outs[2][...] = low
        outs[3][...] = d_pre
        outs[4][...] = own_part(core, (second * gains[1:2] + shifts[1:2]).astype(BF))
        add_sums(grads, second, carried_sums, outs[5])
        carry_over(carried_bias, outs[6])
        outs[6][tag] += jnp.sum(d_pre.astype(F32), axis=0, keepdims=True)


def attn_back_kernel(
    last, start, marks, back, part, other, normal, inv_root, gains, joined, probs, joint, output, *outs
):
    if last:
        carried, *outs = outs
    tag = marks[3 + start + pl.program_id(0)]
    core = marks[1]
    grads = back[...] + (part[...].astype(F32) + other[...].astype(F32))
    back_one = norm_back(grads, normal[...], inv_root[...], gains[0:1])
    low = back_one.astype(BF)
    d_mixed = dot_rows(low, output[tag]).astype(BF)
    width = d_mixed.shape[1]
    q, k, v = [joined[:, j * width : (j + 1) * width] for j in range(3)]
    spans = pair_spans(width)
    d_probs = [pair_scores(v[:, s], d_mixed[:, s]) for s in spans]
    held = [probs[0, 2 * at : 2 * at + 2] for at in range(len(spans))]
    d_scores = []
    for found, kept in zip(d_probs, held):
        wide = kept.astype(F32)
        inner = jnp.sum(wide * found, axis=1, keepdims=True)
        d_scores.append((wide * (found - inner)).astype(BF))
    scale = jnp.asarray(SCALE, BF)
    d_k = [pair_product(d, q[:, s]) * scale for d, s in zip(d_scores, spans)]
    d_v = [pair_product(h, d_mixed[:, s]) for h, s in zip(held, spans)]
    d_q = [pair_product(turned(d), k[:, s]) * scale for d, s in zip(d_scores, spans)]
    pieces = [d_q, d_k, d_v]
    blocks = [jnp.concatenate(p, axis=1) for p in pieces]
    d_rows = sum(dot_rows(blocks[j], joint[tag, j]) for j in range(3)).astype(BF)
    outs[0][...] = own_part(core, back_one) + own_part(core, d_rows).astype(F32)
    outs[1][...] = own_part(1 - core, d_rows)
    if last:
        outs[2][...] = low
        outs[3][...] = jnp.concatenate(blocks, axis=1)
        add_sums(grads, normal[...], carried, outs[4])


def behind(kernel, taken, ignored):
    def call(marks, *refs):
        kernel(marks, *refs[:taken], *refs[taken + ignored :])

    return call


ANY = pl.BlockSpec(memory_space=pl.ANY)
HBM = pl.BlockSpec(memory_space=pltpu.HBM)
TOKEN = jax.ShapeDtypeStruct((8, 128), F32)
TOKEN_BLOCK = pl.BlockSpec((8, 128), lambda *_: (0, 0))


def sign_off(token):
    token[...] = jnp.zeros_like(token)


class Order:
    def __init__(self):
        self.tokens = ()

    def run(self, call, *args):
        *results, token = call(*args, self.tokens)
        self.tokens = (token,)
        return results

    def after(self, value):
        return lax.optimization_barrier((value, *self.tokens))[0]


def run_chains(kernel, name, marks, chains, ins, outs, flops, after):
    specs = []
    for array, kind, first in ins:
        if kind == "rows":
            specs.append(
                pl.BlockSpec((SEQ, array.shape[1]), lambda i, *_, first=first: (first + i, 0))
            )
        elif kind == "chain":
            rest = array.shape[1:]
            specs.append(
                pl.BlockSpec(
                    (1,) + rest, lambda i, *_, first=first, n=len(rest): (first + i,) + (0,) * n
                )
            )
        else:
            specs.append(pl.BlockSpec(memory_space=pltpu.VMEM))
    shapes, out_specs = [], []
    for trailing, dtype, kind in outs:
        if kind == "rows":
            shapes.append(jax.ShapeDtypeStruct((chains * SEQ,) + trailing, dtype))
            out_specs.append(pl.BlockSpec((SEQ,) + trailing, lambda i, *_: (i, 0)))
        elif kind == "chain":
            shapes.append(jax.ShapeDtypeStruct((chains,) + trailing, dtype))
            out_specs.append(
                pl.BlockSpec((1,) + trailing, lambda i, *_, n=len(trailing): (i,) + (0,) * n)
            )
        else:
            shapes.append(jax.ShapeDtypeStruct(trailing, dtype))
            out_specs.append(pl.BlockSpec(trailing, lambda i, *_, n=len(trailing): (0,) * n))
    moved = sum(a.size * a.dtype.itemsize for a, _, _ in ins)
    specs += [ANY] * len(after)
    shapes.append(TOKEN)
    out_specs.append(TOKEN_BLOCK)

    def signing(marks, *refs):
        sign_off(refs[-1])
        kernel(marks, *refs[:-1])

    return pl.pallas_call(
        behind(signing, len(ins), len(after)),
        grid_spec=pltpu.PrefetchScalarGridSpec(
            num_scalar_prefetch=1, grid=(chains,), in_specs=specs, out_specs=out_specs
        ),
        out_shape=shapes,
        compiler_params=pltpu.CompilerParams(vmem_limit_bytes=VMEM_LIMIT),
        cost_estimate=pl.CostEstimate(
            flops=flops // 1000, bytes_accessed=moved // 1000, transcendentals=0
        ),
        name=name,
    )(marks, *[a for a, _, _ in ins], *after)


def ring_spot(marks, step, way):
    return lax.rem(marks[2] + 2 * RING + way * step, RING)


def span(at):
    return pl.ds(pl.multiple_of(at * BLOCK, BLOCK), BLOCK)


def cut(ref, at):
    return ref[:, span(at)]


def set_rows(marks, block, which):
    pieces = []
    for chain in range(block.shape[0] // SEQ):
        piece = block[chain * SEQ : (chain + 1) * SEQ]
        pieces.append(jnp.where(marks[3 + chain] == which, piece, jnp.zeros_like(piece)))
    return jnp.concatenate(pieces, axis=0)


def fetch(lists, scratch, sems):
    @pl.when(pl.program_id(0) == 0)
    def _():
        copies = []
        for refs, held in zip(lists, scratch):
            rows = held.shape[0] // len(refs)
            for at, ref in enumerate(refs):
                copies.append(
                    pltpu.make_async_copy(
                        ref, held.at[at * rows : (at + 1) * rows], sems.at[len(copies)]
                    )
                )
        for copy in copies:
            copy.start()
        for copy in copies:
            copy.wait()


def feed_shard(marks, which, hidden, d_down, low, d_pre):
    return (
        dot_cols(set_rows(marks, hidden, which), d_down).astype(BF),
        dot_cols(set_rows(marks, low, which), d_pre).astype(BF),
    )


def first_shard_kernel(parts, marks, *refs):
    out, token = refs[8 * parts :]
    sign_off(token)
    for which in range(2):
        blocks = []
        for n in range(4):
            at = (4 * which + n) * parts
            blocks.append(jnp.concatenate([ref[...] for ref in refs[at : at + parts]], axis=0))
        out[which, :BLOCK], out[which, BLOCK:] = feed_shard(marks, which, *blocks)


def run_first_shard(marks, lists, after):
    specs, ins = [], []
    for way in (-1, 1):
        for n, arrays in enumerate(lists):
            for array in arrays:

                def index(i, marks, n=n, way=way):
                    spot = ring_spot(marks, 1, way)
                    return 0, (lax.div(spot, 2) if n in (0, 3) else lax.rem(spot, 2))

                specs.append(pl.BlockSpec((array.shape[0], BLOCK), index))
                ins.append(array)
    shape = (2, 2 * BLOCK, BLOCK)
    return pl.pallas_call(
        behind(functools.partial(first_shard_kernel, len(lists[0])), len(ins), len(after)),
        grid_spec=pltpu.PrefetchScalarGridSpec(
            num_scalar_prefetch=1,
            grid=(1,),
            in_specs=specs + [ANY] * len(after),
            out_specs=[pl.BlockSpec(shape, lambda i, *_: (0, 0, 0)), TOKEN_BLOCK],
        ),
        out_shape=[jax.ShapeDtypeStruct(shape, BF), TOKEN],
        compiler_params=pltpu.CompilerParams(vmem_limit_bytes=20 * 1024 * 1024),
        name="first_shard",
    )(marks, *ins, *after)


def feed_weights_kernel(first, parts, marks, *refs):
    out, token, hidden, d_down, low, d_pre, sems = refs[4 * parts :]
    sign_off(token)
    fetch([refs[n * parts : (n + 1) * parts] for n in range(4)], refs[4 * parts + 2 : -1], sems)
    step = first + pl.program_id(0) + 1
    for which, way in ((0, -1), (1, 1)):
        spot = ring_spot(marks, step, way)
        far, near = lax.div(spot, 2), lax.rem(spot, 2)
        out[0, which, :BLOCK], out[0, which, BLOCK:] = feed_shard(
            marks, which, cut(hidden, far), cut(d_down, near), cut(low, near), cut(d_pre, far)
        )


def two_halves(value):
    high = value.astype(BF).astype(F32)
    return jnp.concatenate([high, value - high], axis=0).astype(BF)


def one_whole(rows):
    rows = rows.astype(F32)
    return rows[: TAIL // 2] + rows[TAIL // 2 :]


def count_rows(live, predicted, targets):
    symbols = lax.broadcasted_iota(jnp.int32, (128, live.shape[1]), 0)
    hits = (targets[...] == symbols) & (live[...] > 0)
    right = hits & (predicted[...] == targets[...])
    ones = jnp.ones((8, live.shape[1]), BF)
    found = [dot_rows(ones, h.astype(F32).astype(BF)) for h in (hits, right)]
    return jnp.concatenate(found + [jnp.zeros_like(found[0])], axis=1)[0:1]


def attn_weights_kernel(first, parts, marks, *refs):
    bias, *sums, live, predicted, targets, out, token = refs[4 * parts : -5]
    rows, d_joined, mixed, d_attn, sems = refs[-5:]
    fetch([refs[n * parts : (n + 1) * parts] for n in range(4)], refs[-5:-1], sems)
    sign_off(token)
    step = first + pl.program_id(0) + 1
    for which, way in ((0, -1), (1, 1)):
        spot = ring_spot(marks, step, way)
        far, near = lax.div(spot, 2), lax.rem(spot, 2)

        @pl.when(far < 3)
        def _():
            out[0, which, :BLOCK] = dot_cols(
                set_rows(marks, cut(rows, near), which), cut(d_joined, far)
            ).astype(BF)

        @pl.when(far == 3)
        def _():
            out[0, which, :BLOCK] = dot_cols(
                set_rows(marks, mixed[...], which), cut(d_attn, near)
            ).astype(BF)

        early = far < 2
        small = jnp.where(
            early,
            bias[which, :, span(jnp.where(early, spot, 0))],
            sums[which][jnp.where(early, 0, far - 2), :, span(near)],
        )
        place = lax.broadcasted_iota(jnp.int32, (TAIL // 2, BLOCK), 0)
        small = jnp.where(place == 0, small, 0.0)
        out[0, which, BLOCK:] = two_halves(small)
        if which == 0:

            @pl.when(spot == 0)
            def _():
                counts = count_rows(live, predicted, targets)
                out[0, which, BLOCK:] = two_halves(jnp.where(place == 1, counts, small))


def run_weights(kernel, name, marks, first, steps, lists, rest, rows_out, after):
    ins = [a for arrays in lists for a in arrays] + list(rest)
    shape = (2, rows_out, BLOCK)
    return pl.pallas_call(
        behind(functools.partial(kernel, first, len(lists[0])), len(ins), len(after)),
        grid_spec=pltpu.PrefetchScalarGridSpec(
            num_scalar_prefetch=1,
            grid=(steps,),
            in_specs=[HBM] * (len(ins) - len(rest))
            + [pl.BlockSpec(memory_space=pltpu.VMEM)] * len(rest)
            + [ANY] * len(after),
            out_specs=[pl.BlockSpec((1,) + shape, lambda i, *_: (i, 0, 0, 0)), TOKEN_BLOCK],
            scratch_shapes=[
                pltpu.VMEM((sum(a.shape[0] for a in arrays), arrays[0].shape[1]), BF)
                for arrays in lists
            ]
            + [pltpu.SemaphoreType.DMA((len(ins) - len(rest),))],
        ),
        out_shape=[jax.ShapeDtypeStruct((steps,) + shape, BF), TOKEN],
        compiler_params=pltpu.CompilerParams(vmem_limit_bytes=20 * 1024 * 1024),
        cost_estimate=pl.CostEstimate(
            flops=steps * 4 * rows_out * BLOCK,
            bytes_accessed=steps * rows_out,
            transcendentals=0,
        ),
        name=name,
    )(marks, *ins, *after)


def add_kernel(tail, ahead, back, local, out_ahead, out_back, token):
    sign_off(token)
    for which, (ref, out) in enumerate(((ahead, out_ahead), (back, out_back))):
        total = ref[...].astype(F32) + local[0, which].astype(F32)
        out[...] = total.astype(BF)
        if tail:
            out[tail:] = two_halves(one_whole(total[tail:]))


def add_step(pair, local, at, after):
    shape = local.shape[2:]
    block = pl.BlockSpec(shape, lambda i: (0, 0))

    tail = BLOCK if shape[0] == BLOCK + TAIL else 0

    def call(*refs):
        add_kernel(tail, *refs[:3], *refs[3 + len(after) :])

    return pl.pallas_call(
        call,
        grid=(1,),
        in_specs=[block, block, pl.BlockSpec((1, 2) + shape, lambda i: (at, 0, 0, 0))]
        + [ANY] * len(after),
        out_specs=[block, block, TOKEN_BLOCK],
        out_shape=[jax.ShapeDtypeStruct(shape, BF)] * 2 + [TOKEN],
        compiler_params=pltpu.CompilerParams(vmem_limit_bytes=VMEM_LIMIT),
        cost_estimate=pl.CostEstimate(
            flops=2 * shape[0] * shape[1],
            bytes_accessed=12 * shape[0] * shape[1],
            transcendentals=0,
        ),
        name="ring_add",
    )(*pair, local, *after)


def feed_place_kernel(step, marks, ahead, back, outs, wide, sems):
    down, up = outs
    copies = []
    for which, (ref, way) in enumerate(((ahead, -1), (back, 1))):
        spot = ring_spot(marks, step, way)
        far, near = lax.div(spot, 2), lax.rem(spot, 2)
        wide[which] = ref[...].astype(F32)
        copies += [
            pltpu.make_async_copy(
                wide.at[which, :BLOCK], down.at[which, span(far), span(near)], sems.at[2 * which]
            ),
            pltpu.make_async_copy(
                wide.at[which, BLOCK:], up.at[which, span(near), span(far)], sems.at[2 * which + 1]
            ),
        ]
        for copy in copies[-2:]:
            copy.start()
    for copy in copies:
        copy.wait()


def attn_place_kernel(step, marks, ahead, back, outs, wide, sems):
    joint, output, small = outs
    copies = []
    for which, (ref, way) in enumerate(((ahead, -1), (back, 1))):
        spot = ring_spot(marks, step, way)
        far, near = lax.div(spot, 2), lax.rem(spot, 2)
        wide[which] = ref[...].astype(F32)
        wide[which, BLOCK : BLOCK + TAIL // 2] = one_whole(ref[BLOCK:])
        copy = pltpu.make_async_copy(
            wide.at[which, BLOCK : BLOCK + TAIL // 2], small.at[which, spot], sems.at[2 + which]
        )
        copy.start()
        copies.append(copy)

        @pl.when(far < 3)
        def _():
            copy = pltpu.make_async_copy(
                wide.at[which, :BLOCK], joint.at[which, far, span(near)], sems.at[which]
            )
            copy.start()
            copy.wait()

        @pl.when(far == 3)
        def _():
            copy = pltpu.make_async_copy(
                wide.at[which, :BLOCK], output.at[which, :, span(near)], sems.at[which]
            )
            copy.start()
            copy.wait()

    for copy in copies:
        copy.wait()


def place_step(kernel, name, marks, step, pair, held, after):
    shape = pair[0].shape
    block = pl.BlockSpec(shape, lambda i, *_: (0, 0))

    count = len(held)

    def call(marks, ahead, back, *refs):
        refs = refs[count + len(after) :]
        sign_off(refs[count])
        kernel(step, marks, ahead, back, refs[:count], *refs[count + 1 :])

    return pl.pallas_call(
        call,
        grid_spec=pltpu.PrefetchScalarGridSpec(
            num_scalar_prefetch=1,
            grid=(1,),
            in_specs=[block, block] + [HBM] * count + [ANY] * len(after),
            out_specs=[HBM] * count + [TOKEN_BLOCK],
            scratch_shapes=[pltpu.VMEM((2,) + shape, F32), pltpu.SemaphoreType.DMA((4,))],
        ),
        out_shape=[jax.ShapeDtypeStruct(h.shape, h.dtype) for h in held] + [TOKEN],
        input_output_aliases={3 + i: i for i in range(count)},
        compiler_params=pltpu.CompilerParams(vmem_limit_bytes=VMEM_LIMIT),
        cost_estimate=pl.CostEstimate(
            flops=0, bytes_accessed=12 * shape[0] * shape[1], transcendentals=0
        ),
        name=name,
    )(marks, *pair, *held, *after)


def unwritten(*shapes):
    return pl.pallas_call(
        lambda *refs: None,
        out_specs=[HBM] * len(shapes),
        out_shape=[jax.ShapeDtypeStruct(s, F32) for s in shapes],
        compiler_params=pltpu.CompilerParams(vmem_limit_bytes=1024 * 1024),
        name="unwritten",
    )()


class Ring:
    def __init__(self):
        self.count = lax.axis_size("dp")
        assert self.count % RING == 0
        order = list(range(0, RING, 2)) + list(range(1, RING, 2))[::-1]
        rank = lax.rem(lax.axis_index("dp"), RING)
        self.place = jnp.zeros((), jnp.int32)
        for at, member in enumerate(order):
            self.place = jnp.where(rank == member, at, self.place)
        self.ahead = [
            (base + order[i], base + order[(i + 1) % RING])
            for base in range(0, self.count, RING)
            for i in range(RING)
        ]
        self.back = [(b, a) for a, b in self.ahead]

    def send(self, pair):
        return lax.ppermute(pair[0], "dp", self.ahead), lax.ppermute(pair[1], "dp", self.back)

    def across(self, pair):
        result = []
        for value in pair:
            total = value.astype(F32)
            moving = value
            for _ in range(self.count // RING - 1):
                pairs = [(i, (i + RING) % self.count) for i in range(self.count)]
                moving = lax.ppermute(moving, "dp", pairs)
                total = total + moving.astype(F32)
            low = total.astype(BF)
            if total.shape[0] == BLOCK + TAIL and self.count > RING:
                tail = two_halves(one_whole(total[BLOCK:]))
                low = jnp.concatenate([low[:BLOCK], tail], axis=0)
            result.append(low)
        return result


def shards(
    chain_inputs,
    cotangent,
    chain_tags,
    pad_mask,
    predicted,
    target_ids,
    joint_proj,
    output_proj,
    up_proj,
    up_bias,
    down_proj,
    norm_gain,
    norm_shift,
):
    section = lax.axis_index("section")
    core = lax.axis_index("tensor")
    tokens, half = chain_inputs.shape
    width = 2 * half
    all_chains = tokens // SEQ
    chains = all_chains // PARTS
    tags = (chain_tags > 0).astype(jnp.int32)
    ring = Ring()
    chain_of = jnp.arange(tokens, dtype=jnp.int32)[None] // SEQ
    belongs = chain_of == jnp.arange(all_chains, dtype=jnp.int32)[:, None]
    lengths = jnp.sum(jnp.where(belongs, pad_mask[None], 0), axis=1)
    marks = jnp.concatenate([jnp.stack([section, core, ring.place]).astype(jnp.int32), tags, lengths])
    small = [ids.reshape(1, tokens) for ids in (pad_mask, predicted, target_ids)]
    joint = joint_proj[0].transpose(0, 2, 1, 3)
    output, up, bias, down = output_proj[0], up_proj[0], up_bias[0], down_proj[0]
    gains, shifts = norm_gain[0], norm_shift[0]
    units = up.shape[2]
    local = output.shape[1]
    heads = local // HEAD_DIM
    rows = chains * SEQ
    attn_flops = 2 * rows * (width * 4 * local + 2 * local * SEQ)
    feed_flops = 2 * rows * width * 2 * units

    cot_other = swap(cotangent)
    rows_other = swap(chain_inputs)

    order = Order()

    def attn_forward(p, late, keep):
        start = p * chains
        ins = [(chain_inputs, "rows", start), (rows_other, "rows", start)]
        if late is not None:
            ins += [(late[0], "rows", 0), (late[1], "rows", 0)]
        ins += [(joint, "whole", 0), (output, "whole", 0)]
        outs = [((width,), BF, "rows"), ((width,), BF, "rows")]
        if keep:
            outs += [
                ((3 * local,), BF, "rows"),
                ((heads, SEQ, SEQ), BF, "chain"),
                ((local,), BF, "rows"),
            ]
        kernel = functools.partial(
            attn_forward_kernel, late is not None, keep, start, all_chains
        )
        found = order.run(
            run_chains, kernel, "attn_forward", marks, chains, ins, outs, attn_flops
        )
        names = ("rows", "part", "joined", "probs", "mixed")
        kept = dict(zip(names, found))
        kept["part_other"] = swap(kept["part"])
        return kept

    def feed_forward(p, kept, keep):
        ins = [(kept[n], "rows", 0) for n in ("rows", "part", "part_other")]
        ins += [(a, "whole", 0) for a in (gains, shifts, up, bias, down)]
        outs = [((width,), BF, "rows"), ((width,), F32, "rows")]
        if keep:
            outs += [
                ((1,), F32, "rows"),
                ((width,), BF, "rows"),
                ((units,), BF, "rows"),
                ((units,), BF, "rows"),
            ]
        kernel = functools.partial(feed_forward_kernel, keep, p * chains)
        found = order.run(
            run_chains, kernel, "feed_forward", marks, chains, ins, outs, feed_flops
        )
        names = ("down", "normal", "inv_root", "low", "hidden", "slope")
        kept.update(zip(names, found))
        kept["down_other"] = swap(kept["down"])

    def last_norm(p, kept):
        ins = [(kept[n], "rows", 0) for n in ("normal", "down", "down_other")]
        ins += [(gains, "whole", 0), (shifts, "whole", 0)]
        outs = [((half,), BF, "rows")]
        found = order.run(
            run_chains, last_norm_kernel, "last_norm", marks, chains, ins, outs, 0
        )
        return lax.ppermute(found[0], "section", [(0, 1), (1, 0)])

    def feed_back(p, kept, late, carried=None):
        ins = [(kept[n], "rows", 0) for n in ("normal", "down", "down_other")]
        ins += [(gains, "whole", 0), (shifts, "whole", 0)]
        ins += [(cotangent, "rows", p * chains), (cot_other, "rows", p * chains)]
        if late is not None:
            ins += [(late[0], "rows", 0), (late[1], "rows", 0)]
        ins += [(kept["slope"], "rows", 0), (up, "whole", 0), (down, "whole", 0)]
        if late is not None:
            ins += [(carried["sums"], "whole", 0), (carried["bias"], "whole", 0)]
        outs = [((width,), F32, "rows"), ((width,), BF, "rows")]
        if late is not None:
            outs += [
                ((width,), BF, "rows"),
                ((units,), BF, "rows"),
                ((half,), BF, "rows"),
                ((2, 1, width), F32, "whole"),
                ((2, 1, units), F32, "whole"),
            ]
        kernel = functools.partial(feed_back_kernel, late is not None, p * chains)
        found = order.run(
            run_chains, kernel, "feed_back", marks, chains, ins, outs, feed_flops
        )
        names = ("back", "part", "d_down", "d_pre", "outputs", "sums", "bias")
        found = dict(zip(names, found))
        found["part_other"] = swap(found["part"])
        return found

    def attn_back(p, kept, feed, last, carried=None):
        ins = [(feed[n], "rows", 0) for n in ("back", "part", "part_other")]
        ins += [(kept["normal"], "rows", 0), (kept["inv_root"], "rows", 0), (gains, "whole", 0)]
        ins += [(kept["joined"], "rows", 0), (kept["probs"], "chain", 0)]
        ins += [(joint, "whole", 0), (output, "whole", 0)]
        if last:
            ins.append((carried["sums"], "whole", 0))
        outs = [((half,), F32, "rows"), ((half,), BF, "rows")]
        if last:
            outs += [
                ((width,), BF, "rows"),
                ((3 * local,), BF, "rows"),
                ((2, 1, width), F32, "whole"),
            ]
        kernel = functools.partial(attn_back_kernel, last, p * chains)
        found = order.run(
            run_chains, kernel, "attn_back", marks, chains, ins, outs, attn_flops
        )
        names = ("mine", "theirs", "d_attn", "d_joined", "sums")
        found = dict(zip(names, found))
        found["grads"] = found["mine"] + swap(found["theirs"]).astype(F32)
        return found

    early, sent, late, kept = {}, {}, {}, {}

    def start_early(p):
        early[p] = attn_forward(p, None, False)

    def feed_early(p):
        feed_forward(p, early[p], False)

    def norm_early(p):
        sent[p] = last_norm(p, early[p])

    def receive(p):
        moved = order.after(sent[p])
        late[p] = (moved, swap(moved))

    def start_kept(p):
        kept[p] = attn_forward(p, late[p], True)

    def feed_kept(p):
        feed_forward(p, kept[p], True)

    first_feed, first_attn, sent_back, late_back = {}, {}, {}, {}
    no_sums = jnp.zeros((2, 1, width), F32)
    feed = {-1: dict(sums=no_sums, bias=jnp.zeros((2, 1, units), F32))}
    attn = {-1: dict(sums=no_sums)}

    def feed_first(p):
        first_feed[p] = feed_back(p, kept[p], None)

    def attn_first(p):
        first_attn[p] = attn_back(p, kept[p], first_feed[p], False)
        total = first_attn[p]["grads"].astype(BF)
        sent_back[p] = lax.ppermute(total, "section", [(1, 0), (0, 1)])

    def receive_back(p):
        moved = order.after(sent_back[p])
        late_back[p] = (moved, swap(moved))

    def feed_last(p):
        feed[p] = feed_back(p, kept[p], late_back[p], feed[p - 1])

    def attn_last(p):
        attn[p] = attn_back(p, kept[p], feed[p], True, attn[p - 1])

    for step, p in (
        (start_early, 0),
        (start_early, 1),
        (feed_early, 0),
        (start_early, 2),
        (norm_early, 0),
        (feed_early, 1),
        (norm_early, 1),
        (receive, 0),
        (feed_early, 2),
        (norm_early, 2),
        (receive, 1),
        (start_kept, 0),
        (start_kept, 1),
        (receive, 2),
        (feed_kept, 0),
        (start_kept, 2),
        (feed_kept, 1),
        (feed_kept, 2),
        (feed_first, 0),
        (feed_first, 1),
        (attn_first, 0),
        (feed_first, 2),
        (attn_first, 1),
        (receive_back, 0),
        (attn_first, 2),
        (feed_last, 0),
        (receive_back, 1),
        (feed_last, 1),
        (receive_back, 2),
        (feed_last, 2),
    ):
        step(p)
    parts = range(PARTS)
    feed_lists = [
        [kept[p]["hidden"] for p in parts],
        [feed[p]["d_down"] for p in parts],
        [kept[p]["low"] for p in parts],
        [feed[p]["d_pre"] for p in parts],
    ]

    def feed_weights(first, steps):
        return order.run(
            run_weights,
            feed_weights_kernel,
            "feed_weights",
            marks,
            first,
            steps,
            feed_lists,
            [],
            2 * BLOCK,
        )[0]

    def add_local(pair, local, at):
        return order.run(add_step, pair, local, at)

    first_shards = order.run(run_first_shard, marks, feed_lists)[0]
    feed_pair = ring.send((first_shards[0], first_shards[1]))
    feed_local = feed_weights(1, RING - 1)
    feed_pair = ring.send(add_local(feed_pair, feed_local, 0))
    attn_last(0)
    attn_last(1)
    feed_pair = ring.send(add_local(feed_pair, feed_local, 1))
    attn_last(2)
    attn_lists = [
        [kept[p]["rows"] for p in parts],
        [attn[p]["d_joined"] for p in parts],
        [kept[p]["mixed"] for p in parts],
        [attn[p]["d_attn"] for p in parts],
    ]

    small = [feed[PARTS - 1]["bias"], attn[PARTS - 1]["sums"], feed[PARTS - 1]["sums"], *small]

    def attn_weights(first, steps):
        return order.run(
            run_weights,
            attn_weights_kernel,
            "attn_weights",
            marks,
            first,
            steps,
            attn_lists,
            small,
            BLOCK + TAIL,
        )[0]

    first_shards = attn_weights(0, 1)
    attn_pair = ring.send((first_shards[0, 0], first_shards[0, 1]))
    feed_pair = ring.send(add_local(feed_pair, feed_local, 2))
    attn_local = attn_weights(1, RING - 1)
    streams = [
        dict(
            pair=attn_pair,
            local=attn_local,
            sent=1,
            kernel=attn_place_kernel,
            name="attn_place",
            held=unwritten((2, 3, width, local), (2, local, width), (2, RING, 8, BLOCK)),
        ),
        dict(
            pair=feed_pair,
            local=feed_local,
            sent=4,
            kernel=feed_place_kernel,
            name="feed_place",
            held=unwritten((2, units, width), (2, width, units)),
        ),
    ]

    def turn(stream):
        sent = stream["sent"]
        *pair, token = lax.optimization_barrier((*stream["pair"], *order.tokens))
        order.tokens = (token,)
        if sent < RING:
            pair = add_local(pair, stream["local"], sent - 1)
            if sent == RING - 1:
                pair = ring.across(pair)
        stream["pair"] = ring.send(pair) if sent < 2 * RING - 2 else None
        if sent >= RING - 1:
            stream["held"] = order.run(
                place_step,
                stream["kernel"],
                stream["name"],
                marks,
                sent - RING + 1,
                pair,
                stream["held"],
            )
        stream["sent"] += 1

    attn_stream, feed_stream = streams
    while attn_stream["pair"] is not None or feed_stream["pair"] is not None:
        if attn_stream["pair"] is not None:
            turn(attn_stream)
        if attn_stream["sent"] < feed_stream["sent"]:
            turn(attn_stream)
        if feed_stream["pair"] is not None:
            turn(feed_stream)
    joint_out, output_out, small_out = attn_stream["held"]
    down_out, up_out = feed_stream["held"]

    def whole(pieces):
        return jnp.concatenate(pieces, axis=0)

    input_grads = whole([attn[p]["grads"] for p in parts])
    rows = small_out[:, :, 0]
    bias_grad = rows[:, :4].reshape(2, units)
    sums = rows[:, 4:].reshape(2, 2, width)
    counts = small_out[0, 0, 1].reshape(3, 128)[:2, :SYMBOLS]
    return (
        whole([feed[p]["outputs"] for p in parts])[None],
        input_grads[None],
        joint_out.transpose(0, 2, 1, 3)[None],
        output_out[None],
        up_out[None],
        bias_grad[None],
        down_out[None],
        sums[:, 0][None],
        sums[:, 1][None],
        counts.astype(jnp.int32),
    )


def solution(mesh):
    return jax.shard_map(
        shards,
        mesh=mesh,
        in_specs=(
            P("dp", "tensor"),
            P("dp", "tensor"),
            P("dp"),
            P("dp"),
            P("dp"),
            P("dp"),
            P("section", None, None, None, "tensor"),
            P("section", None, "tensor", None),
            P("section", None, None, "tensor"),
            P("section", None, "tensor"),
            P("section", None, "tensor", None),
            P("section", None, None),
            P("section", None, None),
        ),
        out_specs=(
            P("section", "dp", "tensor"),
            P("section", "dp", "tensor"),
            P("section", None, None, None, "tensor"),
            P("section", None, "tensor", None),
            P("section", None, None, "tensor"),
            P("section", None, "tensor"),
            P("section", None, "tensor", None),
            P("section", None, None),
            P("section", None, None),
            P(),
        ),
        check_vma=False,
    )
```

```python
import functools

import jax
import jax.numpy as jnp
from jax import lax
from jax.experimental import pallas as pl
from jax.experimental.pallas import tpu as pltpu
from jax.sharding import PartitionSpec as P

HEAD_DIM = 64
SYMBOLS = 24
SEQ = 160
PARTS = 3
RING = 8
BLOCK = 384
TAIL = 16
EPS = 1e-05
SCALE = HEAD_DIM**-0.5
VMEM_LIMIT = 10 * 1024 * 1024

root_half = 0.7071067811865476
root_two_pi = 0.3989422804014327
BF = jnp.bfloat16
F32 = jnp.float32


def swap(value):
    return lax.ppermute(value, "tensor", [(0, 1), (1, 0)])


def dot(a, b):
    return jnp.dot(a, b, preferred_element_type=F32)


def dot_rows(a, b):
    return lax.dot_general(a, b, (((1,), (1,)), ((), ())), preferred_element_type=F32)


def dot_cols(a, b):
    return lax.dot_general(a, b, (((0,), (0,)), ((), ())), preferred_element_type=F32)


def in_order(core, own, other):
    first = core == 0
    return jnp.concatenate(
        [jnp.where(first, own, other), jnp.where(first, other, own)], axis=1
    )


def own_part(core, value):
    half = value.shape[1] // 2
    return jnp.where(core == 0, value[:, :half], value[:, half:])


def normalise(rows):
    centred = rows - jnp.mean(rows, axis=-1, keepdims=True)
    inv_root = lax.rsqrt(jnp.mean(centred * centred, axis=-1, keepdims=True) + EPS)
    return centred * inv_root, inv_root


def norm_back(grads, normal, inv_root, gain):
    scaled = grads * gain
    inner = (
        scaled
        - jnp.mean(scaled, axis=-1, keepdims=True)
        - normal * jnp.mean(scaled * normal, axis=-1, keepdims=True)
    )
    return inner * inv_root


def pair_spans(width):
    return [slice(at, at + 2 * HEAD_DIM) for at in range(0, width, 2 * HEAD_DIM)]


def left_head():
    return lax.broadcasted_iota(jnp.int32, (1, 2 * HEAD_DIM), 1) < HEAD_DIM


def pair_scores(first, second):
    left = left_head().astype(BF)
    both = jnp.concatenate([first * left, first * (1 - left)], axis=0)
    return dot_rows(both, second).reshape(2, SEQ, SEQ)


def pair_product(matrices, block):
    found = dot(matrices.reshape(2 * SEQ, SEQ), block)
    return jnp.where(left_head(), found[:SEQ], found[SEQ:]).astype(BF)


def pair_turned(matrices):
    return jnp.concatenate([matrices[0].T, matrices[1].T], axis=0)


def attn_forward_kernel(choose, keep, start, count, chain, marks, *refs):
    refs = list(refs)
    own, other = refs.pop(0), refs.pop(0)
    if choose:
        own_late, other_late = refs.pop(0), refs.pop(0)
    joint, output = refs.pop(0), refs.pop(0)
    tag = marks[3 + start + chain]
    core = marks[1]
    a, b = own[...], other[...]
    if choose:
        early = marks[0] == 0
        a = jnp.where(early, a, own_late[...])
        b = jnp.where(early, b, other_late[...])
    rows = in_order(core, a, b)
    q, k, v = [dot(rows, joint[tag, j]).astype(BF) for j in range(3)]
    key_live = lax.broadcasted_iota(jnp.int32, (1, SEQ, 1), 1) < marks[3 + count + start + chain]
    spans = pair_spans(q.shape[1])
    scores = [pair_scores(k[:, s], q[:, s] * jnp.asarray(SCALE, BF)) for s in spans]
    probs = []
    for found in scores:
        found = jnp.where(key_live, found, -1000000000.0)
        shifted = jnp.exp(found - jnp.max(found, axis=1, keepdims=True))
        probs.append((shifted * (1.0 / jnp.sum(shifted, axis=1, keepdims=True))).astype(BF))
    mixed = jnp.concatenate(
        [pair_product(pair_turned(p), v[:, s]) for p, s in zip(probs, spans)], axis=1
    )
    refs[0][...] = rows
    refs[1][...] = dot(mixed, output[tag]).astype(BF)
    if keep:
        refs[2][...] = jnp.concatenate([q, k, v], axis=1)
        for at, found in enumerate(probs):
            refs[3][0, 2 * at : 2 * at + 2] = found
        refs[4][...] = mixed


def feed_forward_kernel(keep, start, chain, marks, rows, part, other, gains, shifts, up, bias, down, *outs):
    tag = marks[3 + start + chain]
    total = rows[...].astype(F32) + (part[...].astype(F32) + other[...].astype(F32))
    normal, inv_root = normalise(total)
    low = (normal * gains[0:1] + shifts[0:1]).astype(BF)
    pre = dot(low, up[tag]) + jnp.where(tag == 0, bias[0:1], bias[1:2]).astype(F32)
    cdf = 0.5 * (1.0 + lax.erf(pre * root_half))
    hidden = (pre * cdf).astype(BF)
    outs[0][...] = dot(hidden, down[tag]).astype(BF)
    outs[1][...] = normal
    if keep:
        outs[2][...] = inv_root
        outs[3][...] = low
        outs[4][...] = hidden
        outs[5][...] = (cdf + pre * jnp.exp(-0.5 * pre * pre) * root_two_pi).astype(BF)


def second_norm(normal, part, other, gains, shifts):
    first = normal[...] * gains[0:1] + shifts[0:1]
    return normalise(first + (part[...].astype(F32) + other[...].astype(F32)))


def last_norm_kernel(chain, marks, normal, part, other, gains, shifts, out):
    second, _ = second_norm(normal, part, other, gains, shifts)
    out[...] = own_part(marks[1], (second * gains[1:2] + shifts[1:2]).astype(BF))


def carry_over(chain, carried, sums):
    if chain == 0:
        sums[...] = carried[...]


def add_sums(chain, grads, normal, carried, sums):
    carry_over(chain, carried, sums)
    sums[0] += jnp.sum(grads * normal, axis=0, keepdims=True)
    sums[1] += jnp.sum(grads, axis=0, keepdims=True)


def feed_back_kernel(last, start, chain, marks, *refs):
    refs = list(refs)
    normal, part, other, gains, shifts, own_cot, other_cot = refs[:7]
    refs = refs[7:]
    tag = marks[3 + start + chain]
    core = marks[1]
    a, b = own_cot[...], other_cot[...]
    if last:
        late = marks[0] == 1
        a = jnp.where(late, a, refs.pop(0)[...])
        b = jnp.where(late, b, refs.pop(0)[...])
    slope, up, down = refs[:3]
    refs = refs[3:]
    if last:
        carried_sums, carried_bias = refs.pop(0), refs.pop(0)
    outs = refs
    grads = in_order(core, a, b).astype(F32)
    second, inv_root = second_norm(normal, part, other, gains, shifts)
    back = norm_back(grads, second, inv_root, gains[1:2])
    low = back.astype(BF)
    d_pre = (dot(low, down[tag]) * slope[...].astype(F32)).astype(BF)
    outs[0][...] = back
    outs[1][...] = dot(d_pre, up[tag]).astype(BF)
    if last:
        outs[2][...] = low
        outs[3][...] = d_pre
        outs[4][...] = own_part(core, (second * gains[1:2] + shifts[1:2]).astype(BF))
        add_sums(chain, grads, second, carried_sums, outs[5])
        carry_over(chain, carried_bias, outs[6])
        outs[6][tag] += jnp.sum(d_pre.astype(F32), axis=0, keepdims=True)


def attn_back_kernel(
    last, start, chain, marks, back, part, other, normal, inv_root, gains, joined, probs, joint, output, *outs
):
    if last:
        carried, *outs = outs
    tag = marks[3 + start + chain]
    core = marks[1]
    grads = back[...] + (part[...].astype(F32) + other[...].astype(F32))
    back_one = norm_back(grads, normal[...], inv_root[...], gains[0:1])
    low = back_one.astype(BF)
    d_mixed = dot(low, output[tag]).astype(BF)
    width = d_mixed.shape[1]
    q, k, v = [joined[:, j * width : (j + 1) * width] for j in range(3)]
    spans = pair_spans(width)
    d_probs = [pair_scores(v[:, s], d_mixed[:, s]) for s in spans]
    held = [probs[0, 2 * at : 2 * at + 2] for at in range(len(spans))]
    d_scores = []
    for found, kept in zip(d_probs, held):
        wide = kept.astype(F32)
        inner = jnp.sum(wide * found, axis=1, keepdims=True)
        d_scores.append((wide * (found - inner)).astype(BF))
    scale = jnp.asarray(SCALE, BF)
    d_k = [pair_product(d, q[:, s]) * scale for d, s in zip(d_scores, spans)]
    d_v = [pair_product(h, d_mixed[:, s]) for h, s in zip(held, spans)]
    d_q = [pair_product(pair_turned(d), k[:, s]) * scale for d, s in zip(d_scores, spans)]
    pieces = [d_q, d_k, d_v]
    blocks = [jnp.concatenate(p, axis=1) for p in pieces]
    d_rows = sum(dot(blocks[j], joint[tag, j]) for j in range(3)).astype(BF)
    outs[0][...] = own_part(core, back_one) + own_part(core, d_rows).astype(F32)
    outs[1][...] = own_part(1 - core, d_rows)
    if last:
        outs[2][...] = low
        outs[3][...] = jnp.concatenate(blocks, axis=1)
        add_sums(chain, grads, normal[...], carried, outs[4])


def behind(kernel, taken, ignored):
    def call(marks, *refs):
        kernel(marks, *refs[:taken], *refs[taken + ignored :])

    return call


ANY = pl.BlockSpec(memory_space=pl.ANY)
HBM = pl.BlockSpec(memory_space=pltpu.HBM)
TOKEN = jax.ShapeDtypeStruct((8, 128), F32)
TOKEN_BLOCK = pl.BlockSpec((8, 128), lambda *_: (0, 0))


def sign_off(token):
    token[...] = jnp.zeros_like(token)


class Order:
    def __init__(self):
        self.tokens = ()

    def run(self, call, *args):
        *results, token = call(*args, self.tokens)
        self.tokens = (token,)
        return results

    def wait(self, value):
        self.tokens = tuple(lax.optimization_barrier((*self.tokens, value))[:-1])

    def after(self, value):
        return lax.optimization_barrier((value, *self.tokens))[0]


VMEM = pl.BlockSpec(memory_space=pltpu.VMEM)
SMEM = pl.BlockSpec(memory_space=pltpu.SMEM)


def chain_view(ref, kind, at):
    if kind == "rows":
        return ref.at[at * SEQ : (at + 1) * SEQ]
    return ref.at[at : at + 1] if kind == "chain" else ref


def prepare_kernel(chains, count, places, *refs):
    sources, marks, held = refs[:count], refs[count], refs[count + 1 : 2 * count - 1]
    tags, live, sems = refs[2 * count - 1 :]
    copies = [
        pltpu.make_async_copy(source, target, sems.at[at])
        for at, (source, target) in enumerate(zip(sources, (tags, live) + held))
    ]
    for copy in copies:
        copy.start()
    for at in range(3):
        marks[at] = places[at]
    for copy in copies[:2]:
        copy.wait()
    token = lax.broadcasted_iota(jnp.int32, live.shape, 1)
    for chain in range(chains):
        marks[3 + chain] = jnp.where(tags[chain] > 0, 1, 0)
        inside = (token >= chain * SEQ) & (token < (chain + 1) * SEQ)
        marks[3 + chains + chain] = jnp.sum(jnp.where(inside, live[...], 0))
    for copy in copies[2:]:
        copy.wait()


def prepare(places, tags, live, arrays):
    chains = tags.shape[0]
    sources = [tags, live, *arrays]
    count = len(sources)
    return pl.pallas_call(
        functools.partial(prepare_kernel, chains, count),
        in_specs=[SMEM] + [HBM] * count,
        out_specs=[SMEM] + [VMEM] * len(arrays),
        out_shape=[jax.ShapeDtypeStruct((3 + 2 * chains,), jnp.int32)]
        + [jax.ShapeDtypeStruct(a.shape, a.dtype) for a in arrays],
        scratch_shapes=[
            pltpu.SMEM(tags.shape, jnp.int32),
            pltpu.VMEM(live.shape, jnp.int32),
            pltpu.SemaphoreType.DMA((count,)),
        ],
        compiler_params=pltpu.CompilerParams(vmem_limit_bytes=1024 * 1024),
        name="prepare",
    )(places, *[pltpu.with_memory_space_constraint(a, pltpu.HBM) for a in sources])


def turn_kernel(count, *refs):
    for source, target in zip(refs[:count], refs[-1 - count : -1]):
        for at in range(source.shape[0]):
            if len(source.shape) == 3:
                target[at] = source[at].T
            else:
                for each in range(source.shape[1]):
                    target[at, each] = source[at, each].T
    sign_off(refs[-1])


def turn(arrays, after):
    count = len(arrays)
    shapes = [a.shape[:-2] + (a.shape[-1], a.shape[-2]) for a in arrays]
    return pl.pallas_call(
        functools.partial(turn_kernel, count),
        in_specs=[VMEM] * count + [ANY] * len(after),
        out_specs=[VMEM] * (count + 1),
        out_shape=[jax.ShapeDtypeStruct(s, BF) for s in shapes] + [TOKEN],
        compiler_params=pltpu.CompilerParams(vmem_limit_bytes=VMEM_LIMIT),
        cost_estimate=pl.CostEstimate(flops=0, bytes_accessed=0, transcendentals=0),
        name="turn",
    )(*arrays, *after)


def run_chains(kernel, name, marks, chains, ins, outs, after):
    shapes = []
    for trailing, dtype, kind in outs:
        lead = {"rows": (chains * SEQ,), "chain": (chains,), "whole": ()}[kind]
        shapes.append(jax.ShapeDtypeStruct(lead + trailing, dtype))
    kinds = [(kind, first) for _, kind, first in ins] + [(kind, 0) for _, _, kind in outs]

    def call(marks, *refs):
        *refs, token = refs[: len(ins)] + refs[len(ins) + len(after) :]
        sign_off(token)
        for chain in range(chains):
            views = [chain_view(r, kind, first + chain) for r, (kind, first) in zip(refs, kinds)]
            kernel(chain, marks, *views)

    return pl.pallas_call(
        call,
        in_specs=[SMEM] + [VMEM] * len(ins) + [ANY] * len(after),
        out_specs=[VMEM] * (len(outs) + 1),
        out_shape=shapes + [TOKEN],
        compiler_params=pltpu.CompilerParams(vmem_limit_bytes=VMEM_LIMIT),
        cost_estimate=pl.CostEstimate(flops=10**10, bytes_accessed=10**7, transcendentals=0),
        name=name,
    )(marks, *[a for a, _, _ in ins], *after)


def ring_spot(marks, step, way):
    return lax.rem(marks[2] + 2 * RING + way * step, RING)


def span(at):
    return pl.ds(pl.multiple_of(at * BLOCK, BLOCK), BLOCK)


def cut(ref, at):
    return ref[:, span(at)]


def set_rows(marks, block, which):
    pieces = []
    for chain in range(block.shape[0] // SEQ):
        piece = block[chain * SEQ : (chain + 1) * SEQ]
        pieces.append(jnp.where(marks[3 + chain] == which, piece, jnp.zeros_like(piece)))
    return jnp.concatenate(pieces, axis=0)


def all_rows(refs, at):
    return jnp.concatenate([cut(ref, at) for ref in refs], axis=0)


def feed_shard(marks, which, hidden, d_down, low, d_pre):
    return (
        dot_cols(set_rows(marks, hidden, which), d_down).astype(BF),
        dot_cols(set_rows(marks, low, which), d_pre).astype(BF),
    )


def feed_weights_kernel(step, parts, marks, *refs):
    hidden, d_down, low, d_pre = [refs[n * parts : (n + 1) * parts] for n in range(4)]
    out, token = refs[4 * parts :]
    sign_off(token)
    for which, way in ((0, -1), (1, 1)):
        spot = ring_spot(marks, step, way)
        far, near = lax.div(spot, 2), lax.rem(spot, 2)
        out[which, :BLOCK], out[which, BLOCK:] = feed_shard(
            marks,
            which,
            all_rows(hidden, far),
            all_rows(d_down, near),
            all_rows(low, near),
            all_rows(d_pre, far),
        )


def two_halves(value):
    high = value.astype(BF).astype(F32)
    return jnp.concatenate([high, value - high], axis=0).astype(BF)


def one_whole(rows):
    rows = rows.astype(F32)
    return rows[: TAIL // 2] + rows[TAIL // 2 :]


def count_rows(live, predicted, targets):
    symbols = lax.broadcasted_iota(jnp.int32, (128, live.shape[1]), 0)
    hits = (targets[...] == symbols) & (live[...] > 0)
    right = hits & (predicted[...] == targets[...])
    ones = jnp.ones((8, live.shape[1]), BF)
    found = [dot_rows(ones, h.astype(F32).astype(BF)) for h in (hits, right)]
    return jnp.concatenate(found + [jnp.zeros_like(found[0])], axis=1)[0:1]


def attn_weights_kernel(step, parts, marks, *refs):
    rows, d_joined, mixed, d_attn = [refs[n * parts : (n + 1) * parts] for n in range(4)]
    bias, *sums, live, predicted, targets, out, token = refs[4 * parts :]
    sign_off(token)
    for which, way in ((0, -1), (1, 1)):
        spot = ring_spot(marks, step, way)
        far, near = lax.div(spot, 2), lax.rem(spot, 2)

        @pl.when(far < 3)
        def _():
            out[which, :BLOCK] = dot_cols(
                set_rows(marks, all_rows(rows, near), which), all_rows(d_joined, far)
            ).astype(BF)

        @pl.when(far == 3)
        def _():
            out[which, :BLOCK] = dot_cols(
                set_rows(marks, all_rows(mixed, 0), which), all_rows(d_attn, near)
            ).astype(BF)

        early = far < 2
        small = jnp.where(
            early,
            bias[which, :, span(jnp.where(early, spot, 0))],
            sums[which][jnp.where(early, 0, far - 2), :, span(near)],
        )
        place = lax.broadcasted_iota(jnp.int32, (TAIL // 2, BLOCK), 0)
        small = jnp.where(place == 0, small, 0.0)
        out[which, BLOCK:] = two_halves(small)
        if which == 0:

            @pl.when(spot == 0)
            def _():
                counts = count_rows(live, predicted, targets)
                out[which, BLOCK:] = two_halves(jnp.where(place == 1, counts, small))


def run_weights(kernel, name, marks, step, lists, rest, rows_out, after):
    ins = [a for arrays in lists for a in arrays] + list(rest)
    return pl.pallas_call(
        behind(functools.partial(kernel, step + 1, len(lists[0])), len(ins), len(after)),
        in_specs=[SMEM] + [VMEM] * len(ins) + [ANY] * len(after),
        out_specs=[VMEM, VMEM],
        out_shape=[jax.ShapeDtypeStruct((2, rows_out, BLOCK), BF), TOKEN],
        compiler_params=pltpu.CompilerParams(vmem_limit_bytes=VMEM_LIMIT),
        cost_estimate=pl.CostEstimate(flops=3*10**9, bytes_accessed=10**6, transcendentals=0),
        name=name,
    )(marks, *ins, *after)


def add_kernel(tail, ahead, back, local, out_ahead, out_back, token):
    sign_off(token)
    for which, (ref, out) in enumerate(((ahead, out_ahead), (back, out_back))):
        total = ref[...].astype(F32) + local[which].astype(F32)
        out[...] = total.astype(BF)
        if tail:
            out[tail:] = two_halves(one_whole(total[tail:]))


def add_step(pair, local, after):
    shape = local.shape[1:]
    tail = BLOCK if shape[0] == BLOCK + TAIL else 0

    def call(*refs):
        add_kernel(tail, *refs[:3], *refs[3 + len(after) :])

    return pl.pallas_call(
        call,
        in_specs=[VMEM] * 3 + [ANY] * len(after),
        out_specs=[VMEM] * 3,
        out_shape=[jax.ShapeDtypeStruct(shape, BF)] * 2 + [TOKEN],
        compiler_params=pltpu.CompilerParams(vmem_limit_bytes=VMEM_LIMIT),
        cost_estimate=pl.CostEstimate(flops=3*10**9, bytes_accessed=10**6, transcendentals=0),
        name="ring_add",
    )(*pair, local, *after)


def feed_place_kernel(step, marks, ahead, back, outs, wide, sems):
    down, up = outs
    copies = []
    for which, (ref, way) in enumerate(((ahead, -1), (back, 1))):
        spot = ring_spot(marks, step, way)
        far, near = lax.div(spot, 2), lax.rem(spot, 2)
        wide[which] = ref[...].astype(F32)
        copies += [
            pltpu.make_async_copy(
                wide.at[which, :BLOCK], down.at[which, span(far), span(near)], sems.at[2 * which]
            ),
            pltpu.make_async_copy(
                wide.at[which, BLOCK:], up.at[which, span(near), span(far)], sems.at[2 * which + 1]
            ),
        ]
        for copy in copies[-2:]:
            copy.start()
    for copy in copies:
        copy.wait()


def attn_place_kernel(step, marks, ahead, back, outs, wide, sems):
    joint, output, small = outs
    copies = []
    for which, (ref, way) in enumerate(((ahead, -1), (back, 1))):
        spot = ring_spot(marks, step, way)
        far, near = lax.div(spot, 2), lax.rem(spot, 2)
        wide[which] = ref[...].astype(F32)
        wide[which, BLOCK : BLOCK + TAIL // 2] = one_whole(ref[BLOCK:])
        copy = pltpu.make_async_copy(
            wide.at[which, BLOCK : BLOCK + TAIL // 2], small.at[which, spot], sems.at[2 + which]
        )
        copy.start()
        copies.append(copy)

        @pl.when(far < 3)
        def _():
            copy = pltpu.make_async_copy(
                wide.at[which, :BLOCK], joint.at[which, far, span(near)], sems.at[which]
            )
            copy.start()
            copy.wait()

        @pl.when(far == 3)
        def _():
            copy = pltpu.make_async_copy(
                wide.at[which, :BLOCK], output.at[which, :, span(near)], sems.at[which]
            )
            copy.start()
            copy.wait()

    for copy in copies:
        copy.wait()


def place_step(kernel, name, marks, step, pair, held, after):
    shape = pair[0].shape
    block = pl.BlockSpec(shape, lambda i, *_: (0, 0))

    count = len(held)

    def call(marks, ahead, back, *refs):
        refs = refs[count + len(after) :]
        sign_off(refs[count])
        kernel(step, marks, ahead, back, refs[:count], *refs[count + 1 :])

    return pl.pallas_call(
        call,
        grid_spec=pltpu.PrefetchScalarGridSpec(
            num_scalar_prefetch=1,
            grid=(1,),
            in_specs=[block, block] + [HBM] * count + [ANY] * len(after),
            out_specs=[HBM] * count + [TOKEN_BLOCK],
            scratch_shapes=[pltpu.VMEM((2,) + shape, F32), pltpu.SemaphoreType.DMA((4,))],
        ),
        out_shape=[jax.ShapeDtypeStruct(h.shape, h.dtype) for h in held] + [TOKEN],
        input_output_aliases={3 + i: i for i in range(count)},
        compiler_params=pltpu.CompilerParams(vmem_limit_bytes=VMEM_LIMIT),
        cost_estimate=pl.CostEstimate(
            flops=3*10**9, bytes_accessed=10**6, transcendentals=0
        ),
        name=name,
    )(marks, *pair, *held, *after)


def unwritten(*shapes):
    return pl.pallas_call(
        lambda *refs: None,
        out_specs=[HBM] * len(shapes),
        out_shape=[jax.ShapeDtypeStruct(s, F32) for s in shapes],
        compiler_params=pltpu.CompilerParams(vmem_limit_bytes=1024 * 1024),
        name="unwritten",
    )()


class Ring:
    def __init__(self):
        self.count = lax.axis_size("dp")
        assert self.count % RING == 0
        order = list(range(0, RING, 2)) + list(range(1, RING, 2))[::-1]
        rank = lax.rem(lax.axis_index("dp"), RING)
        self.place = jnp.zeros((), jnp.int32)
        for at, member in enumerate(order):
            self.place = jnp.where(rank == member, at, self.place)
        self.ahead = [
            (base + order[i], base + order[(i + 1) % RING])
            for base in range(0, self.count, RING)
            for i in range(RING)
        ]
        self.back = [(b, a) for a, b in self.ahead]

    def send(self, pair):
        return lax.ppermute(pair[0], "dp", self.ahead), lax.ppermute(pair[1], "dp", self.back)

    def across(self, pair):
        result = []
        for value in pair:
            total = value.astype(F32)
            moving = value
            for _ in range(self.count // RING - 1):
                pairs = [(i, (i + RING) % self.count) for i in range(self.count)]
                moving = lax.ppermute(moving, "dp", pairs)
                total = total + moving.astype(F32)
            low = total.astype(BF)
            if total.shape[0] == BLOCK + TAIL and self.count > RING:
                tail = two_halves(one_whole(total[BLOCK:]))
                low = jnp.concatenate([low[:BLOCK], tail], axis=0)
            result.append(low)
        return result


def part_sizes(chains):
    sizes = [(chains + PARTS - 1 - p) // PARTS for p in range(PARTS)]
    return sizes, [sum(sizes[:p]) for p in range(PARTS)]


def shards(
    chain_inputs,
    cotangent,
    chain_tags,
    pad_mask,
    predicted,
    target_ids,
    joint_proj,
    output_proj,
    up_proj,
    up_bias,
    down_proj,
    norm_gain,
    norm_shift,
):
    section = lax.axis_index("section")
    core = lax.axis_index("tensor")
    tokens, half = chain_inputs.shape
    width = 2 * half
    all_chains = tokens // SEQ
    sizes, starts = part_sizes(all_chains)
    parts = range(len(sizes))
    ring = Ring()
    small = [ids.reshape(1, tokens) for ids in (pad_mask, predicted, target_ids)]
    joint = joint_proj[0].transpose(0, 2, 1, 3)
    output, up, bias, down = output_proj[0], up_proj[0], up_bias[0], down_proj[0]
    places = jnp.stack([section, core, ring.place]).astype(jnp.int32)
    marks, joint, output, own_rows = prepare(
        places, chain_tags, small[0], [joint, output, chain_inputs]
    )
    gains, shifts = norm_gain[0], norm_shift[0]
    units = up.shape[2]
    local = output.shape[1]
    heads = local // HEAD_DIM
    cot_other = swap(cotangent)
    rows_other = swap(chain_inputs)

    order = Order()

    def attn_forward(p, late, keep):
        start = starts[p]
        ins = [(own_rows, "rows", start), (rows_other, "rows", start)]
        if late is not None:
            ins += [(late[0], "rows", 0), (late[1], "rows", 0)]
        ins += [(joint, "whole", 0), (output, "whole", 0)]
        outs = [((width,), BF, "rows"), ((width,), BF, "rows")]
        if keep:
            outs += [
                ((3 * local,), BF, "rows"),
                ((heads, SEQ, SEQ), BF, "chain"),
                ((local,), BF, "rows"),
            ]
        kernel = functools.partial(
            attn_forward_kernel, late is not None, keep, start, all_chains
        )
        found = order.run(
            run_chains, kernel, "attn_forward", marks, sizes[p], ins, outs
        )
        names = ("rows", "part", "joined", "probs", "mixed")
        kept = dict(zip(names, found))
        kept["part_other"] = swap(kept["part"])
        return kept

    def feed_forward(p, kept, keep):
        ins = [(kept[n], "rows", 0) for n in ("rows", "part", "part_other")]
        ins += [(a, "whole", 0) for a in (gains, shifts, up, bias, down)]
        outs = [((width,), BF, "rows"), ((width,), F32, "rows")]
        if keep:
            outs += [
                ((1,), F32, "rows"),
                ((width,), BF, "rows"),
                ((units,), BF, "rows"),
                ((units,), BF, "rows"),
            ]
        kernel = functools.partial(feed_forward_kernel, keep, starts[p])
        found = order.run(
            run_chains, kernel, "feed_forward", marks, sizes[p], ins, outs
        )
        names = ("down", "normal", "inv_root", "low", "hidden", "slope")
        kept.update(zip(names, found))
        kept["down_other"] = swap(kept["down"])

    def last_norm(p, kept):
        ins = [(kept[n], "rows", 0) for n in ("normal", "down", "down_other")]
        ins += [(gains, "whole", 0), (shifts, "whole", 0)]
        outs = [((half,), BF, "rows")]
        found = order.run(
            run_chains, last_norm_kernel, "last_norm", marks, sizes[p], ins, outs
        )
        return lax.ppermute(found[0], "section", [(0, 1), (1, 0)])

    def feed_back(p, kept, late, carried=None):
        ins = [(kept[n], "rows", 0) for n in ("normal", "down", "down_other")]
        ins += [(gains, "whole", 0), (shifts, "whole", 0)]
        ins += [(cotangent, "rows", starts[p]), (cot_other, "rows", starts[p])]
        if late is not None:
            ins += [(late[0], "rows", 0), (late[1], "rows", 0)]
        ins += [(kept["slope"], "rows", 0), (turned["up"], "whole", 0), (turned["down"], "whole", 0)]
        if late is not None:
            ins += [(carried["sums"], "whole", 0), (carried["bias"], "whole", 0)]
        outs = [((width,), F32, "rows"), ((width,), BF, "rows")]
        if late is not None:
            outs += [
                ((width,), BF, "rows"),
                ((units,), BF, "rows"),
                ((half,), BF, "rows"),
                ((2, 1, width), F32, "whole"),
                ((2, 1, units), F32, "whole"),
            ]
        kernel = functools.partial(feed_back_kernel, late is not None, starts[p])
        found = order.run(
            run_chains, kernel, "feed_back", marks, sizes[p], ins, outs
        )
        names = ("back", "part", "d_down", "d_pre", "outputs", "sums", "bias")
        found = dict(zip(names, found))
        found["part_other"] = swap(found["part"])
        return found

    def attn_back(p, kept, feed, last, carried=None):
        ins = [(feed[n], "rows", 0) for n in ("back", "part", "part_other")]
        ins += [(kept["normal"], "rows", 0), (kept["inv_root"], "rows", 0), (gains, "whole", 0)]
        ins += [(kept["joined"], "rows", 0), (kept["probs"], "chain", 0)]
        ins += [(turned["joint"], "whole", 0), (turned["output"], "whole", 0)]
        if last:
            ins.append((carried["sums"], "whole", 0))
        outs = [((half,), F32, "rows"), ((half,), BF, "rows")]
        if last:
            outs += [
                ((width,), BF, "rows"),
                ((3 * local,), BF, "rows"),
                ((2, 1, width), F32, "whole"),
            ]
        kernel = functools.partial(attn_back_kernel, last, starts[p])
        found = order.run(
            run_chains, kernel, "attn_back", marks, sizes[p], ins, outs
        )
        names = ("mine", "theirs", "d_attn", "d_joined", "sums")
        found = dict(zip(names, found))
        found["grads"] = found["mine"] + swap(found["theirs"]).astype(F32)
        return found

    early, sent, late, kept = {}, {}, {}, {}

    def start_early(p):
        early[p] = attn_forward(p, None, False)

    def feed_early(p):
        feed_forward(p, early[p], False)

    def norm_early(p):
        sent[p] = last_norm(p, early[p])

    def arrived(p):
        order.wait(sent[p])

    def receive(p):
        moved = order.after(sent[p])
        late[p] = (moved, swap(moved))

    def start_kept(p):
        kept[p] = attn_forward(p, late[p], True)

    def feed_kept(p):
        feed_forward(p, kept[p], True)

    first_feed, first_attn, sent_back, late_back = {}, {}, {}, {}
    no_sums = jnp.zeros((2, 1, width), F32)
    feed = {-1: dict(sums=no_sums, bias=jnp.zeros((2, 1, units), F32))}
    attn = {-1: dict(sums=no_sums)}

    turned = {}

    def turn_feed(p):
        turned["up"], turned["down"] = order.run(turn, [up, down])

    def turn_attn(p):
        turned["joint"], turned["output"] = order.run(turn, [joint, output])

    def feed_first(p):
        first_feed[p] = feed_back(p, kept[p], None)

    def attn_first(p):
        first_attn[p] = attn_back(p, kept[p], first_feed[p], False)
        total = first_attn[p]["grads"].astype(BF)
        sent_back[p] = lax.ppermute(total, "section", [(1, 0), (0, 1)])

    def receive_back(p):
        moved = order.after(sent_back[p])
        late_back[p] = (moved, swap(moved))

    def feed_last(p):
        feed[p] = feed_back(p, kept[p], late_back[p], feed[p - 1])

    def attn_last(p):
        attn[p] = attn_back(p, kept[p], feed[p], True, attn[p - 1])

    for step, p in (
        (start_early, 0),
        (start_early, 1),
        (feed_early, 0),
        (norm_early, 0),
        (start_early, 2),
        (feed_early, 1),
        (feed_early, 2),
        (receive, 0),
        (norm_early, 1),
        (start_kept, 0),
        (norm_early, 2),
        (feed_kept, 0),
        (receive, 1),
        (turn_feed, 0),
        (start_kept, 1),
        (receive, 2),
        (turn_attn, 0),
        (start_kept, 2),
        (feed_kept, 1),
        (feed_kept, 2),
        (feed_first, 0),
        (feed_first, 1),
        (attn_first, 0),
        (attn_first, 1),
        (feed_first, 2),
        (attn_first, 2),
        (receive_back, 0),
        (feed_last, 0),
        (receive_back, 1),
        (feed_last, 1),
        (receive_back, 2),
        (feed_last, 2),
    ):
        step(p)
    feed_lists = [
        [kept[p]["hidden"] for p in parts],
        [feed[p]["d_down"] for p in parts],
        [kept[p]["low"] for p in parts],
        [feed[p]["d_pre"] for p in parts],
    ]

    def feed_weights(step):
        return order.run(
            run_weights, feed_weights_kernel, "feed_weights", marks, step, feed_lists, [], 2 * BLOCK
        )[0]

    def add_local(pair, local):
        return order.run(add_step, pair, local)

    shard = feed_weights(0)
    feed_pair = ring.send((shard[0], shard[1]))
    shard = feed_weights(1)
    for p in parts:
        attn_last(p)
    feed_pair = ring.send(add_local(feed_pair, shard))
    attn_lists = [
        [kept[p]["rows"] for p in parts],
        [attn[p]["d_joined"] for p in parts],
        [kept[p]["mixed"] for p in parts],
        [attn[p]["d_attn"] for p in parts],
    ]

    small = [feed[parts[-1]]["bias"], attn[parts[-1]]["sums"], feed[parts[-1]]["sums"], *small]

    def attn_weights(step):
        return order.run(
            run_weights,
            attn_weights_kernel,
            "attn_weights",
            marks,
            step,
            attn_lists,
            small,
            BLOCK + TAIL,
        )[0]

    feed_local = feed_weights(2)
    shard = attn_weights(0)
    attn_pair = ring.send((shard[0], shard[1]))
    attn_local = attn_weights(1)
    streams = [
        dict(
            pair=attn_pair,
            local=attn_local,
            weights=attn_weights,
            sent=1,
            kernel=attn_place_kernel,
            name="attn_place",
            held=unwritten((2, 3, width, local), (2, local, width), (2, RING, 8, BLOCK)),
        ),
        dict(
            pair=feed_pair,
            local=feed_local,
            weights=feed_weights,
            sent=2,
            kernel=feed_place_kernel,
            name="feed_place",
            held=unwritten((2, units, width), (2, width, units)),
        ),
    ]

    def advance(stream):
        sent = stream["sent"]
        *pair, token = lax.optimization_barrier((*stream["pair"], *order.tokens))
        order.tokens = (token,)
        if sent < RING:
            pair = add_local(pair, stream["local"])
            if sent == RING - 1:
                pair = ring.across(pair)
        stream["pair"] = ring.send(pair) if sent < 2 * RING - 2 else None
        if sent < RING - 1:
            stream["local"] = stream["weights"](sent + 1)
        else:
            stream["held"] = order.run(
                place_step,
                stream["kernel"],
                stream["name"],
                marks,
                sent - RING + 1,
                pair,
                stream["held"],
            )
        stream["sent"] += 1

    attn_stream, feed_stream = streams
    while attn_stream["pair"] is not None or feed_stream["pair"] is not None:
        if feed_stream["pair"] is not None:
            advance(feed_stream)
        if attn_stream["pair"] is not None:
            advance(attn_stream)
    joint_out, output_out, small_out = attn_stream["held"]
    down_out, up_out = feed_stream["held"]

    def whole(pieces):
        return jnp.concatenate(pieces, axis=0)

    input_grads = whole([attn[p]["grads"] for p in parts])
    rows = small_out[:, :, 0]
    bias_grad = rows[:, :4].reshape(2, units)
    sums = rows[:, 4:].reshape(2, 2, width)
    counts = small_out[0, 0, 1].reshape(3, 128)[:2, :SYMBOLS]
    return (
        whole([feed[p]["outputs"] for p in parts])[None],
        input_grads[None],
        joint_out.transpose(0, 2, 1, 3)[None],
        output_out[None],
        up_out[None],
        bias_grad[None],
        down_out[None],
        sums[:, 0][None],
        sums[:, 1][None],
        counts.astype(jnp.int32),
    )


def solution(mesh):
    return jax.shard_map(
        shards,
        mesh=mesh,
        in_specs=(
            P("dp", "tensor"),
            P("dp", "tensor"),
            P("dp"),
            P("dp"),
            P("dp"),
            P("dp"),
            P("section", None, None, None, "tensor"),
            P("section", None, "tensor", None),
            P("section", None, None, "tensor"),
            P("section", None, "tensor"),
            P("section", None, "tensor", None),
            P("section", None, None),
            P("section", None, None),
        ),
        out_specs=(
            P("section", "dp", "tensor"),
            P("section", "dp", "tensor"),
            P("section", None, None, None, "tensor"),
            P("section", None, "tensor", None),
            P("section", None, None, "tensor"),
            P("section", None, "tensor"),
            P("section", None, "tensor", None),
            P("section", None, None),
            P("section", None, None),
            P(),
        ),
        check_vma=False,
    )
```

```python
import functools

import jax
import jax.numpy as jnp
from jax import lax
from jax.experimental import pallas as pl
from jax.experimental.pallas import tpu as pltpu
from jax.sharding import PartitionSpec as P

HEAD_DIM = 64
SYMBOLS = 24
SEQ = 160
PARTS = (2, 2, 2)
RING = 8
BLOCK = 384
TAIL = 16
EPS = 1e-05
SCALE = HEAD_DIM**-0.5
VMEM_LIMIT = 7 * 1024 * 1024

root_half = 0.7071067811865476
root_two_pi = 0.3989422804014327
BF = jnp.bfloat16
F32 = jnp.float32


def swap(value):
    return lax.ppermute(value, "tensor", [(0, 1), (1, 0)])


def dot(a, b):
    return jnp.dot(a, b, preferred_element_type=F32)


def dot_rows(a, b):
    return lax.dot_general(a, b, (((1,), (1,)), ((), ())), preferred_element_type=F32)


def dot_cols(a, b):
    return lax.dot_general(a, b, (((0,), (0,)), ((), ())), preferred_element_type=F32)


def in_order(core, own, other):
    first = core == 0
    return jnp.concatenate(
        [jnp.where(first, own, other), jnp.where(first, other, own)], axis=1
    )


def own_part(core, value):
    half = value.shape[1] // 2
    return jnp.where(core == 0, value[:, :half], value[:, half:])


def normalise(rows):
    centred = rows - jnp.mean(rows, axis=-1, keepdims=True)
    inv_root = lax.rsqrt(jnp.mean(centred * centred, axis=-1, keepdims=True) + EPS)
    return centred * inv_root, inv_root


def norm_back(grads, normal, inv_root, gain):
    scaled = grads * gain
    inner = (
        scaled
        - jnp.mean(scaled, axis=-1, keepdims=True)
        - normal * jnp.mean(scaled * normal, axis=-1, keepdims=True)
    )
    return inner * inv_root


def pair_spans(width):
    return [slice(at, at + 2 * HEAD_DIM) for at in range(0, width, 2 * HEAD_DIM)]


def left_head():
    return lax.broadcasted_iota(jnp.int32, (1, 2 * HEAD_DIM), 1) < HEAD_DIM


def pair_scores(first, second):
    left = left_head().astype(BF)
    both = jnp.concatenate([first * left, first * (1 - left)], axis=0)
    return dot_rows(both, second).reshape(2, SEQ, SEQ)


def pair_product(matrices, block):
    found = dot(matrices.reshape(2 * SEQ, SEQ), block)
    return jnp.where(left_head(), found[:SEQ], found[SEQ:]).astype(BF)


def pair_turned(matrices):
    return jnp.concatenate([matrices[0].T, matrices[1].T], axis=0)


def attn_forward_kernel(start, count, chain, marks, own, other, joint, output, *refs):
    tag = marks[3 + start + chain]
    core = marks[1]
    a, b = own[...], other[...]
    rows = in_order(core, a, b)
    q, k, v = [dot(rows, joint[tag, j]).astype(BF) for j in range(3)]
    key_live = lax.broadcasted_iota(jnp.int32, (1, SEQ, 1), 1) < marks[3 + count + start + chain]
    spans = pair_spans(q.shape[1])
    scores = [pair_scores(k[:, s], q[:, s] * jnp.asarray(SCALE, BF)) for s in spans]
    probs = []
    for found in scores:
        found = jnp.where(key_live, found, -1000000000.0)
        shifted = jnp.exp(found - jnp.max(found, axis=1, keepdims=True))
        probs.append((shifted * (1.0 / jnp.sum(shifted, axis=1, keepdims=True))).astype(BF))
    mixed = jnp.concatenate(
        [pair_product(pair_turned(p), v[:, s]) for p, s in zip(probs, spans)], axis=1
    )
    refs[0][...] = rows
    refs[1][...] = dot(mixed, output[tag]).astype(BF)
    refs[2][...] = jnp.concatenate([q, k, v], axis=1)
    for at, found in enumerate(probs):
        refs[3][0, 2 * at : 2 * at + 2] = found
    refs[4][...] = mixed


def feed_forward_kernel(start, chain, marks, rows, part, other, gains, shifts, up, bias, down, *outs):
    tag = marks[3 + start + chain]
    total = rows[...].astype(F32) + (part[...].astype(F32) + other[...].astype(F32))
    normal, inv_root = normalise(total)
    low = (normal * gains[0:1] + shifts[0:1]).astype(BF)
    pre = dot(low, up[tag]) + jnp.where(tag == 0, bias[0:1], bias[1:2]).astype(F32)
    cdf = 0.5 * (1.0 + lax.erf(pre * root_half))
    hidden = (pre * cdf).astype(BF)
    outs[0][...] = dot(hidden, down[tag]).astype(BF)
    outs[1][...] = normal
    outs[2][...] = inv_root
    outs[3][...] = low
    outs[4][...] = hidden
    outs[5][...] = (cdf + pre * jnp.exp(-0.5 * pre * pre) * root_two_pi).astype(BF)


def second_norm(normal, part, other, gains, shifts):
    first = normal[...] * gains[0:1] + shifts[0:1]
    return normalise(first + (part[...].astype(F32) + other[...].astype(F32)))


def last_norm_kernel(chain, marks, normal, part, other, gains, shifts, out):
    second, _ = second_norm(normal, part, other, gains, shifts)
    out[...] = own_part(marks[1], (second * gains[1:2] + shifts[1:2]).astype(BF))


def add_sums(grads, normal, sums):
    sums[0] += jnp.sum(grads * normal, axis=0, keepdims=True)
    sums[1] += jnp.sum(grads, axis=0, keepdims=True)


def feed_back_kernel(
    start, chain, marks, normal, part, other, gains, shifts, own, partner, slope, up, down, *outs
):
    tag = marks[3 + start + chain]
    core = marks[1]
    a, b = own[...], partner[...]
    grads = in_order(core, a, b).astype(F32)
    second, inv_root = second_norm(normal, part, other, gains, shifts)
    back = norm_back(grads, second, inv_root, gains[1:2])
    low = back.astype(BF)
    d_pre = (dot(low, down[tag]) * slope[...].astype(F32)).astype(BF)
    outs[0][...] = back
    outs[1][...] = dot(d_pre, up[tag]).astype(BF)
    outs[2][...] = low
    outs[3][...] = d_pre
    outs[4][...] = own_part(core, (second * gains[1:2] + shifts[1:2]).astype(BF))
    add_sums(grads, second, outs[5])
    outs[6][tag] += jnp.sum(d_pre.astype(F32), axis=0, keepdims=True)


def attn_back_kernel(
    start, chain, marks, back, part, other, normal, inv_root, gains, joined, probs, joint, output, *outs
):
    tag = marks[3 + start + chain]
    core = marks[1]
    grads = back[...] + (part[...].astype(F32) + other[...].astype(F32))
    back_one = norm_back(grads, normal[...], inv_root[...], gains[0:1])
    low = back_one.astype(BF)
    d_mixed = dot_rows(low, output[tag]).astype(BF)
    width = d_mixed.shape[1]
    q, k, v = [joined[:, j * width : (j + 1) * width] for j in range(3)]
    spans = pair_spans(width)
    d_probs = [pair_scores(v[:, s], d_mixed[:, s]) for s in spans]
    held = [probs[0, 2 * at : 2 * at + 2] for at in range(len(spans))]
    d_scores = []
    for found, kept in zip(d_probs, held):
        wide = kept.astype(F32)
        inner = jnp.sum(wide * found, axis=1, keepdims=True)
        d_scores.append((wide * (found - inner)).astype(BF))
    scale = jnp.asarray(SCALE, BF)
    d_k = [pair_product(d, q[:, s]) * scale for d, s in zip(d_scores, spans)]
    d_v = [pair_product(h, d_mixed[:, s]) for h, s in zip(held, spans)]
    d_q = [pair_product(pair_turned(d), k[:, s]) * scale for d, s in zip(d_scores, spans)]
    pieces = [d_q, d_k, d_v]
    blocks = [jnp.concatenate(p, axis=1) for p in pieces]
    d_rows = sum(dot_rows(blocks[j], joint[tag, j]) for j in range(3)).astype(BF)
    outs[0][...] = own_part(core, back_one) + own_part(core, d_rows).astype(F32)
    outs[1][...] = own_part(1 - core, d_rows)
    outs[2][...] = low
    outs[3][...] = jnp.concatenate(blocks, axis=1)
    add_sums(grads, normal[...], outs[4])


def behind(kernel, taken, ignored):
    def call(marks, *refs):
        kernel(marks, *refs[:taken], *refs[taken + ignored :])

    return call


ANY = pl.BlockSpec(memory_space=pl.ANY)
HBM = pl.BlockSpec(memory_space=pltpu.HBM)
TOKEN = jax.ShapeDtypeStruct((8, 128), F32)
TOKEN_BLOCK = pl.BlockSpec((8, 128), lambda *_: (0, 0))


def sign_off(token):
    token[...] = jnp.zeros_like(token)


class Order:
    def __init__(self):
        self.tokens = ()

    def run(self, call, *args):
        *results, token = call(*args, self.tokens)
        self.tokens = (token,)
        return results

    def wait(self, value):
        self.tokens = tuple(lax.optimization_barrier((*self.tokens, value))[:-1])

    def after(self, value):
        return lax.optimization_barrier((value, *self.tokens))[0]


VMEM = pl.BlockSpec(memory_space=pltpu.VMEM)
SMEM = pl.BlockSpec(memory_space=pltpu.SMEM)


def chain_view(ref, kind, at):
    if kind == "rows":
        return ref.at[at * SEQ : (at + 1) * SEQ]
    return ref.at[at : at + 1] if kind == "chain" else ref


def prepare_kernel(chains, count, places, *refs):
    sources, marks, held = refs[:count], refs[count], refs[count + 1 : 2 * count - 1]
    tags, live, sems = refs[2 * count - 1 :]
    copies = [
        pltpu.make_async_copy(source, target, sems.at[at])
        for at, (source, target) in enumerate(zip(sources, (tags, live) + held))
    ]
    for copy in copies:
        copy.start()
    for at in range(3):
        marks[at] = places[at]
    for copy in copies[:2]:
        copy.wait()
    token = lax.broadcasted_iota(jnp.int32, live.shape, 1)
    for chain in range(chains):
        marks[3 + chain] = jnp.where(tags[chain] > 0, 1, 0)
        inside = (token >= chain * SEQ) & (token < (chain + 1) * SEQ)
        marks[3 + chains + chain] = jnp.sum(jnp.where(inside, live[...], 0))
    for copy in copies[2:]:
        copy.wait()


def prepare(places, tags, live, arrays):
    chains = tags.shape[0]
    sources = [tags, live, *arrays]
    count = len(sources)
    return pl.pallas_call(
        functools.partial(prepare_kernel, chains, count),
        in_specs=[SMEM] + [HBM] * count,
        out_specs=[SMEM] + [VMEM] * len(arrays),
        out_shape=[jax.ShapeDtypeStruct((3 + 2 * chains,), jnp.int32)]
        + [jax.ShapeDtypeStruct(a.shape, a.dtype) for a in arrays],
        scratch_shapes=[
            pltpu.SMEM(tags.shape, jnp.int32),
            pltpu.VMEM(live.shape, jnp.int32),
            pltpu.SemaphoreType.DMA((count,)),
        ],
        compiler_params=pltpu.CompilerParams(vmem_limit_bytes=1024 * 1024),
        name="prepare",
    )(places, *[pltpu.with_memory_space_constraint(a, pltpu.HBM) for a in sources])


def turn(active, marks, arrays, held, after):
    count = len(arrays)
    skipped = count + len(held) + len(after)

    def call(marks, *refs):
        sign_off(refs[-1])

        @pl.when(marks[0] == active)
        def _():
            for source, target in zip(refs[:count], refs[skipped:]):
                for at in range(source.shape[0]):
                    target[at] = source[at].T

    return pl.pallas_call(
        call,
        in_specs=[SMEM] + [VMEM] * (count + len(held)) + [ANY] * len(after),
        out_specs=[VMEM] * (count + 1),
        out_shape=[jax.ShapeDtypeStruct((a.shape[0], a.shape[2], a.shape[1]), BF) for a in arrays]
        + [TOKEN],
        input_output_aliases={1 + count + at: at for at in range(len(held))},
        compiler_params=pltpu.CompilerParams(vmem_limit_bytes=VMEM_LIMIT),
        cost_estimate=pl.CostEstimate(flops=10**10, bytes_accessed=10**7, transcendentals=0),
        name="turn",
    )(marks, *arrays, *held, *after)


def run_chains(kernel, name, active, marks, chains, ins, outs, after):
    shapes, held, aliases = [], [], {}
    for trailing, dtype, kind, array in outs:
        lead = {"rows": (chains * SEQ,), "chain": (chains,), "whole": ()}[kind]
        if array is not None:
            aliases[1 + len(ins) + len(held)] = len(shapes)
            held.append(array)
        shapes.append(jax.ShapeDtypeStruct(lead + trailing, dtype))
    kinds = [(kind, first) for _, kind, first in ins] + [(kind, 0) for _, _, kind, _ in outs]
    skipped = len(ins) + len(held) + len(after)

    def call(marks, *refs):
        *refs, token = refs[: len(ins)] + refs[skipped:]
        sign_off(token)

        @pl.when(marks[0] == active)
        def _():
            for chain in range(chains):
                views = [chain_view(r, kind, first + chain) for r, (kind, first) in zip(refs, kinds)]
                kernel(chain, marks, *views)

    return pl.pallas_call(
        call,
        in_specs=[SMEM] + [VMEM] * (len(ins) + len(held)) + [ANY] * len(after),
        out_specs=[VMEM] * (len(outs) + 1),
        out_shape=shapes + [TOKEN],
        input_output_aliases=aliases,
        compiler_params=pltpu.CompilerParams(vmem_limit_bytes=VMEM_LIMIT),
        cost_estimate=pl.CostEstimate(flops=10**10, bytes_accessed=10**7, transcendentals=0),
        name=name,
    )(marks, *[a for a, _, _ in ins], *held, *after)


def ring_spot(marks, step, way):
    return lax.rem(marks[2] + 2 * RING + way * step, RING)


def span(at):
    return pl.ds(pl.multiple_of(at * BLOCK, BLOCK), BLOCK)


def cut(ref, at):
    return ref[:, span(at)]


def set_rows(marks, block, which):
    pieces = []
    for chain in range(block.shape[0] // SEQ):
        piece = block[chain * SEQ : (chain + 1) * SEQ]
        pieces.append(jnp.where(marks[3 + chain] == which, piece, jnp.zeros_like(piece)))
    return jnp.concatenate(pieces, axis=0)


def all_rows(refs, at):
    return jnp.concatenate([cut(ref, at) for ref in refs], axis=0)


def feed_shard(marks, which, hidden, d_down, low, d_pre):
    return (
        dot_cols(set_rows(marks, hidden, which), d_down).astype(BF),
        dot_cols(set_rows(marks, low, which), d_pre).astype(BF),
    )


def feed_weights_kernel(step, parts, marks, *refs):
    hidden, d_down, low, d_pre = [refs[n * parts : (n + 1) * parts] for n in range(4)]
    out, token = refs[4 * parts :]
    sign_off(token)
    for which, way in ((0, -1), (1, 1)):
        spot = ring_spot(marks, step, way)
        far, near = lax.div(spot, 2), lax.rem(spot, 2)
        out[which, :BLOCK], out[which, BLOCK:] = feed_shard(
            marks,
            which,
            all_rows(hidden, far),
            all_rows(d_down, near),
            all_rows(low, near),
            all_rows(d_pre, far),
        )


def two_halves(value):
    high = value.astype(BF).astype(F32)
    return jnp.concatenate([high, value - high], axis=0).astype(BF)


def one_whole(rows):
    rows = rows.astype(F32)
    return rows[: TAIL // 2] + rows[TAIL // 2 :]


def count_rows(live, predicted, targets):
    symbols = lax.broadcasted_iota(jnp.int32, (128, live.shape[1]), 0)
    hits = (targets[...] == symbols) & (live[...] > 0)
    right = hits & (predicted[...] == targets[...])
    ones = jnp.ones((8, live.shape[1]), BF)
    found = [dot_rows(ones, h.astype(F32).astype(BF)) for h in (hits, right)]
    return jnp.concatenate(found + [jnp.zeros_like(found[0])], axis=1)[0:1]


def attn_weights_kernel(step, parts, marks, *refs):
    rows, d_joined, mixed, d_attn = [refs[n * parts : (n + 1) * parts] for n in range(4)]
    bias, *sums, live, predicted, targets, out, token = refs[4 * parts :]
    sign_off(token)
    for which, way in ((0, -1), (1, 1)):
        spot = ring_spot(marks, step, way)
        far, near = lax.div(spot, 2), lax.rem(spot, 2)

        @pl.when(far < 3)
        def _():
            out[which, :BLOCK] = dot_cols(
                set_rows(marks, all_rows(rows, near), which), all_rows(d_joined, far)
            ).astype(BF)

        @pl.when(far == 3)
        def _():
            out[which, :BLOCK] = dot_cols(
                set_rows(marks, all_rows(mixed, 0), which), all_rows(d_attn, near)
            ).astype(BF)

        early = far < 2
        small = jnp.where(
            early,
            bias[which, :, span(jnp.where(early, spot, 0))],
            sums[which][jnp.where(early, 0, far - 2), :, span(near)],
        )
        place = lax.broadcasted_iota(jnp.int32, (TAIL // 2, BLOCK), 0)
        small = jnp.where(place == 0, small, 0.0)
        out[which, BLOCK:] = two_halves(small)
        if which == 0:

            @pl.when(spot == 0)
            def _():
                counts = count_rows(live, predicted, targets)
                out[which, BLOCK:] = two_halves(jnp.where(place == 1, counts, small))


def run_weights(kernel, name, marks, step, lists, rest, rows_out, cost, after):
    ins = [a for arrays in lists for a in arrays] + list(rest)
    return pl.pallas_call(
        behind(functools.partial(kernel, step + 1, len(lists[0])), len(ins), len(after)),
        in_specs=[SMEM] + [VMEM] * len(ins) + [ANY] * len(after),
        out_specs=[VMEM, VMEM],
        out_shape=[jax.ShapeDtypeStruct((2, rows_out, BLOCK), BF), TOKEN],
        compiler_params=pltpu.CompilerParams(vmem_limit_bytes=VMEM_LIMIT),
        cost_estimate=pl.CostEstimate(flops=cost, bytes_accessed=10**6, transcendentals=0),
        name=name,
    )(marks, *ins, *after)


def add_kernel(tail, ahead, back, local, out_ahead, out_back, token):
    sign_off(token)
    for which, (ref, out) in enumerate(((ahead, out_ahead), (back, out_back))):
        total = ref[...].astype(F32) + local[which].astype(F32)
        out[...] = total.astype(BF)
        if tail:
            out[tail:] = two_halves(one_whole(total[tail:]))


def add_step(pair, local, after):
    shape = local.shape[1:]
    tail = BLOCK if shape[0] == BLOCK + TAIL else 0

    def call(*refs):
        add_kernel(tail, *refs[:3], *refs[3 + len(after) :])

    return pl.pallas_call(
        call,
        in_specs=[VMEM] * 3 + [ANY] * len(after),
        out_specs=[VMEM] * 3,
        out_shape=[jax.ShapeDtypeStruct(shape, BF)] * 2 + [TOKEN],
        compiler_params=pltpu.CompilerParams(vmem_limit_bytes=VMEM_LIMIT),
        cost_estimate=pl.CostEstimate(flops=3*10**9, bytes_accessed=10**6, transcendentals=0),
        name="ring_add",
    )(*pair, local, *after)


def feed_place_kernel(step, marks, ahead, back, outs, wide, sems):
    down, up = outs
    copies = []
    for which, (ref, way) in enumerate(((ahead, -1), (back, 1))):
        spot = ring_spot(marks, step, way)
        far, near = lax.div(spot, 2), lax.rem(spot, 2)
        wide[which] = ref[...].astype(F32)
        copies += [
            pltpu.make_async_copy(
                wide.at[which, :BLOCK], down.at[which, span(far), span(near)], sems.at[2 * which]
            ),
            pltpu.make_async_copy(
                wide.at[which, BLOCK:], up.at[which, span(near), span(far)], sems.at[2 * which + 1]
            ),
        ]
        for copy in copies[-2:]:
            copy.start()
    for copy in copies:
        copy.wait()


def attn_place_kernel(step, marks, ahead, back, outs, wide, sems):
    joint, output, small = outs
    copies = []
    for which, (ref, way) in enumerate(((ahead, -1), (back, 1))):
        spot = ring_spot(marks, step, way)
        far, near = lax.div(spot, 2), lax.rem(spot, 2)
        wide[which] = ref[...].astype(F32)
        wide[which, BLOCK : BLOCK + TAIL // 2] = one_whole(ref[BLOCK:])
        copy = pltpu.make_async_copy(
            wide.at[which, BLOCK : BLOCK + TAIL // 2], small.at[which, spot], sems.at[2 + which]
        )
        copy.start()
        copies.append(copy)

        @pl.when(far < 3)
        def _():
            copy = pltpu.make_async_copy(
                wide.at[which, :BLOCK], joint.at[which, far, span(near)], sems.at[which]
            )
            copy.start()
            copy.wait()

        @pl.when(far == 3)
        def _():
            copy = pltpu.make_async_copy(
                wide.at[which, :BLOCK], output.at[which, :, span(near)], sems.at[which]
            )
            copy.start()
            copy.wait()

    for copy in copies:
        copy.wait()


def place_step(kernel, name, marks, step, pair, held, after):
    shape = pair[0].shape
    block = pl.BlockSpec(shape, lambda i, *_: (0, 0))

    count = len(held)

    def call(marks, ahead, back, *refs):
        refs = refs[count + len(after) :]
        sign_off(refs[count])
        kernel(step, marks, ahead, back, refs[:count], *refs[count + 1 :])

    return pl.pallas_call(
        call,
        grid_spec=pltpu.PrefetchScalarGridSpec(
            num_scalar_prefetch=1,
            grid=(1,),
            in_specs=[block, block] + [HBM] * count + [ANY] * len(after),
            out_specs=[HBM] * count + [TOKEN_BLOCK],
            scratch_shapes=[pltpu.VMEM((2,) + shape, F32), pltpu.SemaphoreType.DMA((4,))],
        ),
        out_shape=[jax.ShapeDtypeStruct(h.shape, h.dtype) for h in held] + [TOKEN],
        input_output_aliases={3 + i: i for i in range(count)},
        compiler_params=pltpu.CompilerParams(vmem_limit_bytes=VMEM_LIMIT),
        cost_estimate=pl.CostEstimate(
            flops=10**10, bytes_accessed=10**6, transcendentals=0
        ),
        name=name,
    )(marks, *pair, *held, *after)


def unwritten(*shapes):
    return pl.pallas_call(
        lambda *refs: None,
        out_specs=[HBM] * len(shapes),
        out_shape=[jax.ShapeDtypeStruct(s, F32) for s in shapes],
        compiler_params=pltpu.CompilerParams(vmem_limit_bytes=1024 * 1024),
        name="unwritten",
    )()


class Ring:
    def __init__(self):
        self.count = lax.axis_size("dp")
        assert self.count % RING == 0
        order = list(range(0, RING, 2)) + list(range(1, RING, 2))[::-1]
        rank = lax.rem(lax.axis_index("dp"), RING)
        self.place = jnp.zeros((), jnp.int32)
        for at, member in enumerate(order):
            self.place = jnp.where(rank == member, at, self.place)
        self.ahead = [
            (base + order[i], base + order[(i + 1) % RING])
            for base in range(0, self.count, RING)
            for i in range(RING)
        ]
        self.back = [(b, a) for a, b in self.ahead]

    def send(self, pair):
        return lax.ppermute(pair[0], "dp", self.ahead), lax.ppermute(pair[1], "dp", self.back)

    def across(self, pair):
        result = []
        for value in pair:
            total = value.astype(F32)
            moving = value
            for _ in range(self.count // RING - 1):
                pairs = [(i, (i + RING) % self.count) for i in range(self.count)]
                moving = lax.ppermute(moving, "dp", pairs)
                total = total + moving.astype(F32)
            low = total.astype(BF)
            if total.shape[0] == BLOCK + TAIL and self.count > RING:
                tail = two_halves(one_whole(total[BLOCK:]))
                low = jnp.concatenate([low[:BLOCK], tail], axis=0)
            result.append(low)
        return result


def part_sizes(chains):
    bounds = [chains * sum(PARTS[:p]) // sum(PARTS) for p in range(len(PARTS) + 1)]
    return [high - low for low, high in zip(bounds, bounds[1:])], bounds[:-1]


def shards(
    chain_inputs,
    cotangent,
    chain_tags,
    pad_mask,
    predicted,
    target_ids,
    joint_proj,
    output_proj,
    up_proj,
    up_bias,
    down_proj,
    norm_gain,
    norm_shift,
):
    section = lax.axis_index("section")
    core = lax.axis_index("tensor")
    tokens, half = chain_inputs.shape
    width = 2 * half
    all_chains = tokens // SEQ
    sizes, starts = part_sizes(all_chains)
    parts = range(len(sizes))
    ring = Ring()
    small = [ids.reshape(1, tokens) for ids in (pad_mask, predicted, target_ids)]
    joint = joint_proj[0].transpose(0, 2, 1, 3)
    output, up, bias, down = output_proj[0], up_proj[0], up_bias[0], down_proj[0]
    places = jnp.stack([section, core, ring.place]).astype(jnp.int32)
    marks, joint, output, own_rows = prepare(
        places, chain_tags, small[0], [joint, output, chain_inputs]
    )
    gains, shifts = norm_gain[0], norm_shift[0]
    units = up.shape[2]
    local = output.shape[1]
    heads = local // HEAD_DIM
    cot_other = swap(cotangent)
    rows_other = swap(chain_inputs)

    order = Order()

    kept = [{} for _ in parts]
    feed = [{} for _ in parts]
    attn = [{} for _ in parts]
    sent = [{} for _ in parts]
    sums = dict(
        feed=jnp.zeros((2, 1, width), F32),
        attn=jnp.zeros((2, 1, width), F32),
        bias=jnp.zeros((2, 1, units), F32),
    )

    def run(kernel, name, active, p, ins, outs, held, totals):
        outs = [(shape, dtype, kind, held.get(key)) for key, shape, dtype, kind in outs] + [
            (sums[key].shape, F32, "whole", sums[key]) for key in totals
        ]
        return order.run(run_chains, kernel, name, active, marks, sizes[p], ins, outs)

    def attn_forward(active, p, own, other, first):
        ins = [(own, "rows", first), (other, "rows", first)]
        ins += [(joint, "whole", 0), (output, "whole", 0)]
        outs = [
            ("rows", (width,), BF, "rows"),
            ("part", (width,), BF, "rows"),
            ("joined", (3 * local,), BF, "rows"),
            ("probs", (heads, SEQ, SEQ), BF, "chain"),
            ("mixed", (local,), BF, "rows"),
        ]
        kernel = functools.partial(attn_forward_kernel, starts[p], all_chains)
        found = run(kernel, "attn_forward", active, p, ins, outs, kept[p], [])
        kept[p].update(zip([o[0] for o in outs], found))
        kept[p]["part_other"] = swap(kept[p]["part"])

    def feed_forward(active, p):
        ins = [(kept[p][n], "rows", 0) for n in ("rows", "part", "part_other")]
        ins += [(a, "whole", 0) for a in (gains, shifts, up, bias, down)]
        outs = [
            ("down", (width,), BF, "rows"),
            ("normal", (width,), F32, "rows"),
            ("inv_root", (1,), F32, "rows"),
            ("low", (width,), BF, "rows"),
            ("hidden", (units,), BF, "rows"),
            ("slope", (units,), BF, "rows"),
        ]
        kernel = functools.partial(feed_forward_kernel, starts[p])
        found = run(kernel, "feed_forward", active, p, ins, outs, kept[p], [])
        kept[p].update(zip([o[0] for o in outs], found))
        kept[p]["down_other"] = swap(kept[p]["down"])

    def feed_back(active, p, own, other, first):
        ins = [(kept[p][n], "rows", 0) for n in ("normal", "down", "down_other")]
        ins += [(gains, "whole", 0), (shifts, "whole", 0)]
        ins += [(own, "rows", first), (other, "rows", first)]
        ins += [(kept[p]["slope"], "rows", 0)]
        ins += [(turned["up"], "whole", 0), (turned["down"], "whole", 0)]
        outs = [
            ("back", (width,), F32, "rows"),
            ("part", (width,), BF, "rows"),
            ("d_down", (width,), BF, "rows"),
            ("d_pre", (units,), BF, "rows"),
            ("outputs", (half,), BF, "rows"),
        ]
        kernel = functools.partial(feed_back_kernel, starts[p])
        *found, sums["feed"], sums["bias"] = run(
            kernel, "feed_back", active, p, ins, outs, feed[p], ["feed", "bias"]
        )
        feed[p].update(zip([o[0] for o in outs], found))
        feed[p]["part_other"] = swap(feed[p]["part"])

    def attn_back(active, p):
        ins = [(feed[p][n], "rows", 0) for n in ("back", "part", "part_other")]
        ins += [(kept[p]["normal"], "rows", 0), (kept[p]["inv_root"], "rows", 0)]
        ins += [(gains, "whole", 0), (kept[p]["joined"], "rows", 0), (kept[p]["probs"], "chain", 0)]
        ins += [(joint, "whole", 0), (output, "whole", 0)]
        outs = [
            ("mine", (half,), F32, "rows"),
            ("theirs", (half,), BF, "rows"),
            ("d_attn", (width,), BF, "rows"),
            ("d_joined", (3 * local,), BF, "rows"),
        ]
        kernel = functools.partial(attn_back_kernel, starts[p])
        *found, sums["attn"] = run(kernel, "attn_back", active, p, ins, outs, attn[p], ["attn"])
        attn[p].update(zip([o[0] for o in outs], found))

    def input_gradient(p, theirs):
        return attn[p]["mine"] + swap(theirs).astype(F32)

    def across(value):
        return lax.ppermute(value, "section", [(0, 1), (1, 0)])

    turned = {}

    def turn_weights(active):
        held = [turned[n] for n in ("up", "down") if n in turned]
        turned["up"], turned["down"] = order.run(turn, active, marks, [up, down], held)

    def attn_early(p):
        attn_forward(0, p, own_rows, rows_other, starts[p])

    def feed_early(p):
        feed_forward(0, p)

    def hand_on(p):
        ins = [(kept[p][n], "rows", 0) for n in ("normal", "down", "down_other")]
        ins += [(gains, "whole", 0), (shifts, "whole", 0)]
        outs = [("moved", (half,), BF, "rows")]
        found = run(last_norm_kernel, "last_norm", 0, p, ins, outs, {}, [])
        sent[p]["on"] = across(found[0])

    def receive(p):
        moved = order.after(sent[p]["on"])
        sent[p]["on"] = (moved, swap(moved))

    def attn_late(p):
        attn_forward(1, p, *sent[p]["on"], 0)

    def feed_late(p):
        feed_forward(1, p)

    def feed_first(p):
        feed_back(1, p, cotangent, cot_other, starts[p])

    def attn_first(p):
        attn_back(1, p)
        sent[p]["back"] = across(input_gradient(p, attn[p]["theirs"]).astype(BF))

    def receive_back(p):
        moved = order.after(sent[p]["back"])
        sent[p]["back"] = (moved, swap(moved))

    def feed_last(p):
        feed_back(0, p, *sent[p]["back"], 0)

    def attn_last(p):
        attn_back(0, p)

    for step, p in (
        (attn_early, 0),
        (attn_early, 1),
        (feed_early, 0),
        (turn_weights, 1),
        (hand_on, 0),
        (feed_early, 1),
        (attn_early, 2),
        (receive, 0),
        (attn_late, 0),
        (hand_on, 1),
        (feed_late, 0),
        (feed_early, 2),
        (feed_first, 0),
        (hand_on, 2),
        (receive, 1),
        (attn_first, 0),
        (attn_late, 1),
        (receive, 2),
        (turn_weights, 0),
        (feed_late, 1),
        (attn_late, 2),
        (feed_first, 1),
        (feed_late, 2),
        (receive_back, 0),
        (attn_first, 1),
        (feed_last, 0),
        (feed_first, 2),
        (receive_back, 1),
        (attn_first, 2),
        (feed_last, 1),
        (receive_back, 2),
        (feed_last, 2),
    ):
        step(p)
    feed_lists = [
        [kept[p]["hidden"] for p in parts],
        [feed[p]["d_down"] for p in parts],
        [kept[p]["low"] for p in parts],
        [feed[p]["d_pre"] for p in parts],
    ]

    def feed_weights(step, cost=3 * 10**9):
        return order.run(
            run_weights,
            feed_weights_kernel,
            "feed_weights",
            marks,
            step,
            feed_lists,
            [],
            2 * BLOCK,
            cost,
        )[0]

    def add_local(pair, local):
        return order.run(add_step, pair, local)

    shard = feed_weights(0)
    feed_pair = ring.send((shard[0], shard[1]))
    shard = feed_weights(1)
    for p in parts:
        attn_last(p)
    feed_pair = ring.send(add_local(feed_pair, shard))
    attn_lists = [
        [kept[p]["rows"] for p in parts],
        [attn[p]["d_joined"] for p in parts],
        [kept[p]["mixed"] for p in parts],
        [attn[p]["d_attn"] for p in parts],
    ]

    small = [sums["bias"], sums["attn"], sums["feed"], *small]

    def attn_weights(step, cost=3 * 10**9):
        return order.run(
            run_weights,
            attn_weights_kernel,
            "attn_weights",
            marks,
            step,
            attn_lists,
            small,
            BLOCK + TAIL,
            cost,
        )[0]

    shard = attn_weights(0, 10**9)
    attn_pair = ring.send((shard[0], shard[1]))
    attn_local = attn_weights(1, 10**9)
    feed_local = feed_weights(2, 10**9)
    streams = [
        dict(
            pair=attn_pair,
            local=attn_local,
            weights=attn_weights,
            sent=1,
            kernel=attn_place_kernel,
            name="attn_place",
            held=unwritten((2, 3, width, local), (2, local, width), (2, RING, 8, BLOCK)),
        ),
        dict(
            pair=feed_pair,
            local=feed_local,
            weights=feed_weights,
            sent=2,
            kernel=feed_place_kernel,
            name="feed_place",
            held=unwritten((2, units, width), (2, width, units)),
        ),
    ]

    def advance(stream):
        sent = stream["sent"]
        *pair, token = lax.optimization_barrier((*stream["pair"], *order.tokens))
        order.tokens = (token,)
        if sent < RING:
            pair = add_local(pair, stream["local"])
            if sent == RING - 1:
                pair = ring.across(pair)
        stream["pair"] = ring.send(pair) if sent < 2 * RING - 2 else None
        if sent < RING - 1:
            stream["local"] = stream["weights"](sent + 1)
        else:
            stream["held"] = order.run(
                place_step,
                stream["kernel"],
                stream["name"],
                marks,
                sent - RING + 1,
                pair,
                stream["held"],
            )
        stream["sent"] += 1

    attn_stream, feed_stream = streams
    input_grads = []
    while attn_stream["pair"] is not None or feed_stream["pair"] is not None:
        if attn_stream["sent"] == 2 * RING - 2:
            input_grads = [input_gradient(p, order.after(attn[p]["theirs"])) for p in parts]
        if feed_stream["pair"] is not None:
            advance(feed_stream)
        if attn_stream["pair"] is not None:
            advance(attn_stream)
    joint_out, output_out, small_out = attn_stream["held"]
    down_out, up_out = feed_stream["held"]

    def whole(pieces):
        return jnp.concatenate(pieces, axis=0)

    input_grads = whole(input_grads)
    rows = small_out[:, :, 0]
    bias_grad = rows[:, :4].reshape(2, units)
    norm_sums = rows[:, 4:].reshape(2, 2, width)
    counts = small_out[0, 0, 1].reshape(3, 128)[:2, :SYMBOLS]
    return (
        whole([feed[p]["outputs"] for p in parts])[None],
        input_grads[None],
        joint_out.transpose(0, 2, 1, 3)[None],
        output_out[None],
        up_out[None],
        bias_grad[None],
        down_out[None],
        norm_sums[:, 0][None],
        norm_sums[:, 1][None],
        counts.astype(jnp.int32),
    )


def solution(mesh):
    return jax.shard_map(
        shards,
        mesh=mesh,
        in_specs=(
            P("dp", "tensor"),
            P("dp", "tensor"),
            P("dp"),
            P("dp"),
            P("dp"),
            P("dp"),
            P("section", None, None, None, "tensor"),
            P("section", None, "tensor", None),
            P("section", None, None, "tensor"),
            P("section", None, "tensor"),
            P("section", None, "tensor", None),
            P("section", None, None),
            P("section", None, None),
        ),
        out_specs=(
            P("section", "dp", "tensor"),
            P("section", "dp", "tensor"),
            P("section", None, None, None, "tensor"),
            P("section", None, "tensor", None),
            P("section", None, None, "tensor"),
            P("section", None, "tensor"),
            P("section", None, "tensor", None),
            P("section", None, None),
            P("section", None, None),
            P(),
        ),
        check_vma=False,
    )
```

```python
import functools

import jax
import jax.numpy as jnp
from jax import lax
from jax.experimental import pallas as pl
from jax.experimental.pallas import tpu as pltpu
from jax.sharding import PartitionSpec as P

HEAD_DIM = 64
SYMBOLS = 24
SEQ = 160
PARTS = (2, 2, 2)
RING = 8
BLOCK = 384
TAIL = 16
EPS = 1e-05
SCALE = HEAD_DIM**-0.5
VMEM_LIMIT = 7 * 1024 * 1024

root_half = 0.7071067811865476
root_two_pi = 0.3989422804014327
BF = jnp.bfloat16
F32 = jnp.float32


def swap(value):
    return lax.ppermute(value, "tensor", [(0, 1), (1, 0)])


def dot(a, b):
    return jnp.dot(a, b, preferred_element_type=F32)


def dot_rows(a, b):
    return lax.dot_general(a, b, (((1,), (1,)), ((), ())), preferred_element_type=F32)


def dot_cols(a, b):
    return lax.dot_general(a, b, (((0,), (0,)), ((), ())), preferred_element_type=F32)


def in_order(core, own, other):
    first = core == 0
    return jnp.concatenate(
        [jnp.where(first, own, other), jnp.where(first, other, own)], axis=1
    )


def own_part(core, value):
    half = value.shape[1] // 2
    return jnp.where(core == 0, value[:, :half], value[:, half:])


def normalise(rows):
    centred = rows - jnp.mean(rows, axis=-1, keepdims=True)
    inv_root = lax.rsqrt(jnp.mean(centred * centred, axis=-1, keepdims=True) + EPS)
    return centred * inv_root, inv_root


def norm_back(grads, normal, inv_root, gain):
    scaled = grads * gain
    inner = (
        scaled
        - jnp.mean(scaled, axis=-1, keepdims=True)
        - normal * jnp.mean(scaled * normal, axis=-1, keepdims=True)
    )
    return inner * inv_root


def pair_spans(width):
    return [slice(at, at + 2 * HEAD_DIM) for at in range(0, width, 2 * HEAD_DIM)]


def left_head():
    return lax.broadcasted_iota(jnp.int32, (1, 2 * HEAD_DIM), 1) < HEAD_DIM


def pair_scores(first, second):
    left = left_head().astype(BF)
    both = jnp.concatenate([first * left, first * (1 - left)], axis=0)
    return dot_rows(both, second).reshape(2, SEQ, SEQ)


def pair_product(matrices, block):
    found = dot(matrices.reshape(2 * SEQ, SEQ), block)
    return jnp.where(left_head(), found[:SEQ], found[SEQ:]).astype(BF)


def pair_turned(matrices):
    return jnp.concatenate([matrices[0].T, matrices[1].T], axis=0)


def attn_forward_kernel(start, count, chain, marks, own, other, joint, output, *refs):
    tag = marks[3 + start + chain]
    core = marks[1]
    a, b = own[...], other[...]
    rows = in_order(core, a, b)
    q, k, v = [dot(rows, joint[tag, j]).astype(BF) for j in range(3)]
    key_live = lax.broadcasted_iota(jnp.int32, (1, SEQ, 1), 1) < marks[3 + count + start + chain]
    spans = pair_spans(q.shape[1])
    scores = [pair_scores(k[:, s], q[:, s] * jnp.asarray(SCALE, BF)) for s in spans]
    probs = []
    for found in scores:
        found = jnp.where(key_live, found, -1000000000.0)
        shifted = jnp.exp(found - jnp.max(found, axis=1, keepdims=True))
        probs.append((shifted * (1.0 / jnp.sum(shifted, axis=1, keepdims=True))).astype(BF))
    mixed = jnp.concatenate(
        [pair_product(pair_turned(p), v[:, s]) for p, s in zip(probs, spans)], axis=1
    )
    refs[0][...] = rows
    refs[1][...] = dot(mixed, output[tag]).astype(BF)
    refs[2][...] = jnp.concatenate([q, k, v], axis=1)
    for at, found in enumerate(probs):
        refs[3][0, 2 * at : 2 * at + 2] = found
    refs[4][...] = mixed


def feed_forward_kernel(start, chain, marks, rows, part, other, gains, shifts, up, bias, down, *outs):
    tag = marks[3 + start + chain]
    total = rows[...].astype(F32) + (part[...].astype(F32) + other[...].astype(F32))
    normal, inv_root = normalise(total)
    low = (normal * gains[0:1] + shifts[0:1]).astype(BF)
    pre = dot(low, up[tag]) + jnp.where(tag == 0, bias[0:1], bias[1:2]).astype(F32)
    cdf = 0.5 * (1.0 + lax.erf(pre * root_half))
    hidden = (pre * cdf).astype(BF)
    outs[0][...] = dot(hidden, down[tag]).astype(BF)
    outs[1][...] = normal.astype(BF)
    outs[2][...] = inv_root
    outs[3][...] = low
    outs[4][...] = hidden
    outs[5][...] = (cdf + pre * jnp.exp(-0.5 * pre * pre) * root_two_pi).astype(BF)


def second_norm(normal, part, other, gains, shifts):
    first = normal[...].astype(F32) * gains[0:1] + shifts[0:1]
    return normalise(first + (part[...].astype(F32) + other[...].astype(F32)))


def last_norm_kernel(chain, marks, normal, part, other, gains, shifts, out):
    second, _ = second_norm(normal, part, other, gains, shifts)
    out[...] = own_part(marks[1], (second * gains[1:2] + shifts[1:2]).astype(BF))


def add_sums(grads, normal, sums):
    sums[0] += jnp.sum(grads * normal, axis=0, keepdims=True)
    sums[1] += jnp.sum(grads, axis=0, keepdims=True)


def feed_back_kernel(
    start, chain, marks, normal, part, other, gains, shifts, own, partner, slope, up, down, *outs
):
    tag = marks[3 + start + chain]
    core = marks[1]
    a, b = own[...], partner[...]
    grads = in_order(core, a, b).astype(F32)
    second, inv_root = second_norm(normal, part, other, gains, shifts)
    back = norm_back(grads, second, inv_root, gains[1:2])
    low = back.astype(BF)
    d_pre = (dot(low, down[tag]) * slope[...].astype(F32)).astype(BF)
    outs[0][...] = dot(d_pre, up[tag]).astype(BF)
    outs[1][...] = low
    outs[2][...] = d_pre
    outs[3][...] = own_part(core, (second * gains[1:2] + shifts[1:2]).astype(BF))
    add_sums(grads, second, outs[4])
    outs[5][tag] += jnp.sum(d_pre.astype(F32), axis=0, keepdims=True)


def attn_back_kernel(
    start, chain, marks, back, part, other, normal, inv_root, gains, joined, probs, joint, output, *outs
):
    tag = marks[3 + start + chain]
    core = marks[1]
    grads = back[...].astype(F32) + (part[...].astype(F32) + other[...].astype(F32))
    normal = normal[...].astype(F32)
    back_one = norm_back(grads, normal, inv_root[...], gains[0:1])
    low = back_one.astype(BF)
    d_mixed = dot_rows(low, output[tag]).astype(BF)
    width = d_mixed.shape[1]
    q, k, v = [joined[:, j * width : (j + 1) * width] for j in range(3)]
    spans = pair_spans(width)
    d_probs = [pair_scores(v[:, s], d_mixed[:, s]) for s in spans]
    held = [probs[0, 2 * at : 2 * at + 2] for at in range(len(spans))]
    d_scores = []
    for found, kept in zip(d_probs, held):
        wide = kept.astype(F32)
        inner = jnp.sum(wide * found, axis=1, keepdims=True)
        d_scores.append((wide * (found - inner)).astype(BF))
    scale = jnp.asarray(SCALE, BF)
    d_k = [pair_product(d, q[:, s]) * scale for d, s in zip(d_scores, spans)]
    d_v = [pair_product(h, d_mixed[:, s]) for h, s in zip(held, spans)]
    d_q = [pair_product(pair_turned(d), k[:, s]) * scale for d, s in zip(d_scores, spans)]
    pieces = [d_q, d_k, d_v]
    blocks = [jnp.concatenate(p, axis=1) for p in pieces]
    d_rows = sum(dot_rows(blocks[j], joint[tag, j]) for j in range(3)).astype(BF)
    outs[0][...] = own_part(core, back_one) + own_part(core, d_rows).astype(F32)
    outs[1][...] = own_part(1 - core, d_rows)
    outs[2][...] = low
    outs[3][...] = jnp.concatenate(blocks, axis=1)
    add_sums(grads, normal, outs[4])


class Marks:
    def __init__(self, ref):
        self.rows = ref[...]

    def __getitem__(self, at):
        return self.rows[0, at]


def behind(kernel, taken, ignored):
    def call(marks, *refs):
        kernel(Marks(marks), *refs[:taken], *refs[taken + ignored :])

    return call


ANY = pl.BlockSpec(memory_space=pl.ANY)
HBM = pl.BlockSpec(memory_space=pltpu.HBM)
TOKEN = jax.ShapeDtypeStruct((8, 128), F32)


def sign_off(token):
    token[...] = jnp.zeros_like(token)


class Order:
    def __init__(self):
        self.tokens = ()

    def run(self, call, *args):
        *results, token = call(*args, self.tokens)
        self.tokens = (token,)
        return results

    def wait(self, value):
        self.tokens = tuple(lax.optimization_barrier((*self.tokens, value))[:-1])

    def after(self, value):
        return lax.optimization_barrier((value, *self.tokens))[0]


VMEM = pl.BlockSpec(memory_space=pltpu.VMEM)
SMEM = pl.BlockSpec(memory_space=pltpu.SMEM)


def chain_view(ref, kind, at):
    if kind == "rows":
        return ref.at[at * SEQ : (at + 1) * SEQ]
    return ref.at[at : at + 1] if kind == "chain" else ref


def prepare_kernel(chains, count, places, *refs):
    sources, marks, held = refs[:count], refs[count], refs[count + 1 : 2 * count - 1]
    tags, live, sems = refs[2 * count - 1 :]
    copies = [
        pltpu.make_async_copy(source, target, sems.at[at])
        for at, (source, target) in enumerate(zip(sources, (tags, live) + held))
    ]
    for copy in copies:
        copy.start()
    for copy in copies[:2]:
        copy.wait()
    token = lax.broadcasted_iota(jnp.int32, live.shape, 1)
    found = [places[at] for at in range(3)]
    found += [jnp.where(tags[chain] > 0, 1, 0) for chain in range(chains)]
    for chain in range(chains):
        inside = (token >= chain * SEQ) & (token < (chain + 1) * SEQ)
        found.append(jnp.sum(jnp.where(inside, live[...], 0)))
    lane = lax.broadcasted_iota(jnp.int32, marks.shape, 1)
    rows = jnp.zeros(marks.shape, jnp.int32)
    for at, value in enumerate(found):
        rows = jnp.where(lane == at, value, rows)
    marks[...] = rows
    for copy in copies[2:]:
        copy.wait()


def prepare(places, tags, live, arrays):
    chains = tags.shape[0]
    sources = [tags, live, *arrays]
    count = len(sources)
    return pl.pallas_call(
        functools.partial(prepare_kernel, chains, count),
        in_specs=[SMEM] + [HBM] * count,
        out_specs=[VMEM] * (1 + len(arrays)),
        out_shape=[jax.ShapeDtypeStruct((8, 128), jnp.int32)]
        + [jax.ShapeDtypeStruct(a.shape, a.dtype) for a in arrays],
        scratch_shapes=[
            pltpu.SMEM(tags.shape, jnp.int32),
            pltpu.VMEM(live.shape, jnp.int32),
            pltpu.SemaphoreType.DMA((count,)),
        ],
        compiler_params=pltpu.CompilerParams(vmem_limit_bytes=1024 * 1024),
        name="prepare",
    )(places, *[pltpu.with_memory_space_constraint(a, pltpu.HBM) for a in sources])


def turn(active, marks, arrays, held, after):
    count = len(arrays)
    skipped = count + len(held) + len(after)

    def call(marks, *refs):
        marks = Marks(marks)
        sign_off(refs[-1])

        @pl.when(marks[0] == active)
        def _():
            for source, target in zip(refs[:count], refs[skipped:]):
                for at in range(source.shape[0]):
                    target[at] = source[at].T

    return pl.pallas_call(
        call,
        in_specs=[VMEM] * (1 + count + len(held)) + [ANY] * len(after),
        out_specs=[VMEM] * (count + 1),
        out_shape=[jax.ShapeDtypeStruct((a.shape[0], a.shape[2], a.shape[1]), BF) for a in arrays]
        + [TOKEN],
        input_output_aliases={1 + count + at: at for at in range(len(held))},
        compiler_params=pltpu.CompilerParams(vmem_limit_bytes=VMEM_LIMIT),
        cost_estimate=pl.CostEstimate(flops=10**10, bytes_accessed=10**7, transcendentals=0),
        name="turn",
    )(marks, *arrays, *held, *after)


def run_chains(kernel, name, active, marks, chains, ins, outs, after):
    shapes, held, aliases = [], [], {}
    for trailing, dtype, kind, array in outs:
        lead = {"rows": (chains * SEQ,), "chain": (chains,), "whole": ()}[kind]
        if array is not None:
            aliases[1 + len(ins) + len(held)] = len(shapes)
            held.append(array)
        shapes.append(jax.ShapeDtypeStruct(lead + trailing, dtype))
    kinds = [(kind, first) for _, kind, first in ins] + [(kind, 0) for _, _, kind, _ in outs]
    skipped = len(ins) + len(held) + len(after)

    def call(marks, *refs):
        marks = Marks(marks)
        *refs, token = refs[: len(ins)] + refs[skipped:]
        sign_off(token)

        @pl.when(marks[0] == active)
        def _():
            for chain in range(chains):
                views = [chain_view(r, kind, first + chain) for r, (kind, first) in zip(refs, kinds)]
                kernel(chain, marks, *views)

    return pl.pallas_call(
        call,
        in_specs=[VMEM] * (1 + len(ins) + len(held)) + [ANY] * len(after),
        out_specs=[VMEM] * (len(outs) + 1),
        out_shape=shapes + [TOKEN],
        input_output_aliases=aliases,
        compiler_params=pltpu.CompilerParams(vmem_limit_bytes=VMEM_LIMIT),
        cost_estimate=pl.CostEstimate(flops=10**10, bytes_accessed=10**7, transcendentals=0),
        name=name,
    )(marks, *[a for a, _, _ in ins], *held, *after)


def ring_spot(marks, step, way):
    return lax.rem(marks[2] + 2 * RING + way * step, RING)


def span(at):
    return pl.ds(pl.multiple_of(at * BLOCK, BLOCK), BLOCK)


def cut(ref, at):
    return ref[:, span(at)]


def set_rows(marks, block, which):
    pieces = []
    for chain in range(block.shape[0] // SEQ):
        piece = block[chain * SEQ : (chain + 1) * SEQ]
        pieces.append(jnp.where(marks[3 + chain] == which, piece, jnp.zeros_like(piece)))
    return jnp.concatenate(pieces, axis=0)


def all_rows(refs, at):
    return jnp.concatenate([cut(ref, at) for ref in refs], axis=0)


def feed_shard(marks, which, hidden, d_down, low, d_pre):
    return (
        dot_cols(set_rows(marks, hidden, which), d_down).astype(BF),
        dot_cols(set_rows(marks, low, which), d_pre).astype(BF),
    )


def feed_weights_kernel(step, parts, marks, *refs):
    hidden, d_down, low, d_pre = [refs[n * parts : (n + 1) * parts] for n in range(4)]
    out, token = refs[4 * parts :]
    sign_off(token)
    for which, way in ((0, -1), (1, 1)):
        spot = ring_spot(marks, step, way)
        far, near = lax.div(spot, 2), lax.rem(spot, 2)
        out[which, :BLOCK], out[which, BLOCK:] = feed_shard(
            marks,
            which,
            all_rows(hidden, far),
            all_rows(d_down, near),
            all_rows(low, near),
            all_rows(d_pre, far),
        )


def two_halves(value):
    high = value.astype(BF).astype(F32)
    return jnp.concatenate([high, value - high], axis=0).astype(BF)


def one_whole(rows):
    rows = rows.astype(F32)
    return rows[: TAIL // 2] + rows[TAIL // 2 :]


def count_rows(live, predicted, targets):
    symbols = lax.broadcasted_iota(jnp.int32, (128, live.shape[1]), 0)
    hits = (targets[...] == symbols) & (live[...] > 0)
    right = hits & (predicted[...] == targets[...])
    ones = jnp.ones((8, live.shape[1]), BF)
    found = [dot_rows(ones, h.astype(F32).astype(BF)) for h in (hits, right)]
    return jnp.concatenate(found + [jnp.zeros_like(found[0])], axis=1)[0:1]


def attn_weights_kernel(step, parts, marks, *refs):
    rows, d_joined, mixed, d_attn = [refs[n * parts : (n + 1) * parts] for n in range(4)]
    bias, *sums, live, predicted, targets, out, token = refs[4 * parts :]
    sign_off(token)
    for which, way in ((0, -1), (1, 1)):
        spot = ring_spot(marks, step, way)
        far, near = lax.div(spot, 2), lax.rem(spot, 2)

        @pl.when(far < 3)
        def _():
            out[which, :BLOCK] = dot_cols(
                set_rows(marks, all_rows(rows, near), which), all_rows(d_joined, far)
            ).astype(BF)

        @pl.when(far == 3)
        def _():
            out[which, :BLOCK] = dot_cols(
                set_rows(marks, all_rows(mixed, 0), which), all_rows(d_attn, near)
            ).astype(BF)

        early = far < 2
        small = jnp.where(
            early,
            bias[which, :, span(jnp.where(early, spot, 0))],
            sums[which][jnp.where(early, 0, far - 2), :, span(near)],
        )
        place = lax.broadcasted_iota(jnp.int32, (TAIL // 2, BLOCK), 0)
        small = jnp.where(place == 0, small, 0.0)
        out[which, BLOCK:] = two_halves(small)
        if which == 0:

            @pl.when(spot == 0)
            def _():
                counts = count_rows(live, predicted, targets)
                out[which, BLOCK:] = two_halves(jnp.where(place == 1, counts, small))


def run_weights(kernel, name, marks, step, lists, rest, rows_out, cost, after):
    ins = [a for arrays in lists for a in arrays] + list(rest)
    return pl.pallas_call(
        behind(functools.partial(kernel, step + 1, len(lists[0])), len(ins), len(after)),
        in_specs=[VMEM] * (1 + len(ins)) + [ANY] * len(after),
        out_specs=[VMEM, VMEM],
        out_shape=[jax.ShapeDtypeStruct((2, rows_out, BLOCK), BF), TOKEN],
        compiler_params=pltpu.CompilerParams(vmem_limit_bytes=VMEM_LIMIT),
        cost_estimate=pl.CostEstimate(flops=cost, bytes_accessed=10**6, transcendentals=0),
        name=name,
    )(marks, *ins, *after)


def add_kernel(tail, ahead, back, local, out_ahead, out_back, token):
    sign_off(token)
    for which, (ref, out) in enumerate(((ahead, out_ahead), (back, out_back))):
        total = ref[...].astype(F32) + local[which].astype(F32)
        out[...] = total.astype(BF)
        if tail:
            out[tail:] = two_halves(one_whole(total[tail:]))


def add_step(pair, local, after):
    shape = local.shape[1:]
    tail = BLOCK if shape[0] == BLOCK + TAIL else 0

    def call(*refs):
        add_kernel(tail, *refs[:3], *refs[3 + len(after) :])

    return pl.pallas_call(
        call,
        in_specs=[VMEM] * 3 + [ANY] * len(after),
        out_specs=[VMEM] * 3,
        out_shape=[jax.ShapeDtypeStruct(shape, BF)] * 2 + [TOKEN],
        compiler_params=pltpu.CompilerParams(vmem_limit_bytes=VMEM_LIMIT),
        cost_estimate=pl.CostEstimate(flops=3*10**9, bytes_accessed=10**6, transcendentals=0),
        name="ring_add",
    )(*pair, local, *after)


def feed_place_kernel(step, marks, ahead, back, outs, wide, sems):
    down, up = outs
    copies = []
    for which, (ref, way) in enumerate(((ahead, -1), (back, 1))):
        spot = ring_spot(marks, step, way)
        far, near = lax.div(spot, 2), lax.rem(spot, 2)
        wide[which] = ref[...].astype(F32)
        copies += [
            pltpu.make_async_copy(
                wide.at[which, :BLOCK], down.at[which, span(far), span(near)], sems.at[2 * which]
            ),
            pltpu.make_async_copy(
                wide.at[which, BLOCK:], up.at[which, span(near), span(far)], sems.at[2 * which + 1]
            ),
        ]
        for copy in copies[-2:]:
            copy.start()
    for copy in copies:
        copy.wait()


def attn_place_kernel(step, marks, ahead, back, outs, wide, sems):
    joint, output, small = outs
    copies = []
    for which, (ref, way) in enumerate(((ahead, -1), (back, 1))):
        spot = ring_spot(marks, step, way)
        far, near = lax.div(spot, 2), lax.rem(spot, 2)
        wide[which] = ref[...].astype(F32)
        wide[which, BLOCK : BLOCK + TAIL // 2] = one_whole(ref[BLOCK:])
        copy = pltpu.make_async_copy(
            wide.at[which, BLOCK : BLOCK + TAIL // 2], small.at[which, spot], sems.at[2 + which]
        )
        copy.start()
        copies.append(copy)

        @pl.when(far < 3)
        def _():
            copy = pltpu.make_async_copy(
                wide.at[which, :BLOCK], joint.at[which, far, span(near)], sems.at[which]
            )
            copy.start()
            copy.wait()

        @pl.when(far == 3)
        def _():
            copy = pltpu.make_async_copy(
                wide.at[which, :BLOCK], output.at[which, :, span(near)], sems.at[which]
            )
            copy.start()
            copy.wait()

    for copy in copies:
        copy.wait()


def place_step(kernel, name, marks, step, pair, held, after):
    shape = pair[0].shape
    count = len(held)

    def call(marks, ahead, back, *refs):
        refs = refs[count + len(after) :]
        sign_off(refs[count])
        kernel(step, Marks(marks), ahead, back, refs[:count], *refs[count + 1 :])

    return pl.pallas_call(
        call,
        in_specs=[VMEM] * 3 + [HBM] * count + [ANY] * len(after),
        out_specs=[HBM] * count + [VMEM],
        scratch_shapes=[pltpu.VMEM((2,) + shape, F32), pltpu.SemaphoreType.DMA((4,))],
        out_shape=[jax.ShapeDtypeStruct(h.shape, h.dtype) for h in held] + [TOKEN],
        input_output_aliases={3 + i: i for i in range(count)},
        compiler_params=pltpu.CompilerParams(vmem_limit_bytes=VMEM_LIMIT),
        cost_estimate=pl.CostEstimate(flops=10**10, bytes_accessed=10**6, transcendentals=0),
        name=name,
    )(marks, *pair, *held, *after)


def unwritten(*shapes):
    return pl.pallas_call(
        lambda *refs: None,
        out_specs=[HBM] * len(shapes),
        out_shape=[jax.ShapeDtypeStruct(s, F32) for s in shapes],
        compiler_params=pltpu.CompilerParams(vmem_limit_bytes=1024 * 1024),
        name="unwritten",
    )()


class Ring:
    def __init__(self):
        self.count = lax.axis_size("dp")
        assert self.count % RING == 0
        order = list(range(0, RING, 2)) + list(range(1, RING, 2))[::-1]
        rank = lax.rem(lax.axis_index("dp"), RING)
        self.place = jnp.zeros((), jnp.int32)
        for at, member in enumerate(order):
            self.place = jnp.where(rank == member, at, self.place)
        self.ahead = [
            (base + order[i], base + order[(i + 1) % RING])
            for base in range(0, self.count, RING)
            for i in range(RING)
        ]
        self.back = [(b, a) for a, b in self.ahead]

    def send(self, pair):
        return lax.ppermute(pair[0], "dp", self.ahead), lax.ppermute(pair[1], "dp", self.back)

    def across(self, pair):
        result = []
        for value in pair:
            total = value.astype(F32)
            moving = value
            for _ in range(self.count // RING - 1):
                pairs = [(i, (i + RING) % self.count) for i in range(self.count)]
                moving = lax.ppermute(moving, "dp", pairs)
                total = total + moving.astype(F32)
            low = total.astype(BF)
            if total.shape[0] == BLOCK + TAIL and self.count > RING:
                tail = two_halves(one_whole(total[BLOCK:]))
                low = jnp.concatenate([low[:BLOCK], tail], axis=0)
            result.append(low)
        return result


def part_sizes(chains):
    bounds = [chains * sum(PARTS[:p]) // sum(PARTS) for p in range(len(PARTS) + 1)]
    return [high - low for low, high in zip(bounds, bounds[1:])], bounds[:-1]


def shards(
    chain_inputs,
    cotangent,
    chain_tags,
    pad_mask,
    predicted,
    target_ids,
    joint_proj,
    output_proj,
    up_proj,
    up_bias,
    down_proj,
    norm_gain,
    norm_shift,
):
    section = lax.axis_index("section")
    core = lax.axis_index("tensor")
    tokens, half = chain_inputs.shape
    width = 2 * half
    all_chains = tokens // SEQ
    sizes, starts = part_sizes(all_chains)
    parts = range(len(sizes))
    ring = Ring()
    small = [ids.reshape(1, tokens) for ids in (pad_mask, predicted, target_ids)]
    joint = joint_proj[0].transpose(0, 2, 1, 3)
    output, up, bias, down = output_proj[0], up_proj[0], up_bias[0], down_proj[0]
    places = jnp.stack([section, core, ring.place]).astype(jnp.int32)
    marks, joint, output, own_rows = prepare(
        places, chain_tags, small[0], [joint, output, chain_inputs]
    )
    gains, shifts = norm_gain[0], norm_shift[0]
    units = up.shape[2]
    local = output.shape[1]
    heads = local // HEAD_DIM
    cot_other = swap(cotangent)
    rows_other = swap(chain_inputs)

    order = Order()

    kept = [{} for _ in parts]
    feed = [{} for _ in parts]
    attn = [{} for _ in parts]
    sent = [{} for _ in parts]
    sums = dict(
        feed=jnp.zeros((2, 1, width), F32),
        attn=jnp.zeros((2, 1, width), F32),
        bias=jnp.zeros((2, 1, units), F32),
    )

    def run(kernel, name, active, p, ins, outs, held, totals):
        outs = [(shape, dtype, kind, held.get(key)) for key, shape, dtype, kind in outs] + [
            (sums[key].shape, F32, "whole", sums[key]) for key in totals
        ]
        return order.run(run_chains, kernel, name, active, marks, sizes[p], ins, outs)

    def attn_forward(active, p, own, other, first):
        ins = [(own, "rows", first), (other, "rows", first)]
        ins += [(joint, "whole", 0), (output, "whole", 0)]
        outs = [
            ("rows", (width,), BF, "rows"),
            ("part", (width,), BF, "rows"),
            ("joined", (3 * local,), BF, "rows"),
            ("probs", (heads, SEQ, SEQ), BF, "chain"),
            ("mixed", (local,), BF, "rows"),
        ]
        kernel = functools.partial(attn_forward_kernel, starts[p], all_chains)
        found = run(kernel, "attn_forward", active, p, ins, outs, kept[p], [])
        kept[p].update(zip([o[0] for o in outs], found))
        kept[p]["part_other"] = swap(kept[p]["part"])

    def feed_forward(active, p):
        ins = [(kept[p][n], "rows", 0) for n in ("rows", "part", "part_other")]
        ins += [(a, "whole", 0) for a in (gains, shifts, up, bias, down)]
        outs = [
            ("down", (width,), BF, "rows"),
            ("normal", (width,), BF, "rows"),
            ("inv_root", (1,), F32, "rows"),
            ("low", (width,), BF, "rows"),
            ("hidden", (units,), BF, "rows"),
            ("slope", (units,), BF, "rows"),
        ]
        kernel = functools.partial(feed_forward_kernel, starts[p])
        found = run(kernel, "feed_forward", active, p, ins, outs, kept[p], [])
        kept[p].update(zip([o[0] for o in outs], found))
        kept[p]["down_other"] = swap(kept[p]["down"])

    def feed_back(active, p, own, other, first):
        ins = [(kept[p][n], "rows", 0) for n in ("normal", "down", "down_other")]
        ins += [(gains, "whole", 0), (shifts, "whole", 0)]
        ins += [(own, "rows", first), (other, "rows", first)]
        ins += [(kept[p]["slope"], "rows", 0)]
        ins += [(turned["up"], "whole", 0), (turned["down"], "whole", 0)]
        outs = [
            ("part", (width,), BF, "rows"),
            ("d_down", (width,), BF, "rows"),
            ("d_pre", (units,), BF, "rows"),
            ("outputs", (half,), BF, "rows"),
        ]
        kernel = functools.partial(feed_back_kernel, starts[p])
        *found, sums["feed"], sums["bias"] = run(
            kernel, "feed_back", active, p, ins, outs, feed[p], ["feed", "bias"]
        )
        feed[p].update(zip([o[0] for o in outs], found))
        feed[p]["part_other"] = swap(feed[p]["part"])

    def attn_back(active, p):
        ins = [(feed[p][n], "rows", 0) for n in ("d_down", "part", "part_other")]
        ins += [(kept[p]["normal"], "rows", 0), (kept[p]["inv_root"], "rows", 0)]
        ins += [(gains, "whole", 0), (kept[p]["joined"], "rows", 0), (kept[p]["probs"], "chain", 0)]
        ins += [(joint, "whole", 0), (output, "whole", 0)]
        outs = [
            ("mine", (half,), F32, "rows"),
            ("theirs", (half,), BF, "rows"),
            ("d_attn", (width,), BF, "rows"),
            ("d_joined", (3 * local,), BF, "rows"),
        ]
        kernel = functools.partial(attn_back_kernel, starts[p])
        *found, sums["attn"] = run(kernel, "attn_back", active, p, ins, outs, attn[p], ["attn"])
        attn[p].update(zip([o[0] for o in outs], found))

    def input_gradient(p, theirs):
        return attn[p]["mine"] + swap(theirs).astype(F32)

    def across(value):
        return lax.ppermute(value, "section", [(0, 1), (1, 0)])

    turned = {}

    def turn_weights(active):
        held = [turned[n] for n in ("up", "down") if n in turned]
        turned["up"], turned["down"] = order.run(turn, active, marks, [up, down], held)

    def attn_early(p):
        attn_forward(0, p, own_rows, rows_other, starts[p])

    def feed_early(p):
        feed_forward(0, p)

    def hand_on(p):
        ins = [(kept[p][n], "rows", 0) for n in ("normal", "down", "down_other")]
        ins += [(gains, "whole", 0), (shifts, "whole", 0)]
        outs = [("moved", (half,), BF, "rows")]
        found = run(last_norm_kernel, "last_norm", 0, p, ins, outs, {}, [])
        sent[p]["on"] = across(found[0])

    def receive(p):
        moved = order.after(sent[p]["on"])
        sent[p]["on"] = (moved, swap(moved))

    def attn_late(p):
        attn_forward(1, p, *sent[p]["on"], 0)

    def feed_late(p):
        feed_forward(1, p)

    def feed_first(p):
        feed_back(1, p, cotangent, cot_other, starts[p])

    def attn_first(p):
        attn_back(1, p)
        sent[p]["back"] = across(input_gradient(p, attn[p]["theirs"]).astype(BF))

    def receive_back(p):
        moved = order.after(sent[p]["back"])
        sent[p]["back"] = (moved, swap(moved))

    def feed_last(p):
        feed_back(0, p, *sent[p]["back"], 0)

    def attn_last(p):
        attn_back(0, p)

    for step, p in (
        (attn_early, 0),
        (attn_early, 1),
        (feed_early, 0),
        (hand_on, 0),
        (feed_early, 1),
        (attn_early, 2),
        (turn_weights, 1),
        (receive, 0),
        (attn_late, 0),
        (hand_on, 1),
        (feed_late, 0),
        (feed_early, 2),
        (feed_first, 0),
        (hand_on, 2),
        (receive, 1),
        (attn_first, 0),
        (attn_late, 1),
        (receive, 2),
        (turn_weights, 0),
        (feed_late, 1),
        (attn_late, 2),
        (feed_first, 1),
        (feed_late, 2),
        (receive_back, 0),
        (attn_first, 1),
        (feed_last, 0),
        (feed_first, 2),
        (receive_back, 1),
        (attn_first, 2),
        (feed_last, 1),
        (receive_back, 2),
        (feed_last, 2),
    ):
        step(p)
    feed_lists = [
        [kept[p]["hidden"] for p in parts],
        [feed[p]["d_down"] for p in parts],
        [kept[p]["low"] for p in parts],
        [feed[p]["d_pre"] for p in parts],
    ]

    def feed_weights(step, cost=3 * 10**9):
        return order.run(
            run_weights,
            feed_weights_kernel,
            "feed_weights",
            marks,
            step,
            feed_lists,
            [],
            2 * BLOCK,
            cost,
        )[0]

    def add_local(pair, local):
        return order.run(add_step, pair, local)

    shard = feed_weights(0)
    feed_pair = ring.send((shard[0], shard[1]))
    shard = feed_weights(1)
    for p in parts:
        attn_last(p)
    feed_pair = ring.send(add_local(feed_pair, shard))
    attn_lists = [
        [kept[p]["rows"] for p in parts],
        [attn[p]["d_joined"] for p in parts],
        [kept[p]["mixed"] for p in parts],
        [attn[p]["d_attn"] for p in parts],
    ]

    small = [sums["bias"], sums["attn"], sums["feed"], *small]

    def attn_weights(step, cost=3 * 10**9):
        return order.run(
            run_weights,
            attn_weights_kernel,
            "attn_weights",
            marks,
            step,
            attn_lists,
            small,
            BLOCK + TAIL,
            cost,
        )[0]

    shard = attn_weights(0, 10**9)
    attn_pair = ring.send((shard[0], shard[1]))
    attn_local = attn_weights(1, 10**9)
    feed_local = feed_weights(2, 10**9)
    streams = [
        dict(
            pair=attn_pair,
            local=attn_local,
            weights=attn_weights,
            sent=1,
            kernel=attn_place_kernel,
            name="attn_place",
            held=unwritten((2, 3, width, local), (2, local, width), (2, RING, 8, BLOCK)),
        ),
        dict(
            pair=feed_pair,
            local=feed_local,
            weights=feed_weights,
            sent=2,
            kernel=feed_place_kernel,
            name="feed_place",
            held=unwritten((2, units, width), (2, width, units)),
        ),
    ]

    def advance(stream):
        sent = stream["sent"]
        *pair, token = lax.optimization_barrier((*stream["pair"], *order.tokens))
        order.tokens = (token,)
        if sent < RING:
            pair = add_local(pair, stream["local"])
            if sent == RING - 1:
                pair = ring.across(pair)
        stream["pair"] = ring.send(pair) if sent < 2 * RING - 2 else None
        if sent < RING - 1:
            stream["local"] = stream["weights"](sent + 1)
        else:
            stream["held"] = order.run(
                place_step,
                stream["kernel"],
                stream["name"],
                marks,
                sent - RING + 1,
                pair,
                stream["held"],
            )
        stream["sent"] += 1

    attn_stream, feed_stream = streams
    input_grads = []
    while attn_stream["pair"] is not None or feed_stream["pair"] is not None:
        if attn_stream["sent"] == 2 * RING - 2:
            input_grads = [input_gradient(p, order.after(attn[p]["theirs"])) for p in parts]
        if feed_stream["pair"] is not None:
            advance(feed_stream)
        if attn_stream["pair"] is not None:
            advance(attn_stream)
    joint_out, output_out, small_out = attn_stream["held"]
    down_out, up_out = feed_stream["held"]

    def whole(pieces):
        return jnp.concatenate(pieces, axis=0)

    input_grads = whole(input_grads)
    rows = small_out[:, :, 0]
    bias_grad = rows[:, :4].reshape(2, units)
    norm_sums = rows[:, 4:].reshape(2, 2, width)
    counts = small_out[0, 0, 1].reshape(3, 128)[:2, :SYMBOLS]
    return (
        whole([feed[p]["outputs"] for p in parts])[None],
        input_grads[None],
        joint_out.transpose(0, 2, 1, 3)[None],
        output_out[None],
        up_out[None],
        bias_grad[None],
        down_out[None],
        norm_sums[:, 0][None],
        norm_sums[:, 1][None],
        counts.astype(jnp.int32),
    )


def solution(mesh):
    return jax.shard_map(
        shards,
        mesh=mesh,
        in_specs=(
            P("dp", "tensor"),
            P("dp", "tensor"),
            P("dp"),
            P("dp"),
            P("dp"),
            P("dp"),
            P("section", None, None, None, "tensor"),
            P("section", None, "tensor", None),
            P("section", None, None, "tensor"),
            P("section", None, "tensor"),
            P("section", None, "tensor", None),
            P("section", None, None),
            P("section", None, None),
        ),
        out_specs=(
            P("section", "dp", "tensor"),
            P("section", "dp", "tensor"),
            P("section", None, None, None, "tensor"),
            P("section", None, "tensor", None),
            P("section", None, None, "tensor"),
            P("section", None, "tensor"),
            P("section", None, "tensor", None),
            P("section", None, None),
            P("section", None, None),
            P(),
        ),
        check_vma=False,
    )
```

```python
import functools

import jax
import jax.numpy as jnp
from jax import lax
from jax.experimental import pallas as pl
from jax.experimental.pallas import tpu as pltpu
from jax.sharding import PartitionSpec as P

HEAD_DIM = 64
SYMBOLS = 24
SEQ = 160
PARTS = (2, 2, 2)
RING = 8
BLOCK = 384
TAIL = 16
EPS = 1e-05
SCALE = HEAD_DIM**-0.5
VMEM_LIMIT = 7 * 1024 * 1024
CHAIN_LIMIT = 7 * 1024 * 1024

root_half = 0.7071067811865476
root_two_pi = 0.3989422804014327
BF = jnp.bfloat16
F32 = jnp.float32


def swap(value):
    return lax.ppermute(value, "tensor", [(0, 1), (1, 0)])


def dot(a, b):
    return jnp.dot(a, b, preferred_element_type=F32)


def dot_rows(a, b):
    return lax.dot_general(a, b, (((1,), (1,)), ((), ())), preferred_element_type=F32)


def dot_cols(a, b):
    return lax.dot_general(a, b, (((0,), (0,)), ((), ())), preferred_element_type=F32)


def in_order(core, own, other):
    first = core == 0
    return jnp.concatenate(
        [jnp.where(first, own, other), jnp.where(first, other, own)], axis=1
    )


def own_part(core, value):
    half = value.shape[1] // 2
    return jnp.where(core == 0, value[:, :half], value[:, half:])


def normalise(rows):
    centred = rows - jnp.mean(rows, axis=-1, keepdims=True)
    inv_root = lax.rsqrt(jnp.mean(centred * centred, axis=-1, keepdims=True) + EPS)
    return centred * inv_root, inv_root


def norm_back(grads, normal, inv_root, gain):
    scaled = grads * gain
    inner = (
        scaled
        - jnp.mean(scaled, axis=-1, keepdims=True)
        - normal * jnp.mean(scaled * normal, axis=-1, keepdims=True)
    )
    return inner * inv_root


def pair_spans(width):
    return [slice(at, at + 2 * HEAD_DIM) for at in range(0, width, 2 * HEAD_DIM)]


def left_head():
    return lax.broadcasted_iota(jnp.int32, (1, 2 * HEAD_DIM), 1) < HEAD_DIM


def pair_scores(first, second):
    left = left_head().astype(BF)
    both = jnp.concatenate([first * left, first * (1 - left)], axis=0)
    return dot_rows(both, second).reshape(2, SEQ, SEQ)


def pair_product(matrices, block):
    found = dot(matrices.reshape(2 * SEQ, SEQ), block)
    return jnp.where(left_head(), found[:SEQ], found[SEQ:]).astype(BF)


def pair_turned(matrices):
    return jnp.concatenate([matrices[0].T, matrices[1].T], axis=0)


def attn_forward_kernel(start, count, chain, marks, own, other, joint, output, *refs):
    tag = marks[3 + start + chain]
    core = marks[1]
    a, b = own[...], other[...]
    rows = in_order(core, a, b)
    q, k, v = [dot(rows, joint[tag, j]).astype(BF) for j in range(3)]
    key_live = lax.broadcasted_iota(jnp.int32, (1, SEQ, 1), 1) < marks[3 + count + start + chain]
    spans = pair_spans(q.shape[1])
    scores = [pair_scores(k[:, s], q[:, s] * jnp.asarray(SCALE, BF)) for s in spans]
    probs = []
    for found in scores:
        found = jnp.where(key_live, found, -1000000000.0)
        shifted = jnp.exp(found - jnp.max(found, axis=1, keepdims=True))
        probs.append((shifted * (1.0 / jnp.sum(shifted, axis=1, keepdims=True))).astype(BF))
    mixed = jnp.concatenate(
        [pair_product(pair_turned(p), v[:, s]) for p, s in zip(probs, spans)], axis=1
    )
    refs[0][...] = rows
    refs[1][...] = dot(mixed, output[tag]).astype(BF)
    refs[2][...] = jnp.concatenate([q, k, v], axis=1)
    for at, found in enumerate(probs):
        refs[3][0, 2 * at : 2 * at + 2] = found
    refs[4][...] = mixed


def feed_forward_kernel(start, chain, marks, rows, part, other, gains, shifts, up, bias, down, *outs):
    tag = marks[3 + start + chain]
    total = rows[...].astype(F32) + (part[...].astype(F32) + other[...].astype(F32))
    normal, inv_root = normalise(total)
    low = (normal * gains[0:1] + shifts[0:1]).astype(BF)
    pre = dot(low, up[tag]) + jnp.where(tag == 0, bias[0:1], bias[1:2]).astype(F32)
    cdf = 0.5 * (1.0 + lax.erf(pre * root_half))
    hidden = (pre * cdf).astype(BF)
    outs[0][...] = dot(hidden, down[tag]).astype(BF)
    outs[1][...] = normal.astype(BF)
    outs[2][...] = inv_root
    outs[3][...] = low
    outs[4][...] = hidden
    outs[5][...] = (cdf + pre * jnp.exp(-0.5 * pre * pre) * root_two_pi).astype(BF)


def second_norm(normal, part, other, gains, shifts):
    first = normal[...].astype(F32) * gains[0:1] + shifts[0:1]
    return normalise(first + (part[...].astype(F32) + other[...].astype(F32)))


def last_norm_kernel(chain, marks, normal, part, other, gains, shifts, out):
    second, _ = second_norm(normal, part, other, gains, shifts)
    out[...] = own_part(marks[1], (second * gains[1:2] + shifts[1:2]).astype(BF))


def add_sums(grads, normal, sums):
    sums[0] += jnp.sum(grads * normal, axis=0, keepdims=True)
    sums[1] += jnp.sum(grads, axis=0, keepdims=True)


def feed_back_kernel(
    start, chain, marks, normal, part, other, gains, shifts, own, partner, slope, up, down, *outs
):
    tag = marks[3 + start + chain]
    core = marks[1]
    a, b = own[...], partner[...]
    grads = in_order(core, a, b).astype(F32)
    second, inv_root = second_norm(normal, part, other, gains, shifts)
    back = norm_back(grads, second, inv_root, gains[1:2])
    low = back.astype(BF)
    d_pre = (dot(low, down[tag]) * slope[...].astype(F32)).astype(BF)
    outs[0][...] = dot(d_pre, up[tag]).astype(BF)
    outs[1][...] = low
    outs[2][...] = d_pre
    outs[3][...] = own_part(core, (second * gains[1:2] + shifts[1:2]).astype(BF))
    add_sums(grads, second, outs[4])
    outs[5][tag] += jnp.sum(d_pre.astype(F32), axis=0, keepdims=True)


def attn_back_kernel(
    start, chain, marks, back, part, other, normal, inv_root, gains, joined, probs, joint, output, *outs
):
    tag = marks[3 + start + chain]
    core = marks[1]
    grads = back[...].astype(F32) + (part[...].astype(F32) + other[...].astype(F32))
    normal = normal[...].astype(F32)
    back_one = norm_back(grads, normal, inv_root[...], gains[0:1])
    low = back_one.astype(BF)
    d_mixed = dot_rows(low, output[tag]).astype(BF)
    width = d_mixed.shape[1]
    q, k, v = [joined[:, j * width : (j + 1) * width] for j in range(3)]
    spans = pair_spans(width)
    d_probs = [pair_scores(v[:, s], d_mixed[:, s]) for s in spans]
    held = [probs[0, 2 * at : 2 * at + 2] for at in range(len(spans))]
    d_scores = []
    for found, kept in zip(d_probs, held):
        wide = kept.astype(F32)
        inner = jnp.sum(wide * found, axis=1, keepdims=True)
        d_scores.append((wide * (found - inner)).astype(BF))
    scale = jnp.asarray(SCALE, BF)
    d_k = [pair_product(d, q[:, s]) * scale for d, s in zip(d_scores, spans)]
    d_v = [pair_product(h, d_mixed[:, s]) for h, s in zip(held, spans)]
    d_q = [pair_product(pair_turned(d), k[:, s]) * scale for d, s in zip(d_scores, spans)]
    pieces = [d_q, d_k, d_v]
    blocks = [jnp.concatenate(p, axis=1) for p in pieces]
    d_rows = sum(dot_rows(blocks[j], joint[tag, j]) for j in range(3)).astype(BF)
    outs[0][...] = own_part(core, back_one) + own_part(core, d_rows).astype(F32)
    outs[1][...] = own_part(1 - core, d_rows)
    outs[2][...] = low
    outs[3][...] = jnp.concatenate(blocks, axis=1)
    add_sums(grads, normal, outs[4])


class Marks:
    def __init__(self, ref):
        self.rows = ref[...]

    def __getitem__(self, at):
        return self.rows[0, at]


def behind(kernel, taken, ignored):
    def call(marks, *refs):
        kernel(Marks(marks), *refs[:taken], *refs[taken + ignored :])

    return call


ANY = pl.BlockSpec(memory_space=pl.ANY)
HBM = pl.BlockSpec(memory_space=pltpu.HBM)
TOKEN = jax.ShapeDtypeStruct((8, 128), F32)


def sign_off(token):
    token[...] = jnp.zeros_like(token)


class Order:
    def __init__(self):
        self.tokens = ()

    def run(self, call, *args):
        *results, token = call(*args, self.tokens)
        self.tokens = (token,)
        return results

    def wait(self, value):
        self.tokens = tuple(lax.optimization_barrier((*self.tokens, value))[:-1])

    def after(self, value):
        return lax.optimization_barrier((value, *self.tokens))[0]


VMEM = pl.BlockSpec(memory_space=pltpu.VMEM)
SMEM = pl.BlockSpec(memory_space=pltpu.SMEM)


def chain_view(ref, kind, at):
    if kind == "rows":
        return ref.at[at * SEQ : (at + 1) * SEQ]
    return ref.at[at : at + 1] if kind == "chain" else ref


def prepare_kernel(chains, count, places, *refs):
    sources, marks, held = refs[:count], refs[count], refs[count + 1 : 2 * count - 1]
    tags, live, sems = refs[2 * count - 1 :]
    copies = [
        pltpu.make_async_copy(source, target, sems.at[at])
        for at, (source, target) in enumerate(zip(sources, (tags, live) + held))
    ]
    for copy in copies:
        copy.start()
    for copy in copies[:2]:
        copy.wait()
    token = lax.broadcasted_iota(jnp.int32, live.shape, 1)
    found = [places[at] for at in range(3)]
    found += [jnp.where(tags[chain] > 0, 1, 0) for chain in range(chains)]
    for chain in range(chains):
        inside = (token >= chain * SEQ) & (token < (chain + 1) * SEQ)
        found.append(jnp.sum(jnp.where(inside, live[...], 0)))
    lane = lax.broadcasted_iota(jnp.int32, marks.shape, 1)
    rows = jnp.zeros(marks.shape, jnp.int32)
    for at, value in enumerate(found):
        rows = jnp.where(lane == at, value, rows)
    marks[...] = rows
    for copy in copies[2:]:
        copy.wait()


def prepare(places, tags, live, arrays):
    chains = tags.shape[0]
    sources = [tags, live, *arrays]
    count = len(sources)
    return pl.pallas_call(
        functools.partial(prepare_kernel, chains, count),
        in_specs=[SMEM] + [HBM] * count,
        out_specs=[VMEM] * (1 + len(arrays)),
        out_shape=[jax.ShapeDtypeStruct((8, 128), jnp.int32)]
        + [jax.ShapeDtypeStruct(a.shape, a.dtype) for a in arrays],
        scratch_shapes=[
            pltpu.SMEM(tags.shape, jnp.int32),
            pltpu.VMEM(live.shape, jnp.int32),
            pltpu.SemaphoreType.DMA((count,)),
        ],
        compiler_params=pltpu.CompilerParams(vmem_limit_bytes=1024 * 1024),
        name="prepare",
    )(places, *[pltpu.with_memory_space_constraint(a, pltpu.HBM) for a in sources])


def turn(active, marks, arrays, held, after):
    count = len(arrays)
    skipped = count + len(held) + len(after)

    def call(marks, *refs):
        marks = Marks(marks)
        sign_off(refs[-1])

        @pl.when(marks[0] == active)
        def _():
            for source, target in zip(refs[:count], refs[skipped:]):
                for at in range(source.shape[0]):
                    target[at] = source[at].T

    return pl.pallas_call(
        call,
        in_specs=[VMEM] * (1 + count + len(held)) + [ANY] * len(after),
        out_specs=[VMEM] * (count + 1),
        out_shape=[jax.ShapeDtypeStruct((a.shape[0], a.shape[2], a.shape[1]), BF) for a in arrays]
        + [TOKEN],
        input_output_aliases={1 + count + at: at for at in range(len(held))},
        compiler_params=pltpu.CompilerParams(vmem_limit_bytes=VMEM_LIMIT),
        cost_estimate=pl.CostEstimate(flops=10**10, bytes_accessed=10**7, transcendentals=0),
        name="turn",
    )(marks, *arrays, *held, *after)


def run_chains(kernel, name, active, marks, chains, ins, outs, after):
    shapes, held, aliases = [], [], {}
    for trailing, dtype, kind, array in outs:
        lead = {"rows": (chains * SEQ,), "chain": (chains,), "whole": ()}[kind]
        if array is not None:
            aliases[1 + len(ins) + len(held)] = len(shapes)
            held.append(array)
        shapes.append(jax.ShapeDtypeStruct(lead + trailing, dtype))
    kinds = [(kind, first) for _, kind, first in ins] + [(kind, 0) for _, _, kind, _ in outs]
    skipped = len(ins) + len(held) + len(after)

    def call(marks, *refs):
        marks = Marks(marks)
        *refs, token = refs[: len(ins)] + refs[skipped:]
        sign_off(token)

        @pl.when(marks[0] == active)
        def _():
            for chain in range(chains):
                views = [chain_view(r, kind, first + chain) for r, (kind, first) in zip(refs, kinds)]
                kernel(chain, marks, *views)

    return pl.pallas_call(
        call,
        in_specs=[VMEM] * (1 + len(ins) + len(held)) + [ANY] * len(after),
        out_specs=[VMEM] * (len(outs) + 1),
        out_shape=shapes + [TOKEN],
        input_output_aliases=aliases,
        compiler_params=pltpu.CompilerParams(vmem_limit_bytes=CHAIN_LIMIT),
        cost_estimate=pl.CostEstimate(flops=10**10, bytes_accessed=10**7, transcendentals=0),
        name=name,
    )(marks, *[a for a, _, _ in ins], *held, *after)


def ring_spot(marks, step, way):
    return lax.rem(marks[2] + 2 * RING + way * step, RING)


def span(at):
    return pl.ds(pl.multiple_of(at * BLOCK, BLOCK), BLOCK)


def cut(ref, at):
    return ref[:, span(at)]


def set_rows(marks, block, which):
    pieces = []
    for chain in range(block.shape[0] // SEQ):
        piece = block[chain * SEQ : (chain + 1) * SEQ]
        pieces.append(jnp.where(marks[3 + chain] == which, piece, jnp.zeros_like(piece)))
    return jnp.concatenate(pieces, axis=0)


def all_rows(refs, at):
    return jnp.concatenate([cut(ref, at) for ref in refs], axis=0)


def feed_shard(marks, which, hidden, d_down, low, d_pre):
    return (
        dot_cols(set_rows(marks, hidden, which), d_down).astype(BF),
        dot_cols(set_rows(marks, low, which), d_pre).astype(BF),
    )


def feed_weights_kernel(step, parts, marks, *refs):
    hidden, d_down, low, d_pre = [refs[n * parts : (n + 1) * parts] for n in range(4)]
    out, token = refs[4 * parts :]
    sign_off(token)
    for which, way in ((0, -1), (1, 1)):
        spot = ring_spot(marks, step, way)
        far, near = lax.div(spot, 2), lax.rem(spot, 2)
        out[which, :BLOCK], out[which, BLOCK:] = feed_shard(
            marks,
            which,
            all_rows(hidden, far),
            all_rows(d_down, near),
            all_rows(low, near),
            all_rows(d_pre, far),
        )


def two_halves(value):
    high = value.astype(BF).astype(F32)
    return jnp.concatenate([high, value - high], axis=0).astype(BF)


def one_whole(rows):
    rows = rows.astype(F32)
    return rows[: TAIL // 2] + rows[TAIL // 2 :]


def count_rows(live, predicted, targets):
    symbols = lax.broadcasted_iota(jnp.int32, (128, live.shape[1]), 0)
    hits = (targets[...] == symbols) & (live[...] > 0)
    right = hits & (predicted[...] == targets[...])
    ones = jnp.ones((8, live.shape[1]), BF)
    found = [dot_rows(ones, h.astype(F32).astype(BF)) for h in (hits, right)]
    return jnp.concatenate(found + [jnp.zeros_like(found[0])], axis=1)[0:1]


def attn_weights_kernel(step, parts, marks, *refs):
    rows, d_joined, mixed, d_attn = [refs[n * parts : (n + 1) * parts] for n in range(4)]
    bias, *sums, live, predicted, targets, out, token = refs[4 * parts :]
    sign_off(token)
    for which, way in ((0, -1), (1, 1)):
        spot = ring_spot(marks, step, way)
        far, near = lax.div(spot, 2), lax.rem(spot, 2)

        @pl.when(far < 3)
        def _():
            out[which, :BLOCK] = dot_cols(
                set_rows(marks, all_rows(rows, near), which), all_rows(d_joined, far)
            ).astype(BF)

        @pl.when(far == 3)
        def _():
            out[which, :BLOCK] = dot_cols(
                set_rows(marks, all_rows(mixed, 0), which), all_rows(d_attn, near)
            ).astype(BF)

        early = far < 2
        small = jnp.where(
            early,
            bias[which, :, span(jnp.where(early, spot, 0))],
            sums[which][jnp.where(early, 0, far - 2), :, span(near)],
        )
        place = lax.broadcasted_iota(jnp.int32, (TAIL // 2, BLOCK), 0)
        small = jnp.where(place == 0, small, 0.0)
        out[which, BLOCK:] = two_halves(small)
        if which == 0:

            @pl.when(spot == 0)
            def _():
                counts = count_rows(live, predicted, targets)
                out[which, BLOCK:] = two_halves(jnp.where(place == 1, counts, small))


def run_weights(kernel, name, marks, step, lists, rest, rows_out, cost, after):
    ins = [a for arrays in lists for a in arrays] + list(rest)
    return pl.pallas_call(
        behind(functools.partial(kernel, step + 1, len(lists[0])), len(ins), len(after)),
        in_specs=[VMEM] * (1 + len(ins)) + [ANY] * len(after),
        out_specs=[VMEM, VMEM],
        out_shape=[jax.ShapeDtypeStruct((2, rows_out, BLOCK), BF), TOKEN],
        compiler_params=pltpu.CompilerParams(vmem_limit_bytes=VMEM_LIMIT),
        cost_estimate=pl.CostEstimate(flops=cost, bytes_accessed=10**6, transcendentals=0),
        name=name,
    )(marks, *ins, *after)


def add_kernel(tail, ahead, back, local, out_ahead, out_back, token):
    sign_off(token)
    for which, (ref, out) in enumerate(((ahead, out_ahead), (back, out_back))):
        total = ref[...].astype(F32) + local[which].astype(F32)
        out[...] = total.astype(BF)
        if tail:
            out[tail:] = two_halves(one_whole(total[tail:]))


def add_step(pair, local, after):
    shape = local.shape[1:]
    tail = BLOCK if shape[0] == BLOCK + TAIL else 0

    def call(*refs):
        add_kernel(tail, *refs[:3], *refs[3 + len(after) :])

    return pl.pallas_call(
        call,
        in_specs=[VMEM] * 3 + [ANY] * len(after),
        out_specs=[VMEM] * 3,
        out_shape=[jax.ShapeDtypeStruct(shape, BF)] * 2 + [TOKEN],
        compiler_params=pltpu.CompilerParams(vmem_limit_bytes=VMEM_LIMIT),
        cost_estimate=pl.CostEstimate(flops=3*10**9, bytes_accessed=10**6, transcendentals=0),
        name="ring_add",
    )(*pair, local, *after)


def feed_place_kernel(steps, marks, pairs, outs, wide, sems):
    down, up = outs
    copies = []
    for at, (step, pair) in enumerate(zip(steps, pairs)):
        for which, (ref, way) in enumerate(zip(pair, (-1, 1))):
            spot = ring_spot(marks, step, way)
            far, near = lax.div(spot, 2), lax.rem(spot, 2)
            slot = 2 * at + which
            wide[slot] = ref[...].astype(F32)
            copies += [
                pltpu.make_async_copy(
                    wide.at[slot, :BLOCK], down.at[which, span(far), span(near)], sems.at[2 * slot]
                ),
                pltpu.make_async_copy(
                    wide.at[slot, BLOCK:], up.at[which, span(near), span(far)], sems.at[2 * slot + 1]
                ),
            ]
            for copy in copies[-2:]:
                copy.start()
    for copy in copies:
        copy.wait()


def attn_place_kernel(steps, marks, pairs, outs, wide, sems):
    joint, output, small = outs
    waits = []
    for at, (step, pair) in enumerate(zip(steps, pairs)):
        for which, (ref, way) in enumerate(zip(pair, (-1, 1))):
            spot = ring_spot(marks, step, way)
            far, near = lax.div(spot, 2), lax.rem(spot, 2)
            slot = 2 * at + which
            wide[slot] = ref[...].astype(F32)
            wide[slot, BLOCK : BLOCK + TAIL // 2] = one_whole(ref[BLOCK:])
            tail = pltpu.make_async_copy(
                wide.at[slot, BLOCK : BLOCK + TAIL // 2],
                small.at[which, spot],
                sems.at[2 * slot + 1],
            )
            to_joint = pltpu.make_async_copy(
                wide.at[slot, :BLOCK],
                joint.at[which, jnp.minimum(far, 2), span(near)],
                sems.at[2 * slot],
            )
            to_output = pltpu.make_async_copy(
                wide.at[slot, :BLOCK], output.at[which, :, span(near)], sems.at[2 * slot]
            )
            tail.start()
            pl.when(far < 3)(to_joint.start)
            pl.when(far == 3)(to_output.start)
            waits.append((far, tail, to_joint, to_output))
    for far, tail, to_joint, to_output in waits:
        tail.wait()
        pl.when(far < 3)(to_joint.wait)
        pl.when(far == 3)(to_output.wait)


def place_step(kernel, name, marks, steps, pairs, held, after):
    shape = pairs[0][0].shape
    count = len(held)
    given = 2 * len(pairs)

    def call(marks, *refs):
        taken = [refs[at : at + 2] for at in range(0, given, 2)]
        refs = refs[given + count + len(after) :]
        sign_off(refs[count])
        kernel(steps, Marks(marks), taken, refs[:count], *refs[count + 1 :])

    return pl.pallas_call(
        call,
        in_specs=[VMEM] * (1 + given) + [HBM] * count + [ANY] * len(after),
        out_specs=[HBM] * count + [VMEM],
        scratch_shapes=[
            pltpu.VMEM((given,) + shape, F32),
            pltpu.SemaphoreType.DMA((2 * given,)),
        ],
        out_shape=[jax.ShapeDtypeStruct(h.shape, h.dtype) for h in held] + [TOKEN],
        input_output_aliases={1 + given + i: i for i in range(count)},
        compiler_params=pltpu.CompilerParams(vmem_limit_bytes=VMEM_LIMIT),
        cost_estimate=pl.CostEstimate(flops=10**10, bytes_accessed=10**6, transcendentals=0),
        name=name,
    )(marks, *[value for pair in pairs for value in pair], *held, *after)


def finish(mine, theirs, outputs, after):
    count = len(mine)
    rows, half = sum(a.shape[0] for a in mine), mine[0].shape[1]

    def call(*refs):
        grads, whole, token = refs[3 * count + len(after) :]
        sign_off(token)
        at = 0
        for own, other, output in zip(refs, refs[count:], refs[2 * count : 3 * count]):
            here = slice(at, at + own.shape[0])
            grads[here] = own[...] + other[...].astype(F32)
            whole[here] = output[...]
            at += own.shape[0]

    return pl.pallas_call(
        call,
        in_specs=[VMEM] * (3 * count) + [ANY] * len(after),
        out_specs=[VMEM] * 3,
        out_shape=[
            jax.ShapeDtypeStruct((rows, half), F32),
            jax.ShapeDtypeStruct((rows, half), BF),
            TOKEN,
        ],
        compiler_params=pltpu.CompilerParams(vmem_limit_bytes=VMEM_LIMIT),
        cost_estimate=pl.CostEstimate(flops=10**10, bytes_accessed=10**6, transcendentals=0),
        name="finish",
    )(*mine, *theirs, *outputs, *after)


def unwritten(*shapes):
    return pl.pallas_call(
        lambda *refs: None,
        out_specs=[HBM] * len(shapes),
        out_shape=[jax.ShapeDtypeStruct(s, F32) for s in shapes],
        compiler_params=pltpu.CompilerParams(vmem_limit_bytes=1024 * 1024),
        name="unwritten",
    )()


class Ring:
    def __init__(self):
        self.count = lax.axis_size("dp")
        assert self.count % RING == 0
        order = list(range(0, RING, 2)) + list(range(1, RING, 2))[::-1]
        rank = lax.rem(lax.axis_index("dp"), RING)
        self.place = jnp.zeros((), jnp.int32)
        for at, member in enumerate(order):
            self.place = jnp.where(rank == member, at, self.place)
        self.ahead = [
            (base + order[i], base + order[(i + 1) % RING])
            for base in range(0, self.count, RING)
            for i in range(RING)
        ]
        self.back = [(b, a) for a, b in self.ahead]

    def send(self, pair):
        return lax.ppermute(pair[0], "dp", self.ahead), lax.ppermute(pair[1], "dp", self.back)

    def across(self, pair):
        result = []
        for value in pair:
            total = value.astype(F32)
            moving = value
            for _ in range(self.count // RING - 1):
                pairs = [(i, (i + RING) % self.count) for i in range(self.count)]
                moving = lax.ppermute(moving, "dp", pairs)
                total = total + moving.astype(F32)
            low = total.astype(BF)
            if total.shape[0] == BLOCK + TAIL and self.count > RING:
                tail = two_halves(one_whole(total[BLOCK:]))
                low = jnp.concatenate([low[:BLOCK], tail], axis=0)
            result.append(low)
        return result


def part_sizes(chains):
    bounds = [chains * sum(PARTS[:p]) // sum(PARTS) for p in range(len(PARTS) + 1)]
    return [high - low for low, high in zip(bounds, bounds[1:])], bounds[:-1]


def shards(
    chain_inputs,
    cotangent,
    chain_tags,
    pad_mask,
    predicted,
    target_ids,
    joint_proj,
    output_proj,
    up_proj,
    up_bias,
    down_proj,
    norm_gain,
    norm_shift,
):
    section = lax.axis_index("section")
    core = lax.axis_index("tensor")
    tokens, half = chain_inputs.shape
    width = 2 * half
    all_chains = tokens // SEQ
    sizes, starts = part_sizes(all_chains)
    parts = range(len(sizes))
    ring = Ring()
    small = [ids.reshape(1, tokens) for ids in (pad_mask, predicted, target_ids)]
    joint = joint_proj[0].transpose(0, 2, 1, 3)
    output, up, bias, down = output_proj[0], up_proj[0], up_bias[0], down_proj[0]
    places = jnp.stack([section, core, ring.place]).astype(jnp.int32)
    marks, joint, output, own_rows = prepare(
        places, chain_tags, small[0], [joint, output, chain_inputs]
    )
    gains, shifts = norm_gain[0], norm_shift[0]
    units = up.shape[2]
    local = output.shape[1]
    heads = local // HEAD_DIM
    cot_other = swap(cotangent)
    rows_other = swap(chain_inputs)

    order = Order()

    kept = [{} for _ in parts]
    feed = [{} for _ in parts]
    attn = [{} for _ in parts]
    sent = [{} for _ in parts]
    sums = dict(
        feed=jnp.zeros((2, 1, width), F32),
        attn=jnp.zeros((2, 1, width), F32),
        bias=jnp.zeros((2, 1, units), F32),
    )

    def run(kernel, name, active, p, ins, outs, held, totals):
        outs = [(shape, dtype, kind, held.get(key)) for key, shape, dtype, kind in outs] + [
            (sums[key].shape, F32, "whole", sums[key]) for key in totals
        ]
        return order.run(run_chains, kernel, name, active, marks, sizes[p], ins, outs)

    def attn_forward(active, p, own, other, first):
        ins = [(own, "rows", first), (other, "rows", first)]
        ins += [(joint, "whole", 0), (output, "whole", 0)]
        outs = [
            ("rows", (width,), BF, "rows"),
            ("part", (width,), BF, "rows"),
            ("joined", (3 * local,), BF, "rows"),
            ("probs", (heads, SEQ, SEQ), BF, "chain"),
            ("mixed", (local,), BF, "rows"),
        ]
        kernel = functools.partial(attn_forward_kernel, starts[p], all_chains)
        found = run(kernel, "attn_forward", active, p, ins, outs, kept[p], [])
        kept[p].update(zip([o[0] for o in outs], found))
        kept[p]["part_other"] = swap(kept[p]["part"])

    def feed_forward(active, p):
        ins = [(kept[p][n], "rows", 0) for n in ("rows", "part", "part_other")]
        ins += [(a, "whole", 0) for a in (gains, shifts, up, bias, down)]
        outs = [
            ("down", (width,), BF, "rows"),
            ("normal", (width,), BF, "rows"),
            ("inv_root", (1,), F32, "rows"),
            ("low", (width,), BF, "rows"),
            ("hidden", (units,), BF, "rows"),
            ("slope", (units,), BF, "rows"),
        ]
        kernel = functools.partial(feed_forward_kernel, starts[p])
        found = run(kernel, "feed_forward", active, p, ins, outs, kept[p], [])
        kept[p].update(zip([o[0] for o in outs], found))
        kept[p]["down_other"] = swap(kept[p]["down"])

    def feed_back(active, p, own, other, first):
        ins = [(kept[p][n], "rows", 0) for n in ("normal", "down", "down_other")]
        ins += [(gains, "whole", 0), (shifts, "whole", 0)]
        ins += [(own, "rows", first), (other, "rows", first)]
        ins += [(kept[p]["slope"], "rows", 0)]
        ins += [(turned["up"], "whole", 0), (turned["down"], "whole", 0)]
        outs = [
            ("part", (width,), BF, "rows"),
            ("d_down", (width,), BF, "rows"),
            ("d_pre", (units,), BF, "rows"),
            ("outputs", (half,), BF, "rows"),
        ]
        kernel = functools.partial(feed_back_kernel, starts[p])
        *found, sums["feed"], sums["bias"] = run(
            kernel, "feed_back", active, p, ins, outs, feed[p], ["feed", "bias"]
        )
        feed[p].update(zip([o[0] for o in outs], found))
        feed[p]["part_other"] = swap(feed[p]["part"])

    def attn_back(active, p):
        ins = [(feed[p][n], "rows", 0) for n in ("d_down", "part", "part_other")]
        ins += [(kept[p]["normal"], "rows", 0), (kept[p]["inv_root"], "rows", 0)]
        ins += [(gains, "whole", 0), (kept[p]["joined"], "rows", 0), (kept[p]["probs"], "chain", 0)]
        ins += [(joint, "whole", 0), (output, "whole", 0)]
        outs = [
            ("mine", (half,), F32, "rows"),
            ("theirs", (half,), BF, "rows"),
            ("d_attn", (width,), BF, "rows"),
            ("d_joined", (3 * local,), BF, "rows"),
        ]
        kernel = functools.partial(attn_back_kernel, starts[p])
        *found, sums["attn"] = run(kernel, "attn_back", active, p, ins, outs, attn[p], ["attn"])
        attn[p].update(zip([o[0] for o in outs], found))

    def across(value):
        return lax.ppermute(value, "section", [(0, 1), (1, 0)])

    turned = {}

    def turn_weights(active):
        held = [turned[n] for n in ("up", "down") if n in turned]
        turned["up"], turned["down"] = order.run(turn, active, marks, [up, down], held)

    def attn_early(p):
        attn_forward(0, p, own_rows, rows_other, starts[p])

    def feed_early(p):
        feed_forward(0, p)

    def hand_on(p):
        ins = [(kept[p][n], "rows", 0) for n in ("normal", "down", "down_other")]
        ins += [(gains, "whole", 0), (shifts, "whole", 0)]
        outs = [("moved", (half,), BF, "rows")]
        found = run(last_norm_kernel, "last_norm", 0, p, ins, outs, {}, [])
        sent[p]["on"] = across(found[0])

    def receive(p):
        moved = order.after(sent[p]["on"])
        sent[p]["on"] = (moved, swap(moved))

    def attn_late(p):
        attn_forward(1, p, *sent[p]["on"], 0)

    def feed_late(p):
        feed_forward(1, p)

    def feed_first(p):
        feed_back(1, p, cotangent, cot_other, starts[p])

    def attn_first(p):
        attn_back(1, p)
        total = attn[p]["mine"] + swap(attn[p]["theirs"]).astype(F32)
        sent[p]["back"] = across(total.astype(BF))

    def receive_back(p):
        moved = order.after(sent[p]["back"])
        sent[p]["back"] = (moved, swap(moved))

    def feed_last(p):
        feed_back(0, p, *sent[p]["back"], 0)

    def attn_last(p):
        attn_back(0, p)

    for step, p in (
        (attn_early, 0),
        (attn_early, 1),
        (feed_early, 0),
        (hand_on, 0),
        (feed_early, 1),
        (attn_early, 2),
        (turn_weights, 1),
        (receive, 0),
        (attn_late, 0),
        (hand_on, 1),
        (feed_late, 0),
        (feed_early, 2),
        (feed_first, 0),
        (hand_on, 2),
        (receive, 1),
        (attn_first, 0),
        (attn_late, 1),
        (receive, 2),
        (turn_weights, 0),
        (feed_late, 1),
        (attn_late, 2),
        (feed_first, 1),
        (feed_late, 2),
        (receive_back, 0),
        (attn_first, 1),
        (feed_last, 0),
        (feed_first, 2),
        (receive_back, 1),
        (attn_first, 2),
        (feed_last, 1),
        (receive_back, 2),
        (feed_last, 2),
    ):
        step(p)
    feed_lists = [
        [kept[p]["hidden"] for p in parts],
        [feed[p]["d_down"] for p in parts],
        [kept[p]["low"] for p in parts],
        [feed[p]["d_pre"] for p in parts],
    ]

    def feed_weights(step, cost=3 * 10**9):
        return order.run(
            run_weights,
            feed_weights_kernel,
            "feed_weights",
            marks,
            step,
            feed_lists,
            [],
            2 * BLOCK,
            cost,
        )[0]

    def add_local(pair, local):
        return order.run(add_step, pair, local)

    shard = feed_weights(0)
    feed_pair = ring.send((shard[0], shard[1]))
    shard = feed_weights(1)
    for p in parts:
        attn_last(p)
    feed_pair = ring.send(add_local(feed_pair, shard))
    attn_lists = [
        [kept[p]["rows"] for p in parts],
        [attn[p]["d_joined"] for p in parts],
        [kept[p]["mixed"] for p in parts],
        [attn[p]["d_attn"] for p in parts],
    ]

    small = [sums["bias"], sums["attn"], sums["feed"], *small]

    def attn_weights(step, cost=3 * 10**9):
        return order.run(
            run_weights,
            attn_weights_kernel,
            "attn_weights",
            marks,
            step,
            attn_lists,
            small,
            BLOCK + TAIL,
            cost,
        )[0]

    shard = attn_weights(0, 10**9)
    attn_pair = ring.send((shard[0], shard[1]))
    attn_local = attn_weights(1, 10**9)
    feed_local = feed_weights(2, 10**9)
    streams = [
        dict(
            pair=attn_pair,
            local=attn_local,
            weights=attn_weights,
            steps=[],
            pairs=[],
            joins=True,
            sent=1,
            kernel=attn_place_kernel,
            name="attn_place",
            held=unwritten((2, 3, width, local), (2, local, width), (2, RING, 8, BLOCK)),
        ),
        dict(
            pair=feed_pair,
            local=feed_local,
            weights=feed_weights,
            steps=[],
            pairs=[],
            joins=False,
            sent=2,
            kernel=feed_place_kernel,
            name="feed_place",
            held=unwritten((2, units, width), (2, width, units)),
        ),
    ]

    def advance(stream):
        sent = stream["sent"]
        *pair, token = lax.optimization_barrier((*stream["pair"], *order.tokens))
        order.tokens = (token,)
        if sent < RING:
            pair = add_local(pair, stream["local"])
            if sent == RING - 1:
                pair = ring.across(pair)
        stream["pair"] = ring.send(pair) if sent < 2 * RING - 2 else None
        if sent < RING - 1:
            stream["local"] = stream["weights"](sent + 1)
        else:
            stream["steps"].append(sent - RING + 1)
            stream["pairs"].append(pair)
            if sent != 2 * RING - 3 or not stream["joins"]:
                stream["held"] = order.run(
                    place_step,
                    stream["kernel"],
                    stream["name"],
                    marks,
                    tuple(stream["steps"]),
                    stream["pairs"],
                    stream["held"],
                )
                stream["steps"], stream["pairs"] = [], []
        stream["sent"] += 1

    attn_stream, feed_stream = streams
    while attn_stream["pair"] is not None or feed_stream["pair"] is not None:
        if attn_stream["sent"] == 2 * RING - 2:
            input_grads, layer_outputs = order.run(
                finish,
                [attn[p]["mine"] for p in parts],
                [swap(order.after(attn[p]["theirs"])) for p in parts],
                [feed[p]["outputs"] for p in parts],
            )
        if feed_stream["pair"] is not None:
            advance(feed_stream)
        if attn_stream["pair"] is not None:
            advance(attn_stream)
    joint_out, output_out, small_out = attn_stream["held"]
    down_out, up_out = feed_stream["held"]

    rows = small_out[:, :, 0]
    bias_grad = rows[:, :4].reshape(2, units)
    norm_sums = rows[:, 4:].reshape(2, 2, width)
    counts = small_out[0, 0, 1].reshape(3, 128)[:2, :SYMBOLS]
    return (
        layer_outputs[None],
        input_grads[None],
        joint_out.transpose(0, 2, 1, 3)[None],
        output_out[None],
        up_out[None],
        bias_grad[None],
        down_out[None],
        norm_sums[:, 0][None],
        norm_sums[:, 1][None],
        counts.astype(jnp.int32),
    )


def solution(mesh):
    return jax.shard_map(
        shards,
        mesh=mesh,
        in_specs=(
            P("dp", "tensor"),
            P("dp", "tensor"),
            P("dp"),
            P("dp"),
            P("dp"),
            P("dp"),
            P("section", None, None, None, "tensor"),
            P("section", None, "tensor", None),
            P("section", None, None, "tensor"),
            P("section", None, "tensor"),
            P("section", None, "tensor", None),
            P("section", None, None),
            P("section", None, None),
        ),
        out_specs=(
            P("section", "dp", "tensor"),
            P("section", "dp", "tensor"),
            P("section", None, None, None, "tensor"),
            P("section", None, "tensor", None),
            P("section", None, None, "tensor"),
            P("section", None, "tensor"),
            P("section", None, "tensor", None),
            P("section", None, None),
            P("section", None, None),
            P(),
        ),
        check_vma=False,
    )
```

```python
import functools

import jax
import jax.numpy as jnp
from jax import lax
from jax.experimental import pallas as pl
from jax.experimental.pallas import tpu as pltpu
from jax.sharding import PartitionSpec as P

HEAD_DIM = 64
SYMBOLS = 24
SEQ = 160
PARTS = (2, 2, 2)
RING = 8
BLOCK = 384
TAIL = 16
EPS = 1e-05
SCALE = HEAD_DIM**-0.5
VMEM_LIMIT = 7 * 1024 * 1024
CHAIN_LIMIT = 7 * 1024 * 1024

root_half = 0.7071067811865476
root_two_pi = 0.3989422804014327
BF = jnp.bfloat16
F32 = jnp.float32


def swap(value):
    return lax.ppermute(value, "tensor", [(0, 1), (1, 0)])


def dot(a, b):
    return jnp.dot(a, b, preferred_element_type=F32)


def dot_rows(a, b):
    return lax.dot_general(a, b, (((1,), (1,)), ((), ())), preferred_element_type=F32)


def dot_cols(a, b):
    return lax.dot_general(a, b, (((0,), (0,)), ((), ())), preferred_element_type=F32)


def in_order(core, own, other):
    first = core == 0
    return jnp.concatenate(
        [jnp.where(first, own, other), jnp.where(first, other, own)], axis=1
    )


def own_part(core, value):
    half = value.shape[1] // 2
    return jnp.where(core == 0, value[:, :half], value[:, half:])


def normalise(rows):
    centred = rows - jnp.mean(rows, axis=-1, keepdims=True)
    inv_root = lax.rsqrt(jnp.mean(centred * centred, axis=-1, keepdims=True) + EPS)
    return centred * inv_root, inv_root


def norm_back(grads, normal, inv_root, gain):
    scaled = grads * gain
    inner = (
        scaled
        - jnp.mean(scaled, axis=-1, keepdims=True)
        - normal * jnp.mean(scaled * normal, axis=-1, keepdims=True)
    )
    return inner * inv_root


def pair_spans(width):
    return [slice(at, at + 2 * HEAD_DIM) for at in range(0, width, 2 * HEAD_DIM)]


def left_head():
    return lax.broadcasted_iota(jnp.int32, (1, 2 * HEAD_DIM), 1) < HEAD_DIM


def pair_scores(first, second):
    left = left_head().astype(BF)
    both = jnp.concatenate([first * left, first * (1 - left)], axis=0)
    return dot_rows(both, second).reshape(2, SEQ, SEQ)


def pair_product(matrices, block):
    found = dot(matrices.reshape(2 * SEQ, SEQ), block)
    return jnp.where(left_head(), found[:SEQ], found[SEQ:]).astype(BF)


def pair_turned(matrices):
    return jnp.concatenate([matrices[0].T, matrices[1].T], axis=0)


def attn_forward_kernel(start, count, chain, marks, own, other, joint, output, *refs):
    tag = marks[3 + start + chain]
    core = marks[1]
    a, b = own[...], other[...]
    rows = in_order(core, a, b)
    q, k, v = [dot(rows, joint[tag, j]).astype(BF) for j in range(3)]
    key_live = lax.broadcasted_iota(jnp.int32, (1, SEQ, 1), 1) < marks[3 + count + start + chain]
    spans = pair_spans(q.shape[1])
    scores = [pair_scores(k[:, s], q[:, s] * jnp.asarray(SCALE, BF)) for s in spans]
    probs = []
    for found in scores:
        found = jnp.where(key_live, found, -1000000000.0)
        shifted = jnp.exp(found - jnp.max(found, axis=1, keepdims=True))
        probs.append((shifted * (1.0 / jnp.sum(shifted, axis=1, keepdims=True))).astype(BF))
    mixed = jnp.concatenate(
        [pair_product(pair_turned(p), v[:, s]) for p, s in zip(probs, spans)], axis=1
    )
    refs[0][...] = rows
    refs[1][...] = dot(mixed, output[tag]).astype(BF)
    refs[2][...] = jnp.concatenate([q, k, v], axis=1)
    for at, found in enumerate(probs):
        refs[3][0, 2 * at : 2 * at + 2] = found
    refs[4][...] = mixed


def feed_forward_kernel(start, chain, marks, rows, part, other, gains, shifts, up, bias, down, *outs):
    tag = marks[3 + start + chain]
    total = rows[...].astype(F32) + (part[...].astype(F32) + other[...].astype(F32))
    normal, inv_root = normalise(total)
    low = (normal * gains[0:1] + shifts[0:1]).astype(BF)
    pre = dot(low, up[tag]) + jnp.where(tag == 0, bias[0:1], bias[1:2]).astype(F32)
    cdf = 0.5 * (1.0 + lax.erf(pre * root_half))
    hidden = (pre * cdf).astype(BF)
    outs[0][...] = dot(hidden, down[tag]).astype(BF)
    outs[1][...] = normal.astype(BF)
    outs[2][...] = inv_root
    outs[3][...] = low
    outs[4][...] = hidden
    outs[5][...] = (cdf + pre * jnp.exp(-0.5 * pre * pre) * root_two_pi).astype(BF)


def second_norm(normal, part, other, gains, shifts):
    first = normal[...].astype(F32) * gains[0:1] + shifts[0:1]
    return normalise(first + (part[...].astype(F32) + other[...].astype(F32)))


def last_norm_kernel(chain, marks, normal, part, other, gains, shifts, out):
    second, _ = second_norm(normal, part, other, gains, shifts)
    out[...] = own_part(marks[1], (second * gains[1:2] + shifts[1:2]).astype(BF))


def add_sums(grads, normal, sums):
    sums[0] += jnp.sum(grads * normal, axis=0, keepdims=True)
    sums[1] += jnp.sum(grads, axis=0, keepdims=True)


def feed_back_kernel(
    start, chain, marks, normal, part, other, gains, shifts, own, partner, slope, up, down, *outs
):
    tag = marks[3 + start + chain]
    core = marks[1]
    a, b = own[...], partner[...]
    grads = in_order(core, a, b).astype(F32)
    second, inv_root = second_norm(normal, part, other, gains, shifts)
    back = norm_back(grads, second, inv_root, gains[1:2])
    low = back.astype(BF)
    d_pre = (dot(low, down[tag]) * slope[...].astype(F32)).astype(BF)
    outs[0][...] = dot(d_pre, up[tag]).astype(BF)
    outs[1][...] = low
    outs[2][...] = d_pre
    outs[3][...] = own_part(core, (second * gains[1:2] + shifts[1:2]).astype(BF))
    add_sums(grads, second, outs[4])
    outs[5][tag] += jnp.sum(d_pre.astype(F32), axis=0, keepdims=True)


def attn_back_kernel(
    start, chain, marks, back, part, other, normal, inv_root, gains, joined, probs, joint, output, *outs
):
    tag = marks[3 + start + chain]
    core = marks[1]
    grads = back[...].astype(F32) + (part[...].astype(F32) + other[...].astype(F32))
    normal = normal[...].astype(F32)
    back_one = norm_back(grads, normal, inv_root[...], gains[0:1])
    low = back_one.astype(BF)
    d_mixed = dot_rows(low, output[tag]).astype(BF)
    width = d_mixed.shape[1]
    q, k, v = [joined[:, j * width : (j + 1) * width] for j in range(3)]
    spans = pair_spans(width)
    d_probs = [pair_scores(v[:, s], d_mixed[:, s]) for s in spans]
    held = [probs[0, 2 * at : 2 * at + 2] for at in range(len(spans))]
    d_scores = []
    for found, kept in zip(d_probs, held):
        wide = kept.astype(F32)
        inner = jnp.sum(wide * found, axis=1, keepdims=True)
        d_scores.append((wide * (found - inner)).astype(BF))
    scale = jnp.asarray(SCALE, BF)
    d_k = [pair_product(d, q[:, s]) * scale for d, s in zip(d_scores, spans)]
    d_v = [pair_product(h, d_mixed[:, s]) for h, s in zip(held, spans)]
    d_q = [pair_product(pair_turned(d), k[:, s]) * scale for d, s in zip(d_scores, spans)]
    pieces = [d_q, d_k, d_v]
    blocks = [jnp.concatenate(p, axis=1) for p in pieces]
    d_rows = sum(dot_rows(blocks[j], joint[tag, j]) for j in range(3)).astype(BF)
    outs[0][...] = own_part(core, back_one) + own_part(core, d_rows).astype(F32)
    outs[1][...] = own_part(1 - core, d_rows)
    outs[2][...] = low
    outs[3][...] = jnp.concatenate(blocks, axis=1)
    add_sums(grads, normal, outs[4])


class Marks:
    def __init__(self, ref):
        self.rows = ref[...]

    def __getitem__(self, at):
        return self.rows[0, at]


def behind(kernel, taken, ignored):
    def call(marks, *refs):
        kernel(Marks(marks), *refs[:taken], *refs[taken + ignored :])

    return call


ANY = pl.BlockSpec(memory_space=pl.ANY)
HBM = pl.BlockSpec(memory_space=pltpu.HBM)
TOKEN = jax.ShapeDtypeStruct((8, 128), F32)


def sign_off(token):
    token[...] = jnp.zeros_like(token)


class Order:
    def __init__(self):
        self.tokens = ()

    def run(self, call, *args):
        *results, token = call(*args, self.tokens)
        self.tokens = (token,)
        return results

    def wait(self, value):
        self.tokens = tuple(lax.optimization_barrier((*self.tokens, value))[:-1])

    def after(self, value):
        return lax.optimization_barrier((value, *self.tokens))[0]


VMEM = pl.BlockSpec(memory_space=pltpu.VMEM)
SMEM = pl.BlockSpec(memory_space=pltpu.SMEM)


def chain_view(ref, kind, at):
    if kind == "rows":
        return ref.at[at * SEQ : (at + 1) * SEQ]
    return ref.at[at : at + 1] if kind == "chain" else ref


def prepare_kernel(chains, count, places, *refs):
    sources, marks, held = refs[:count], refs[count], refs[count + 1 : 2 * count - 1]
    tags, live, sems = refs[2 * count - 1 :]
    copies = [
        pltpu.make_async_copy(source, target, sems.at[at])
        for at, (source, target) in enumerate(zip(sources, (tags, live) + held))
    ]
    for copy in copies:
        copy.start()
    for copy in copies[:2]:
        copy.wait()
    token = lax.broadcasted_iota(jnp.int32, live.shape, 1)
    found = [places[at] for at in range(3)]
    found += [jnp.where(tags[chain] > 0, 1, 0) for chain in range(chains)]
    for chain in range(chains):
        inside = (token >= chain * SEQ) & (token < (chain + 1) * SEQ)
        found.append(jnp.sum(jnp.where(inside, live[...], 0)))
    lane = lax.broadcasted_iota(jnp.int32, marks.shape, 1)
    rows = jnp.zeros(marks.shape, jnp.int32)
    for at, value in enumerate(found):
        rows = jnp.where(lane == at, value, rows)
    marks[...] = rows
    for copy in copies[2:]:
        copy.wait()


def prepare(places, tags, live, arrays):
    chains = tags.shape[0]
    sources = [tags, live, *arrays]
    count = len(sources)
    return pl.pallas_call(
        functools.partial(prepare_kernel, chains, count),
        in_specs=[SMEM] + [HBM] * count,
        out_specs=[VMEM] * (1 + len(arrays)),
        out_shape=[jax.ShapeDtypeStruct((8, 128), jnp.int32)]
        + [jax.ShapeDtypeStruct(a.shape, a.dtype) for a in arrays],
        scratch_shapes=[
            pltpu.SMEM(tags.shape, jnp.int32),
            pltpu.VMEM(live.shape, jnp.int32),
            pltpu.SemaphoreType.DMA((count,)),
        ],
        compiler_params=pltpu.CompilerParams(vmem_limit_bytes=1024 * 1024),
        name="prepare",
    )(places, *[pltpu.with_memory_space_constraint(a, pltpu.HBM) for a in sources])


def turn(active, marks, arrays, held, after):
    count = len(arrays)
    skipped = count + len(held) + len(after)

    def call(marks, *refs):
        marks = Marks(marks)
        sign_off(refs[-1])

        @pl.when(marks[0] == active)
        def _():
            for source, target in zip(refs[:count], refs[skipped:]):
                for at in range(source.shape[0]):
                    target[at] = source[at].T

    return pl.pallas_call(
        call,
        in_specs=[VMEM] * (1 + count + len(held)) + [ANY] * len(after),
        out_specs=[VMEM] * (count + 1),
        out_shape=[jax.ShapeDtypeStruct((a.shape[0], a.shape[2], a.shape[1]), BF) for a in arrays]
        + [TOKEN],
        input_output_aliases={1 + count + at: at for at in range(len(held))},
        compiler_params=pltpu.CompilerParams(vmem_limit_bytes=VMEM_LIMIT),
        cost_estimate=pl.CostEstimate(flops=10**10, bytes_accessed=10**7, transcendentals=0),
        name="turn",
    )(marks, *arrays, *held, *after)


def run_chains(kernel, name, active, marks, chains, ins, outs, after):
    shapes, held, aliases = [], [], {}
    for trailing, dtype, kind, array in outs:
        lead = {"rows": (chains * SEQ,), "chain": (chains,), "whole": ()}[kind]
        if array is not None:
            aliases[1 + len(ins) + len(held)] = len(shapes)
            held.append(array)
        shapes.append(jax.ShapeDtypeStruct(lead + trailing, dtype))
    kinds = [(kind, first) for _, kind, first in ins] + [(kind, 0) for _, _, kind, _ in outs]
    skipped = len(ins) + len(held) + len(after)

    def call(marks, *refs):
        marks = Marks(marks)
        *refs, token = refs[: len(ins)] + refs[skipped:]
        sign_off(token)

        @pl.when(marks[0] == active)
        def _():
            for chain in range(chains):
                views = [chain_view(r, kind, first + chain) for r, (kind, first) in zip(refs, kinds)]
                kernel(chain, marks, *views)

    return pl.pallas_call(
        call,
        in_specs=[VMEM] * (1 + len(ins) + len(held)) + [ANY] * len(after),
        out_specs=[VMEM] * (len(outs) + 1),
        out_shape=shapes + [TOKEN],
        input_output_aliases=aliases,
        compiler_params=pltpu.CompilerParams(vmem_limit_bytes=CHAIN_LIMIT),
        cost_estimate=pl.CostEstimate(flops=10**10, bytes_accessed=10**7, transcendentals=0),
        name=name,
    )(marks, *[a for a, _, _ in ins], *held, *after)


def ring_spot(marks, step, way):
    return lax.rem(marks[2] + 2 * RING + way * step, RING)


def span(at):
    return pl.ds(pl.multiple_of(at * BLOCK, BLOCK), BLOCK)


def cut(ref, at):
    return ref[:, span(at)]


def set_rows(marks, block, which):
    pieces = []
    for chain in range(block.shape[0] // SEQ):
        piece = block[chain * SEQ : (chain + 1) * SEQ]
        pieces.append(jnp.where(marks[3 + chain] == which, piece, jnp.zeros_like(piece)))
    return jnp.concatenate(pieces, axis=0)


def all_rows(refs, at):
    return jnp.concatenate([cut(ref, at) for ref in refs], axis=0)


def feed_shard(marks, which, hidden, d_down, low, d_pre):
    return (
        dot_cols(set_rows(marks, hidden, which), d_down).astype(BF),
        dot_cols(set_rows(marks, low, which), d_pre).astype(BF),
    )


def feed_weights_kernel(step, parts, marks, *refs):
    hidden, d_down, low, d_pre = [refs[n * parts : (n + 1) * parts] for n in range(4)]
    out, token = refs[4 * parts :]
    sign_off(token)
    for which, way in ((0, -1), (1, 1)):
        spot = ring_spot(marks, step, way)
        far, near = lax.div(spot, 2), lax.rem(spot, 2)
        out[which, :BLOCK], out[which, BLOCK:] = feed_shard(
            marks,
            which,
            all_rows(hidden, far),
            all_rows(d_down, near),
            all_rows(low, near),
            all_rows(d_pre, far),
        )


def two_halves(value):
    high = value.astype(BF).astype(F32)
    return jnp.concatenate([high, value - high], axis=0).astype(BF)


def one_whole(rows):
    rows = rows.astype(F32)
    return rows[: TAIL // 2] + rows[TAIL // 2 :]


def count_rows(live, predicted, targets):
    symbols = lax.broadcasted_iota(jnp.int32, (128, live.shape[1]), 0)
    hits = (targets[...] == symbols) & (live[...] > 0)
    right = hits & (predicted[...] == targets[...])
    ones = jnp.ones((8, live.shape[1]), BF)
    found = [dot_rows(ones, h.astype(F32).astype(BF)) for h in (hits, right)]
    return jnp.concatenate(found + [jnp.zeros_like(found[0])], axis=1)[0:1]


def attn_weights_kernel(step, parts, marks, *refs):
    rows, d_joined, mixed, d_attn = [refs[n * parts : (n + 1) * parts] for n in range(4)]
    bias, *sums, live, predicted, targets, out, token = refs[4 * parts :]
    sign_off(token)
    for which, way in ((0, -1), (1, 1)):
        spot = ring_spot(marks, step, way)
        far, near = lax.div(spot, 2), lax.rem(spot, 2)

        @pl.when(far < 3)
        def _():
            out[which, :BLOCK] = dot_cols(
                set_rows(marks, all_rows(rows, near), which), all_rows(d_joined, far)
            ).astype(BF)

        @pl.when(far == 3)
        def _():
            out[which, :BLOCK] = dot_cols(
                set_rows(marks, all_rows(mixed, 0), which), all_rows(d_attn, near)
            ).astype(BF)

        early = far < 2
        small = jnp.where(
            early,
            bias[which, :, span(jnp.where(early, spot, 0))],
            sums[which][jnp.where(early, 0, far - 2), :, span(near)],
        )
        place = lax.broadcasted_iota(jnp.int32, (TAIL // 2, BLOCK), 0)
        small = jnp.where(place == 0, small, 0.0)
        out[which, BLOCK:] = two_halves(small)
        if which == 0:

            @pl.when(spot == 0)
            def _():
                counts = count_rows(live, predicted, targets)
                out[which, BLOCK:] = two_halves(jnp.where(place == 1, counts, small))


def run_weights(kernel, name, marks, step, lists, rest, rows_out, cost, after):
    ins = [a for arrays in lists for a in arrays] + list(rest)
    return pl.pallas_call(
        behind(functools.partial(kernel, step + 1, len(lists[0])), len(ins), len(after)),
        in_specs=[VMEM] * (1 + len(ins)) + [ANY] * len(after),
        out_specs=[VMEM, VMEM],
        out_shape=[jax.ShapeDtypeStruct((2, rows_out, BLOCK), BF), TOKEN],
        compiler_params=pltpu.CompilerParams(vmem_limit_bytes=VMEM_LIMIT),
        cost_estimate=pl.CostEstimate(flops=cost, bytes_accessed=10**6, transcendentals=0),
        name=name,
    )(marks, *ins, *after)


def add_kernel(tail, ahead, back, local, out_ahead, out_back, token):
    sign_off(token)
    for which, (ref, out) in enumerate(((ahead, out_ahead), (back, out_back))):
        total = ref[...].astype(F32) + local[which].astype(F32)
        out[...] = total.astype(BF)
        if tail:
            out[tail:] = two_halves(one_whole(total[tail:]))


def add_step(pair, local, after):
    shape = local.shape[1:]
    tail = BLOCK if shape[0] == BLOCK + TAIL else 0

    def call(*refs):
        add_kernel(tail, *refs[:3], *refs[3 + len(after) :])

    return pl.pallas_call(
        call,
        in_specs=[VMEM] * 3 + [ANY] * len(after),
        out_specs=[VMEM] * 3,
        out_shape=[jax.ShapeDtypeStruct(shape, BF)] * 2 + [TOKEN],
        compiler_params=pltpu.CompilerParams(vmem_limit_bytes=VMEM_LIMIT),
        cost_estimate=pl.CostEstimate(flops=3*10**9, bytes_accessed=10**6, transcendentals=0),
        name="ring_add",
    )(*pair, local, *after)


def feed_place_kernel(steps, marks, pairs, outs, wide, sems):
    down, up = outs
    copies = []
    for at, (step, pair) in enumerate(zip(steps, pairs)):
        for which, (ref, way) in enumerate(zip(pair, (-1, 1))):
            spot = ring_spot(marks, step, way)
            far, near = lax.div(spot, 2), lax.rem(spot, 2)
            slot = 2 * at + which
            wide[slot] = ref[...].astype(F32)
            copies += [
                pltpu.make_async_copy(
                    wide.at[slot, :BLOCK], down.at[which, span(far), span(near)], sems.at[2 * slot]
                ),
                pltpu.make_async_copy(
                    wide.at[slot, BLOCK:], up.at[which, span(near), span(far)], sems.at[2 * slot + 1]
                ),
            ]
            for copy in copies[-2:]:
                copy.start()
    for copy in copies:
        copy.wait()


def attn_place_kernel(steps, marks, pairs, outs, wide, sems):
    joint, output, small = outs
    waits = []
    for at, (step, pair) in enumerate(zip(steps, pairs)):
        for which, (ref, way) in enumerate(zip(pair, (-1, 1))):
            spot = ring_spot(marks, step, way)
            far, near = lax.div(spot, 2), lax.rem(spot, 2)
            slot = 2 * at + which
            wide[slot] = ref[...].astype(F32)
            wide[slot, BLOCK : BLOCK + TAIL // 2] = one_whole(ref[BLOCK:])
            tail = pltpu.make_async_copy(
                wide.at[slot, BLOCK : BLOCK + TAIL // 2],
                small.at[which, spot],
                sems.at[2 * slot + 1],
            )
            to_joint = pltpu.make_async_copy(
                wide.at[slot, :BLOCK],
                joint.at[which, jnp.minimum(far, 2), span(near)],
                sems.at[2 * slot],
            )
            to_output = pltpu.make_async_copy(
                wide.at[slot, :BLOCK], output.at[which, :, span(near)], sems.at[2 * slot]
            )
            tail.start()
            pl.when(far < 3)(to_joint.start)
            pl.when(far == 3)(to_output.start)
            waits.append((far, tail, to_joint, to_output))
    for far, tail, to_joint, to_output in waits:
        tail.wait()
        pl.when(far < 3)(to_joint.wait)
        pl.when(far == 3)(to_output.wait)


def place_step(kernel, name, marks, steps, pairs, held, after):
    shape = pairs[0][0].shape
    count = len(held)
    given = 2 * len(pairs)

    def call(marks, *refs):
        taken = [refs[at : at + 2] for at in range(0, given, 2)]
        refs = refs[given + count + len(after) :]
        sign_off(refs[count])
        kernel(steps, Marks(marks), taken, refs[:count], *refs[count + 1 :])

    return pl.pallas_call(
        call,
        in_specs=[VMEM] * (1 + given) + [HBM] * count + [ANY] * len(after),
        out_specs=[HBM] * count + [VMEM],
        scratch_shapes=[
            pltpu.VMEM((given,) + shape, F32),
            pltpu.SemaphoreType.DMA((2 * given,)),
        ],
        out_shape=[jax.ShapeDtypeStruct(h.shape, h.dtype) for h in held] + [TOKEN],
        input_output_aliases={1 + given + i: i for i in range(count)},
        compiler_params=pltpu.CompilerParams(vmem_limit_bytes=VMEM_LIMIT),
        cost_estimate=pl.CostEstimate(flops=10**10, bytes_accessed=10**6, transcendentals=0),
        name=name,
    )(marks, *[value for pair in pairs for value in pair], *held, *after)


def finish(mine, theirs, outputs, after):
    count = len(mine)
    rows, half = sum(a.shape[0] for a in mine), mine[0].shape[1]

    def call(*refs):
        grads, whole, token = refs[3 * count + len(after) :]
        sign_off(token)
        at = 0
        for own, other, output in zip(refs, refs[count:], refs[2 * count : 3 * count]):
            here = slice(at, at + own.shape[0])
            grads[here] = own[...] + other[...].astype(F32)
            whole[here] = output[...]
            at += own.shape[0]

    return pl.pallas_call(
        call,
        in_specs=[VMEM] * (3 * count) + [ANY] * len(after),
        out_specs=[VMEM] * 3,
        out_shape=[
            jax.ShapeDtypeStruct((rows, half), F32),
            jax.ShapeDtypeStruct((rows, half), BF),
            TOKEN,
        ],
        compiler_params=pltpu.CompilerParams(vmem_limit_bytes=VMEM_LIMIT),
        cost_estimate=pl.CostEstimate(flops=10**10, bytes_accessed=10**6, transcendentals=0),
        name="finish",
    )(*mine, *theirs, *outputs, *after)


def unwritten(*shapes):
    return pl.pallas_call(
        lambda *refs: None,
        out_specs=[HBM] * len(shapes),
        out_shape=[jax.ShapeDtypeStruct(s, F32) for s in shapes],
        compiler_params=pltpu.CompilerParams(vmem_limit_bytes=1024 * 1024),
        name="unwritten",
    )()


class Ring:
    def __init__(self):
        self.count = lax.axis_size("dp")
        assert self.count % RING == 0
        order = list(range(0, RING, 2)) + list(range(1, RING, 2))[::-1]
        rank = lax.rem(lax.axis_index("dp"), RING)
        self.place = jnp.zeros((), jnp.int32)
        for at, member in enumerate(order):
            self.place = jnp.where(rank == member, at, self.place)
        self.ahead = [
            (base + order[i], base + order[(i + 1) % RING])
            for base in range(0, self.count, RING)
            for i in range(RING)
        ]
        self.back = [(b, a) for a, b in self.ahead]

    def send(self, pair):
        return lax.ppermute(pair[0], "dp", self.ahead), lax.ppermute(pair[1], "dp", self.back)

    def across(self, pair):
        result = []
        for value in pair:
            total = value.astype(F32)
            moving = value
            for _ in range(self.count // RING - 1):
                pairs = [(i, (i + RING) % self.count) for i in range(self.count)]
                moving = lax.ppermute(moving, "dp", pairs)
                total = total + moving.astype(F32)
            low = total.astype(BF)
            if total.shape[0] == BLOCK + TAIL and self.count > RING:
                tail = two_halves(one_whole(total[BLOCK:]))
                low = jnp.concatenate([low[:BLOCK], tail], axis=0)
            result.append(low)
        return result


def part_sizes(chains):
    bounds = [chains * sum(PARTS[:p]) // sum(PARTS) for p in range(len(PARTS) + 1)]
    return [high - low for low, high in zip(bounds, bounds[1:])], bounds[:-1]


def shards(
    chain_inputs,
    cotangent,
    chain_tags,
    pad_mask,
    predicted,
    target_ids,
    joint_proj,
    output_proj,
    up_proj,
    up_bias,
    down_proj,
    norm_gain,
    norm_shift,
):
    section = lax.axis_index("section")
    core = lax.axis_index("tensor")
    tokens, half = chain_inputs.shape
    width = 2 * half
    all_chains = tokens // SEQ
    sizes, starts = part_sizes(all_chains)
    parts = range(len(sizes))
    ring = Ring()
    small = [ids.reshape(1, tokens) for ids in (pad_mask, predicted, target_ids)]
    joint = joint_proj[0].transpose(0, 2, 1, 3)
    output, up, bias, down = output_proj[0], up_proj[0], up_bias[0], down_proj[0]
    places = jnp.stack([section, core, ring.place]).astype(jnp.int32)
    marks, joint, output, own_rows = prepare(
        places, chain_tags, small[0], [joint, output, chain_inputs]
    )
    gains, shifts = norm_gain[0], norm_shift[0]
    units = up.shape[2]
    local = output.shape[1]
    heads = local // HEAD_DIM
    cot_other = swap(cotangent)
    rows_other = swap(chain_inputs)

    order = Order()

    kept = [{} for _ in parts]
    feed = [{} for _ in parts]
    attn = [{} for _ in parts]
    sent = [{} for _ in parts]
    sums = dict(
        feed=jnp.zeros((2, 1, width), F32),
        attn=jnp.zeros((2, 1, width), F32),
        bias=jnp.zeros((2, 1, units), F32),
    )

    def run(kernel, name, active, p, ins, outs, held, totals):
        outs = [(shape, dtype, kind, held.get(key)) for key, shape, dtype, kind in outs] + [
            (sums[key].shape, F32, "whole", sums[key]) for key in totals
        ]
        return order.run(run_chains, kernel, name, active, marks, sizes[p], ins, outs)

    def attn_forward(active, p, own, other, first):
        ins = [(own, "rows", first), (other, "rows", first)]
        ins += [(joint, "whole", 0), (output, "whole", 0)]
        outs = [
            ("rows", (width,), BF, "rows"),
            ("part", (width,), BF, "rows"),
            ("joined", (3 * local,), BF, "rows"),
            ("probs", (heads, SEQ, SEQ), BF, "chain"),
            ("mixed", (local,), BF, "rows"),
        ]
        kernel = functools.partial(attn_forward_kernel, starts[p], all_chains)
        found = run(kernel, "attn_forward", active, p, ins, outs, kept[p], [])
        kept[p].update(zip([o[0] for o in outs], found))
        kept[p]["part_other"] = swap(kept[p]["part"])

    def feed_forward(active, p):
        ins = [(kept[p][n], "rows", 0) for n in ("rows", "part", "part_other")]
        ins += [(a, "whole", 0) for a in (gains, shifts, up, bias, down)]
        outs = [
            ("down", (width,), BF, "rows"),
            ("normal", (width,), BF, "rows"),
            ("inv_root", (1,), F32, "rows"),
            ("low", (width,), BF, "rows"),
            ("hidden", (units,), BF, "rows"),
            ("slope", (units,), BF, "rows"),
        ]
        kernel = functools.partial(feed_forward_kernel, starts[p])
        found = run(kernel, "feed_forward", active, p, ins, outs, kept[p], [])
        kept[p].update(zip([o[0] for o in outs], found))
        kept[p]["down_other"] = swap(kept[p]["down"])

    def feed_back(active, p, own, other, first):
        ins = [(kept[p][n], "rows", 0) for n in ("normal", "down", "down_other")]
        ins += [(gains, "whole", 0), (shifts, "whole", 0)]
        ins += [(own, "rows", first), (other, "rows", first)]
        ins += [(kept[p]["slope"], "rows", 0)]
        ins += [(turned["up"], "whole", 0), (turned["down"], "whole", 0)]
        outs = [
            ("part", (width,), BF, "rows"),
            ("d_down", (width,), BF, "rows"),
            ("d_pre", (units,), BF, "rows"),
            ("outputs", (half,), BF, "rows"),
        ]
        kernel = functools.partial(feed_back_kernel, starts[p])
        *found, sums["feed"], sums["bias"] = run(
            kernel, "feed_back", active, p, ins, outs, feed[p], ["feed", "bias"]
        )
        feed[p].update(zip([o[0] for o in outs], found))
        feed[p]["part_other"] = swap(feed[p]["part"])

    def attn_back(active, p):
        ins = [(feed[p][n], "rows", 0) for n in ("d_down", "part", "part_other")]
        ins += [(kept[p]["normal"], "rows", 0), (kept[p]["inv_root"], "rows", 0)]
        ins += [(gains, "whole", 0), (kept[p]["joined"], "rows", 0), (kept[p]["probs"], "chain", 0)]
        ins += [(joint, "whole", 0), (output, "whole", 0)]
        outs = [
            ("mine", (half,), F32, "rows"),
            ("theirs", (half,), BF, "rows"),
            ("d_attn", (width,), BF, "rows"),
            ("d_joined", (3 * local,), BF, "rows"),
        ]
        kernel = functools.partial(attn_back_kernel, starts[p])
        *found, sums["attn"] = run(kernel, "attn_back", active, p, ins, outs, attn[p], ["attn"])
        attn[p].update(zip([o[0] for o in outs], found))

    def across(value):
        return lax.ppermute(value, "section", [(0, 1), (1, 0)])

    turned = {}

    def turn_weights(active):
        held = [turned[n] for n in ("up", "down") if n in turned]
        turned["up"], turned["down"] = order.run(turn, active, marks, [up, down], held)

    def attn_early(p):
        attn_forward(0, p, own_rows, rows_other, starts[p])

    def feed_early(p):
        feed_forward(0, p)

    def hand_on(p):
        ins = [(kept[p][n], "rows", 0) for n in ("normal", "down", "down_other")]
        ins += [(gains, "whole", 0), (shifts, "whole", 0)]
        outs = [("moved", (half,), BF, "rows")]
        found = run(last_norm_kernel, "last_norm", 0, p, ins, outs, {}, [])
        sent[p]["on"] = across(found[0])

    def receive(p):
        moved = order.after(sent[p]["on"])
        sent[p]["on"] = (moved, swap(moved))

    def attn_late(p):
        attn_forward(1, p, *sent[p]["on"], 0)

    def feed_late(p):
        feed_forward(1, p)

    def feed_first(p):
        feed_back(1, p, cotangent, cot_other, starts[p])

    def attn_first(p):
        attn_back(1, p)
        total = attn[p]["mine"] + swap(attn[p]["theirs"]).astype(F32)
        sent[p]["back"] = across(total.astype(BF))

    def receive_back(p):
        moved = order.after(sent[p]["back"])
        sent[p]["back"] = (moved, swap(moved))

    def feed_last(p):
        feed_back(0, p, *sent[p]["back"], 0)

    def attn_last(p):
        attn_back(0, p)

    for step, p in (
        (attn_early, 0),
        (attn_early, 1),
        (feed_early, 0),
        (hand_on, 0),
        (feed_early, 1),
        (attn_early, 2),
        (turn_weights, 1),
        (receive, 0),
        (attn_late, 0),
        (hand_on, 1),
        (feed_late, 0),
        (feed_early, 2),
        (feed_first, 0),
        (hand_on, 2),
        (receive, 1),
        (attn_late, 1),
        (attn_first, 0),
        (receive, 2),
        (turn_weights, 0),
        (feed_late, 1),
        (attn_late, 2),
        (feed_first, 1),
        (feed_late, 2),
        (receive_back, 0),
        (attn_first, 1),
        (feed_last, 0),
        (feed_first, 2),
        (receive_back, 1),
        (attn_first, 2),
        (feed_last, 1),
        (receive_back, 2),
        (feed_last, 2),
    ):
        step(p)
    feed_lists = [
        [kept[p]["hidden"] for p in parts],
        [feed[p]["d_down"] for p in parts],
        [kept[p]["low"] for p in parts],
        [feed[p]["d_pre"] for p in parts],
    ]

    def feed_weights(step, cost=3 * 10**9):
        return order.run(
            run_weights,
            feed_weights_kernel,
            "feed_weights",
            marks,
            step,
            feed_lists,
            [],
            2 * BLOCK,
            cost,
        )[0]

    def add_local(pair, local):
        return order.run(add_step, pair, local)

    shard = feed_weights(0)
    feed_pair = ring.send((shard[0], shard[1]))
    shard = feed_weights(1)
    for p in parts:
        attn_last(p)
    feed_pair = ring.send(add_local(feed_pair, shard))
    attn_lists = [
        [kept[p]["rows"] for p in parts],
        [attn[p]["d_joined"] for p in parts],
        [kept[p]["mixed"] for p in parts],
        [attn[p]["d_attn"] for p in parts],
    ]

    small = [sums["bias"], sums["attn"], sums["feed"], *small]

    def attn_weights(step, cost=3 * 10**9):
        return order.run(
            run_weights,
            attn_weights_kernel,
            "attn_weights",
            marks,
            step,
            attn_lists,
            small,
            BLOCK + TAIL,
            cost,
        )[0]

    shard = attn_weights(0, 10**9)
    attn_pair = ring.send((shard[0], shard[1]))
    attn_local = attn_weights(1, 10**9)
    feed_local = feed_weights(2, 10**9)
    streams = [
        dict(
            pair=attn_pair,
            local=attn_local,
            weights=attn_weights,
            steps=[],
            pairs=[],
            joins=True,
            sent=1,
            kernel=attn_place_kernel,
            name="attn_place",
            held=unwritten((2, 3, width, local), (2, local, width), (2, RING, 8, BLOCK)),
        ),
        dict(
            pair=feed_pair,
            local=feed_local,
            weights=feed_weights,
            steps=[],
            pairs=[],
            joins=False,
            sent=2,
            kernel=feed_place_kernel,
            name="feed_place",
            held=unwritten((2, units, width), (2, width, units)),
        ),
    ]

    def advance(stream):
        sent = stream["sent"]
        *pair, token = lax.optimization_barrier((*stream["pair"], *order.tokens))
        order.tokens = (token,)
        if sent < RING:
            pair = add_local(pair, stream["local"])
            if sent == RING - 1:
                pair = ring.across(pair)
        stream["pair"] = ring.send(pair) if sent < 2 * RING - 2 else None
        if sent < RING - 1:
            stream["local"] = stream["weights"](sent + 1)
        else:
            stream["steps"].append(sent - RING + 1)
            stream["pairs"].append(pair)
            if sent != 2 * RING - 3 or not stream["joins"]:
                stream["held"] = order.run(
                    place_step,
                    stream["kernel"],
                    stream["name"],
                    marks,
                    tuple(stream["steps"]),
                    stream["pairs"],
                    stream["held"],
                )
                stream["steps"], stream["pairs"] = [], []
        stream["sent"] += 1

    attn_stream, feed_stream = streams
    while attn_stream["pair"] is not None or feed_stream["pair"] is not None:
        if attn_stream["sent"] == 2 * RING - 2:
            input_grads, layer_outputs = order.run(
                finish,
                [attn[p]["mine"] for p in parts],
                [swap(order.after(attn[p]["theirs"])) for p in parts],
                [feed[p]["outputs"] for p in parts],
            )
        if feed_stream["pair"] is not None:
            advance(feed_stream)
        if attn_stream["pair"] is not None:
            advance(attn_stream)
    joint_out, output_out, small_out = attn_stream["held"]
    down_out, up_out = feed_stream["held"]

    rows = small_out[:, :, 0]
    bias_grad = rows[:, :4].reshape(2, units)
    norm_sums = rows[:, 4:].reshape(2, 2, width)
    counts = small_out[0, 0, 1].reshape(3, 128)[:2, :SYMBOLS]
    return (
        layer_outputs[None],
        input_grads[None],
        joint_out.transpose(0, 2, 1, 3)[None],
        output_out[None],
        up_out[None],
        bias_grad[None],
        down_out[None],
        norm_sums[:, 0][None],
        norm_sums[:, 1][None],
        counts.astype(jnp.int32),
    )


def solution(mesh):
    return jax.shard_map(
        shards,
        mesh=mesh,
        in_specs=(
            P("dp", "tensor"),
            P("dp", "tensor"),
            P("dp"),
            P("dp"),
            P("dp"),
            P("dp"),
            P("section", None, None, None, "tensor"),
            P("section", None, "tensor", None),
            P("section", None, None, "tensor"),
            P("section", None, "tensor"),
            P("section", None, "tensor", None),
            P("section", None, None),
            P("section", None, None),
        ),
        out_specs=(
            P("section", "dp", "tensor"),
            P("section", "dp", "tensor"),
            P("section", None, None, None, "tensor"),
            P("section", None, "tensor", None),
            P("section", None, None, "tensor"),
            P("section", None, "tensor"),
            P("section", None, "tensor", None),
            P("section", None, None),
            P("section", None, None),
            P(),
        ),
        check_vma=False,
    )
```
